256 devices in a mesh: dp: 16 (over y_lo, x, core), fsdp: 16 (over y_hi, z).
Axes of the slice: x: 4, y: 4 (y_hi: 2, y_lo: 2; y = y_hi * 2 + y_lo), z: 8, core: 2. Of those that a mesh axis runs over, the one named last changes fastest.
Arguments:
- inputs: bfloat16 [98304, 3584], P(('dp', 'fsdp')), may hold values from -7 to 7
- queries: bfloat16 [98304, 1792], P(('dp', 'fsdp')), may hold values from -14 to 14
- out_grad: bfloat16 [98304, 1792], P(('dp', 'fsdp')), may hold values from -6 to 6
- kv_weight: bfloat16 [3584, 512], P('fsdp'), may hold values from -0.09375 to 0.09375
- passage_blocks: int32 [256, 6], P(('dp', 'fsdp')), may hold values from 0 to 5, as said below
- handover: int32 [256, 6], P(('dp', 'fsdp')), may hold values from 0 to 1, as said below
Outputs:
- grad_input: bfloat16 [98304, 3584], P(('dp', 'fsdp'))
- grad_query: bfloat16 [98304, 1792], P(('dp', 'fsdp'))
- grad_weight: float32 [3584, 512], P('fsdp')
The draws below stay inside these ranges and needn't reach their ends.
Inputs may be any that keep to these rules, and one draw needn't show every extreme that they name: `passage_blocks`: each row starts at 0 and rises by 0 or 1 from block to block; a passage's blocks all carry the same handover flag. `handover`: partners hand over the same number of blocks, at least one and at most 5.
All inputs are finite; a program needn't handle non-finite values.
Results may differ from the reference program's by a relative error of at most 0.013.
The reference program's roundings to bfloat16 on the way count: a program that leaves them out, or rounds other values in their place, can miss the bound.
Values may be sent and summed in bfloat16 or wider, within the bound.
A program may use at most 128 MiB of HBM per device.

```python
import jax
import jax.numpy as jnp
from jax import lax

D = 3584
KVH = 2
GROUP = 7
HD = 128
NB = 6
BLK = 64
QH = 14
TOKENS = 98304
N_DP = 16
N_FSDP = 16


def plan_tables(key):
    key = jax.random.fold_in(key, 11)
    count = N_DP * N_FSDP
    half = N_DP // 2
    device_ids = jnp.arange(count, dtype=jnp.int32)
    pair = device_ids // N_FSDP % half * N_FSDP + device_ids % N_FSDP
    given = jax.random.randint(jax.random.fold_in(key, 1), (half * N_FSDP,), 1, NB)[pair]
    keys = jax.random.split(jax.random.fold_in(key, 2), count)

    def shuffle(one_key):
        return jax.random.permutation(one_key, NB)
    orders = jax.vmap(shuffle)(keys)
    handover = (orders < given[:, None]).astype(jnp.int32)
    cuts = jax.random.randint(jax.random.fold_in(key, 3), (count, NB), 0, 3) == 0
    change = handover[:, 1:] != handover[:, :-1]
    first_device = (device_ids == 0)[:, None]
    bounds = cuts[:, 1:] | change | first_device
    bounds = jnp.concatenate([jnp.zeros((count, 1), jnp.int32), bounds.astype(jnp.int32)], axis=1)
    ids = jnp.cumsum(bounds, axis=1).astype(jnp.int32)
    return (ids, handover)


def draw_passage_blocks(key, part):
    return plan_tables(key)[0]


def draw_handover(key, part):
    return plan_tables(key)[1]


def draw_queries(key, part):
    key = jax.random.fold_in(key, 5)
    shape = (N_DP * N_FSDP * NB * BLK, KVH * GROUP * HD)
    values = jnp.clip(jax.random.normal(key, shape), -6.0, 6.0)
    return values.astype(jnp.bfloat16)


def draw_inputs(key, part):
    key = jax.random.fold_in(key, 7)
    shape = (N_DP * N_FSDP * NB * BLK, D)
    values = jnp.clip(jax.random.normal(key, shape), -6.0, 6.0)
    return values.astype(jnp.bfloat16)


def block_scale(key, shape, shards, low, largest):
    gain, own = 1.0, jax.random.fold_in(key, 6)
    for axis_at, parts in shards:
        draws = jnp.exp(jax.random.uniform(jax.random.fold_in(own, axis_at), (parts,), jnp.float32, low / len(shards), largest / len(shards)))
        gain = gain * jnp.repeat(draws, shape[axis_at] // parts).reshape([-1 if axis == axis_at else 1 for axis in range(len(shape))])
    return gain


def bell_draw(stream_key, shape, deviation, reach, shards=(), kind=jnp.bfloat16):
    loudness = block_scale(stream_key, shape, shards, -0.22, 0.18) if shards else 1.0
    drawn = jax.random.normal(stream_key, shape, jnp.float32) * deviation * loudness
    return jnp.minimum(jnp.maximum(drawn, -reach), reach).astype(kind)


def setup_inputs(seed: int = 0) -> dict:
    streams_of = jax.random.split(jax.random.key(seed), 7)
    inputs = draw_inputs(jax.random.fold_in(streams_of[6], 71), 0)
    queries = draw_queries(jax.random.fold_in(streams_of[6], 71), 0)
    out_grad = bell_draw(streams_of[2], (TOKENS, QH * HD), 1.0, 6.0, ((0, 256),))
    kv_weight = bell_draw(streams_of[3], (D, 2 * KVH * HD), D ** -0.5, 0.09375, ((0, 16),))
    passage_blocks = draw_passage_blocks(jax.random.fold_in(streams_of[6], 71), 0)
    handover = draw_handover(jax.random.fold_in(streams_of[6], 71), 0)
    return dict(inputs=inputs, queries=queries, out_grad=out_grad, kv_weight=kv_weight, passage_blocks=passage_blocks, handover=handover)


rope_base = 1000000.0


def block_offsets(ids, block_rows):
    count = ids.shape[0]
    order = jnp.arange(count, dtype=jnp.int32)
    same = ids[:, None] == ids[None, :]
    first = jnp.min(jnp.where(same, order[None, :], count), axis=1).astype(jnp.int32)
    return ((order - first) * block_rows).astype(jnp.int32)


def expand_rows(values, block_rows):
    inner = jnp.zeros((block_rows,), jnp.int32)
    return (values[:, None] + inner[None, :]).reshape(-1)


def row_positions(offsets, block_rows):
    inner = jnp.arange(block_rows, dtype=jnp.int32)
    return (offsets[:, None] + inner[None, :]).reshape(-1)


def rotary(positions):
    half = HD // 2
    freq = rope_base ** (-(jnp.arange(half, dtype=jnp.float32) * 2.0) / HD)
    angle = positions.astype(jnp.float32)[:, None] * freq[None, :]
    cosine = jnp.concatenate([jnp.cos(angle), jnp.cos(angle)], axis=1)
    sine = jnp.concatenate([jnp.sin(angle), jnp.sin(angle)], axis=1)
    return cosine[:, None, :], sine[:, None, :]


def rotate(values, cosine, sine):
    half = HD // 2
    turned = jnp.concatenate([-values[..., half:], values[..., :half]], axis=-1)
    return values * cosine + turned * sine


def unrotate(grads, cosine, sine):
    half = HD // 2
    scaled = grads * sine
    turned = jnp.concatenate([scaled[..., half:], -scaled[..., :half]], axis=-1)
    return grads * cosine + turned


def attend(queries, keys, values, out_grad, labels):
    rows = queries.shape[0]
    scale = 1.0 / (HD ** 0.5)
    q_heads = queries.reshape(rows, KVH, GROUP, HD).astype(jnp.float32)
    k_heads = keys.reshape(rows, KVH, HD).astype(jnp.float32)
    v_heads = values.reshape(rows, KVH, HD).astype(jnp.float32)
    g_heads = out_grad.reshape(rows, KVH, GROUP, HD).astype(jnp.float32)
    scores = jnp.einsum('qghd,kgd->ghqk', q_heads, k_heads) * scale
    same = labels[:, None] == labels[None, :]
    scores = jnp.where(same[None, None], scores, -jnp.inf)
    top = jnp.max(scores, axis=-1, keepdims=True)
    weights = jnp.exp(scores - top)
    probs = weights / jnp.sum(weights, axis=-1, keepdims=True)
    probs_b = probs.astype(jnp.bfloat16).astype(jnp.float32)
    attended = jnp.einsum('ghqk,kgd->qghd', probs_b, v_heads)
    delta = jnp.sum(g_heads * attended, axis=-1)
    dprobs = jnp.einsum('qghd,kgd->ghqk', g_heads, v_heads)
    dscores = probs * (dprobs - jnp.transpose(delta, (1, 2, 0))[..., None])
    dscores_b = dscores.astype(jnp.bfloat16).astype(jnp.float32)
    query_grad = (jnp.einsum('ghqk,kgd->qghd', dscores_b, k_heads) * scale).astype(jnp.bfloat16)
    key_grad = jnp.einsum('ghqk,qghd->kgd', dscores_b, q_heads) * scale
    value_grad = jnp.einsum('ghqk,qghd->kgd', probs_b, g_heads)
    return query_grad.reshape(rows, QH * HD), key_grad, value_grad


def device_grads(inputs, queries, out_grad, labels, positions, kv_weight):
    rows = inputs.shape[0]
    projected = jnp.dot(inputs, kv_weight, preferred_element_type=jnp.float32)
    cosine, sine = rotary(positions)
    raw_keys = projected[:, :KVH * HD].reshape(rows, KVH, HD)
    keys = rotate(raw_keys, cosine, sine).astype(jnp.bfloat16).reshape(rows, KVH * HD)
    values = projected[:, KVH * HD:].astype(jnp.bfloat16)
    query_grad, key_grad, value_grad = attend(queries, keys, values, out_grad, labels)
    raw_key_grad = unrotate(key_grad, cosine, sine)
    kv_grad = jnp.concatenate([raw_key_grad.reshape(rows, KVH * HD), value_grad.reshape(rows, KVH * HD)], axis=1).astype(jnp.bfloat16)
    input_grad = jnp.dot(kv_grad, kv_weight.T, preferred_element_type=jnp.float32).astype(jnp.bfloat16)
    return input_grad, query_grad, kv_grad


def reference(inputs, queries, out_grad, kv_weight, passage_blocks, handover):
    count = N_DP * N_FSDP
    rows = NB * BLK
    x_dev = inputs.reshape(count, rows, D)
    q_dev = queries.reshape(count, rows, QH * HD)
    g_dev = out_grad.reshape(count, rows, QH * HD)

    def one_device(total, packed):
        x_rows, q_rows, g_rows, ids = packed
        labels = expand_rows(ids, BLK)
        positions = row_positions(block_offsets(ids, BLK), BLK)
        input_grad, query_grad, kv_grad = device_grads(x_rows, q_rows, g_rows, labels, positions, kv_weight)
        total = total + jnp.dot(x_rows.T, kv_grad, preferred_element_type=jnp.float32)
        return total, (input_grad, query_grad)

    start = jnp.zeros((D, 2 * KVH * HD), jnp.float32)
    grad_weight, (input_all, query_all) = lax.scan(one_device, start, (x_dev, q_dev, g_dev, passage_blocks))
    device_ids = jnp.arange(count, dtype=jnp.int32)
    partner = jnp.bitwise_xor(device_ids, (N_DP // 2) * N_FSDP).astype(jnp.int32)
    mine = handover
    theirs = handover[partner]
    rank_mine = (jnp.cumsum(mine, axis=1) - 1).astype(jnp.int32)
    rank_theirs = (jnp.cumsum(theirs, axis=1) - 1).astype(jnp.int32)
    select = (mine[:, :, None] == 1) & (theirs[:, None, :] == 1) & (rank_mine[:, :, None] == rank_theirs[:, None, :])
    block_ids = jnp.arange(NB, dtype=jnp.int32)
    picked = jnp.sum(jnp.where(select, block_ids[None, None, :], 0), axis=2).astype(jnp.int32)
    source_block = jnp.where(mine == 1, picked, block_ids[None, :]).astype(jnp.int32)
    source_device = jnp.where(mine == 1, partner[:, None], device_ids[:, None]).astype(jnp.int32)
    flat = (source_device * NB + source_block).reshape(-1).astype(jnp.int32)
    grad_input = input_all.reshape(count * NB, BLK, D)[flat].reshape(count * rows, D)
    grad_query = query_all.reshape(count * NB, BLK, QH * HD)[flat].reshape(count * rows, QH * HD)
    return grad_input, grad_query, grad_weight
```

```python
import functools

import jax
import jax.numpy as jnp
import numpy as np
from jax import lax
from jax.experimental import pallas as pl
from jax.experimental.pallas import tpu as pltpu
from jax.sharding import PartitionSpec as P

KVH = 2
GROUP = 7
HD = 128
QH = 14
NB = 6
BLK = 64
SENT = NB - 1
ROWS = NB * BLK
D = 3584
NX, NZ, NF = 4, 8, 16
SHARD = D // NF
HALF = SHARD // 2
KV = 2 * KVH * HD
ROPE_BASE = 1000000.0
MESH = pl.DeviceIdType.MESH
VMEM = pl.BlockSpec(memory_space=pltpu.VMEM)
LIMIT = 50 * 1024 * 1024
f32, bf16 = jnp.float32, jnp.bfloat16


def place():
    d, f = lax.axis_index("dp"), lax.axis_index("fsdp")
    return d // 8, (d // 2) % NX, d % 2, f // NZ, f % NZ


def device(lo, x, c, hi, z):
    return (lo * 8 + x * 2 + c, hi * NZ + z)


def greet(peers):
    barrier = pltpu.get_barrier_semaphore()
    for peer in peers:
        pl.semaphore_signal(barrier, inc=1, device_id=peer, device_id_type=MESH)
    pl.semaphore_wait(barrier, len(peers))


def columns(index, width=HD):
    return pl.ds(pl.multiple_of(index * width, width), width)


HOPS = {(0, 1): 4, (0, -1): 3, (1, 1): 3, (1, -1): 4}
RINGS = list(HOPS)


def gather_kernel(w_ref, out_ref, send, ring_recv, x_recv, own_recv, far_recv, y_recv):
    lo, x, c, hi, z = place()
    right_z, left_z = (z + 1) % NZ, (z + NZ - 1) % NZ
    z_peer = {1: device(lo, x, c, hi, right_z), -1: device(lo, x, c, hi, left_z)}
    x_peer = {1: device(lo, (x + 1) % NX, c, hi, z), -1: device(lo, (x + NX - 1) % NX, c, hi, z)}
    y_peer = device(1 - lo, x, c, 1 - hi, z)
    sibling = device(lo, x, 1 - c, hi, z)
    greet([z_peer[1], z_peer[-1], x_peer[1], x_peer[-1], y_peer, sibling])
    out_ref[hi, z] = w_ref[...]
    near = columns(2 * (x % 2) + c)
    far = columns(2 * (1 - x % 2) + c)
    side = (hi, 1 - hi)
    started = []

    def push(part, peer, recv):
        copy = pltpu.make_async_remote_copy(
            src_ref=part,
            dst_ref=part,
            send_sem=send.at[len(started)],
            recv_sem=recv,
            device_id=peer,
            device_id_type=MESH,
        )
        copy.start()
        started.append(copy)

    def arrived(part, recv):
        pltpu.make_async_remote_copy(
            src_ref=part,
            dst_ref=part,
            send_sem=send.at[0],
            recv_sem=recv,
            device_id=sibling,
            device_id_type=MESH,
        ).wait_recv()

    def piece(ring, way, hop, cols):
        source = (z + NZ - way * hop) % NZ
        return out_ref.at[side[ring], source, :, cols]

    def slot(ring, way, hop):
        return RINGS.index((ring, way)) * 4 + hop

    push(out_ref.at[hi, z], y_peer, y_recv.at[0])
    for way in (1, -1):
        push(piece(0, way, 0, near), z_peer[way], ring_recv.at[slot(0, way, 0)])
    arrived(out_ref.at[1 - hi, z], y_recv.at[0])
    for way in (-1, 1):
        push(piece(1, way, 0, near), z_peer[way], ring_recv.at[slot(1, way, 0)])

    def across(ring, way, hop):
        part = piece(ring, way, hop, far)
        arrived(part, x_recv.at[slot(ring, way, hop - 1)])
        push(part, sibling, far_recv.at[slot(ring, way, hop - 1)])

    late = []
    for hop in range(1, 5):
        for ring, way in RINGS:
            if hop > HOPS[ring, way]:
                continue
            part = piece(ring, way, hop, near)
            at = slot(ring, way, hop - 1)
            arrived(part, ring_recv.at[at])
            if hop < HOPS[ring, way]:
                push(part, z_peer[way], ring_recv.at[at + 1])
            push(part, x_peer[way], x_recv.at[at])
            push(part, sibling, own_recv.at[at])
            late.append((ring, way, hop))
            if len(late) > 3:
                across(*late.pop(0))
    for item in late:
        across(*item)
    for ring, way in RINGS:
        for hop in range(1, HOPS[ring, way] + 1):
            at = slot(ring, way, hop - 1)
            arrived(piece(ring, way, hop, columns(2 * (x % 2) + 1 - c)), own_recv.at[at])
            arrived(piece(ring, way, hop, columns(2 * (1 - x % 2) + 1 - c)), far_recv.at[at])
    for copy in started:
        copy.wait_send()


def gather_weight(weight):
    dma = pltpu.SemaphoreType.DMA
    out = pl.pallas_call(
        gather_kernel,
        name="gather_weight",
        out_shape=jax.ShapeDtypeStruct((2, NZ, SHARD, KV), bf16),
        in_specs=[VMEM],
        out_specs=VMEM,
        scratch_shapes=[dma((64,)), dma((16,)), dma((16,)), dma((16,)), dma((16,)), dma((1,))],
        compiler_params=pltpu.CompilerParams(
            collective_id=0, has_side_effects=True, vmem_limit_bytes=LIMIT
        ),
    )(weight)
    return out.reshape(D, KV)


def handed_blocks(flags):
    rank, ranks = jnp.int32(0), []
    for b in range(NB):
        ranks.append(rank)
        rank = rank + flags[b]
    picks = []
    for r in range(SENT):
        pick = jnp.int32(0)
        for b in range(NB):
            pick = jnp.where((flags[b] == 1) & (ranks[b] == r), b, pick)
        picks.append(pick)
    return ranks, picks


def dot(a, b, dims):
    return lax.dot_general(a, b, ((dims[:1], dims[1:]), ((), ())), preferred_element_type=f32)


def attend_kernel(
    ids_ref, flags_ref, x_ref, w_ref, freq_ref, q_ref, g_ref,
    qg_ref, qp_ref, kvg_ref, kvp_ref,
    keys, keys_t, vals, kacc, vacc, bias, cosine, sine,
):
    h = pl.program_id(0)
    group = h // GROUP
    member = h % GROUP
    scale = 1.0 / HD**0.5
    picks = handed_blocks([flags_ref[0, b] for b in range(NB)])[1]

    @pl.when(h == 0)
    def _():
        ids = [ids_ref[0, b] for b in range(NB)]
        first = [jnp.int32(0)]
        for b in range(1, NB):
            first.append(jnp.where(ids[b] == ids[b - 1], first[b - 1], b * BLK))
        row = lax.broadcasted_iota(jnp.int32, (ROWS, HD), 0)
        tall = lax.broadcasted_iota(jnp.int32, (ROWS, ROWS), 0)
        wide = lax.broadcasted_iota(jnp.int32, (ROWS, ROWS), 1)
        start = jnp.zeros((ROWS, HD), jnp.int32)
        label_k = jnp.zeros((ROWS, ROWS), jnp.int32)
        label_q = jnp.zeros((ROWS, ROWS), jnp.int32)
        for b in range(NB):
            start = jnp.where(row >= b * BLK, first[b], start)
            label_k = jnp.where(tall >= b * BLK, ids[b], label_k)
            label_q = jnp.where(wide >= b * BLK, ids[b], label_q)
        bias[...] = jnp.where(label_k == label_q, 0.0, -jnp.inf)
        angle = (row - start).astype(f32) * freq_ref[...]
        cosine[...] = jnp.cos(angle)
        lane = lax.broadcasted_iota(jnp.int32, (ROWS, HD), 1)
        turn = jnp.sin(angle)
        sine[...] = jnp.where(lane < HD // 2, -turn, turn)
        projected = dot(x_ref[...], w_ref[...], (1, 0))
        for g in range(KVH):
            raw = projected[:, g * HD : (g + 1) * HD]
            key = raw * cosine[...] + pltpu.roll(raw, HD // 2, 1) * sine[...]
            keys[g] = key.astype(bf16)
            keys_t[g] = key.T.astype(bf16)
            vals[g] = projected[:, (KVH + g) * HD : (KVH + g + 1) * HD].astype(bf16)

    @pl.when(member == 0)
    def _():
        kacc[...] = jnp.zeros_like(kacc)
        vacc[...] = jnp.zeros_like(vacc)

    query, grad = q_ref[...], g_ref[...]
    scores = dot(keys[group], query, (1, 1)) * scale + bias[...]
    weights = jnp.exp(scores - jnp.max(scores, axis=0, keepdims=True))
    probs = weights * (1.0 / jnp.sum(weights, axis=0, keepdims=True))
    probs_b = probs.astype(bf16)
    dprobs = dot(vals[group], grad, (1, 1))
    delta = jnp.sum(probs_b.astype(f32) * dprobs, axis=0, keepdims=True)
    dscores_b = (probs * (dprobs - delta)).astype(bf16)
    vacc[...] += dot(probs_b, grad, (1, 0))
    kacc[...] += dot(dscores_b, query, (1, 0))
    query_grad = dot(keys_t[group], dscores_b, (1, 0)) * scale
    qg_ref[...] = query_grad.T.astype(bf16)
    for r in range(SENT):
        at = pl.ds(pl.multiple_of(picks[r] * BLK, BLK), BLK)
        qp_ref[r * BLK : (r + 1) * BLK, :] = qg_ref[at, :]

    @pl.when(member == GROUP - 1)
    def _():
        grad_k = kacc[...] * scale
        raw = grad_k * cosine[...] - pltpu.roll(grad_k, HD // 2, 1) * sine[...]
        kvg_ref[:, columns(group)] = raw.astype(bf16)
        kvg_ref[:, columns(KVH + group)] = vacc[...].astype(bf16)

    @pl.when(h == QH - 1)
    def _():
        for r in range(SENT):
            at = pl.ds(pl.multiple_of(picks[r] * BLK, BLK), BLK)
            kvp_ref[r * BLK : (r + 1) * BLK, :] = kvg_ref[at, :]


def whole(*shape):
    return pl.BlockSpec(shape, lambda *_: (0,) * len(shape))


def attend(inputs, queries, out_grad, weight, ids, flags):
    freq = ROPE_BASE ** (-(np.arange(HD // 2, dtype=np.float32) * 2.0) / HD)
    freq = jnp.asarray(np.concatenate([freq, freq])[None, :].astype(np.float32))
    head = pl.BlockSpec((ROWS, HD), lambda h, *_: (0, h))
    packed = pl.BlockSpec((SENT * BLK, HD), lambda h, *_: (0, h))
    return pl.pallas_call(
        attend_kernel,
        name="attention_backward",
        out_shape=(
            jax.ShapeDtypeStruct((ROWS, QH * HD), bf16),
            jax.ShapeDtypeStruct((SENT * BLK, QH * HD), bf16),
            jax.ShapeDtypeStruct((ROWS, KV), bf16),
            jax.ShapeDtypeStruct((SENT * BLK, KV), bf16),
        ),
        grid_spec=pltpu.PrefetchScalarGridSpec(
            num_scalar_prefetch=2,
            grid=(QH,),
            in_specs=[whole(ROWS, D), whole(D, KV), whole(1, HD), head, head],
            out_specs=(head, packed, whole(ROWS, KV), whole(SENT * BLK, KV)),
            scratch_shapes=[
                pltpu.VMEM((KVH, ROWS, HD), bf16),
                pltpu.VMEM((KVH, HD, ROWS), bf16),
                pltpu.VMEM((KVH, ROWS, HD), bf16),
                pltpu.VMEM((ROWS, HD), f32),
                pltpu.VMEM((ROWS, HD), f32),
                pltpu.VMEM((ROWS, ROWS), f32),
                pltpu.VMEM((ROWS, HD), f32),
                pltpu.VMEM((ROWS, HD), f32),
            ],
        ),
        compiler_params=pltpu.CompilerParams(vmem_limit_bytes=LIMIT),
    )(ids, flags, inputs, weight, freq, queries, out_grad)


CH = 4
PER = NF // CH


def exchange_kernel(
    x_ref, kvg_ref, qp_ref, kvp_ref,
    qr_ref, kvr_ref, gw_ref,
    part, sib, tot, relay_in, relay_out, direct, summed, after_x, z_in, after_z, y_in, final,
    send, swap_recv, sib_recv, relay_recv, direct_recv, summed_recv, z_recv, y_recv, share_recv,
):
    lo, x, c, hi, z = place()
    y = 2 * hi + lo
    sibling = device(lo, x, 1 - c, hi, z)
    partner = device(1 - lo, x, c, hi, z)
    cross = device(1 - lo, x, c, 1 - hi, z)
    across = device(lo, x, c, 1 - hi, z)
    xp, xm, xo = (x + 1) % NX, (x + NX - 1) % NX, (x + 2) % NX
    x_side = (xp, xm)
    x_peer = [device(lo, xs, c, hi, z) for xs in x_side]
    z_peer = [device(lo, x, c, hi, (z + s) % NZ) for s in range(1, NZ)]
    row_peer = [
        device(lo, (x + dx) % NX, (c + dc) % 2, hi, z)
        for dx in range(NX)
        for dc in range(2)
        if dx or dc
    ]
    greet(row_peer + z_peer + [partner, cross, across])
    started = []

    def push(src, dst, peer, recv):
        copy = pltpu.make_async_remote_copy(
            src_ref=src,
            dst_ref=dst,
            send_sem=send.at[len(started)],
            recv_sem=recv,
            device_id=peer,
            device_id_type=MESH,
        )
        copy.start()
        started.append(copy)

    def arrived(dst, recv):
        pltpu.make_async_remote_copy(
            src_ref=dst,
            dst_ref=dst,
            send_sem=send.at[0],
            recv_sem=recv,
            device_id=sibling,
            device_id_type=MESH,
        ).wait_recv()

    push(kvp_ref, kvr_ref, partner, swap_recv.at[0])
    push(qp_ref, qr_ref, partner, swap_recv.at[1])

    def owners(k):
        return pl.ds(k * PER, PER)

    def sub(k, side):
        return pl.ds(k * PER + 2 * side, 2)

    def box(xs):
        return pl.ds(pl.multiple_of((xs // 2) * HALF, HALF), HALF), columns(xs % 2)

    def chunk_sum(k):
        arrived(sib.at[owners(k)], sib_recv.at[k])
        own = part[owners(k), :, columns(c, 2 * HD)].astype(f32)
        tot[owners(k)] = (own + sib[owners(k)].astype(f32)).astype(bf16)
        far_rows, far_cols = box(xo)
        for side in range(2):
            at = 2 * k + side
            push(
                tot.at[sub(k, side), far_rows, far_cols],
                relay_in.at[at],
                x_peer[side],
                relay_recv.at[at],
            )
        for side in range(2):
            rows, cols = box(x_side[side])
            at = 2 * k + side
            push(tot.at[sub(k, 1 - side), rows, cols], direct.at[at], x_peer[side], direct_recv.at[at])

    def relay(k):
        for side in range(2):
            at = 2 * k + side
            rows, cols = box(x_side[side])
            arrived(relay_in.at[at], relay_recv.at[at])
            mine = tot[sub(k, side), rows, cols].astype(f32)
            relay_out[at] = (mine + relay_in[at].astype(f32)).astype(bf16)
            push(relay_out.at[at], summed.at[at], x_peer[side], summed_recv.at[at])

    def x_total(k):
        rows, cols = box(x)
        for side in range(2):
            at, other = 2 * k + side, 2 * k + 1 - side
            arrived(direct.at[other], direct_recv.at[other])
            arrived(summed.at[at], summed_recv.at[at])
            mine = tot[sub(k, side), rows, cols].astype(f32)
            got = summed[at].astype(f32) + direct[other].astype(f32)
            after_x[sub(k, side)] = (mine + got).astype(bf16)

    for k in range(CH):
        wide = SHARD * PER
        product = dot(x_ref[:, k * wide : (k + 1) * wide], kvg_ref[...], (0, 0))
        part[owners(k)] = product.astype(bf16).reshape(PER, SHARD, KV)
        push(
            part.at[owners(k), :, columns(1 - c, 2 * HD)],
            sib.at[owners(k)],
            sibling,
            sib_recv.at[k],
        )
        if k:
            chunk_sum(k - 1)
    chunk_sum(CH - 1)
    for k in range(CH):
        relay(k)
    for side in range(2):
        for k in (2 * side, 2 * side + 1):
            x_total(k)
        for s in range(1, NZ):
            at = side * (NZ - 1) + s - 1
            push(after_x.at[side * NZ + (z + s) % NZ], z_in.at[at], z_peer[s - 1], z_recv.at[at])
    for side in range(2):
        total = after_x[side * NZ + z].astype(f32)
        for s in range(1, NZ):
            at = side * (NZ - 1) + s - 1
            arrived(z_in.at[at], z_recv.at[at])
            total = total + z_in[at].astype(f32)
        after_z[side] = total.astype(bf16)
    y_in[y] = after_z[hi]
    push(after_z.at[hi], y_in.at[y], partner, y_recv.at[0])
    push(after_z.at[1 - hi], y_in.at[y], cross, y_recv.at[1])
    push(after_z.at[1 - hi], y_in.at[y], across, y_recv.at[2])
    arrived(y_in.at[2 * hi + 1 - lo], y_recv.at[0])
    arrived(y_in.at[2 * (1 - hi) + 1 - lo], y_recv.at[1])
    arrived(y_in.at[2 * (1 - hi) + lo], y_recv.at[2])
    total = y_in[0].astype(f32)
    for at in range(1, 4):
        total = total + y_in[at].astype(f32)
    final[...] = total.astype(bf16)

    def place_of(xs, cs):
        return gw_ref.at[
            pl.ds(pl.multiple_of((xs // 2) * HALF, HALF), HALF), columns(2 * cs + xs % 2)
        ]

    at = 0
    for dx in range(NX):
        for dc in range(2):
            if dx or dc:
                push(final, place_of(x, c), row_peer[at], share_recv.at[at])
                at += 1
    gw_ref[pl.ds(pl.multiple_of((x // 2) * HALF, HALF), HALF), columns(2 * c + x % 2)] = final[...]
    at = 0
    for dx in range(NX):
        for dc in range(2):
            if dx or dc:
                arrived(place_of((x + NX - dx) % NX, (c + dc) % 2), share_recv.at[at])
                at += 1
    arrived(kvr_ref, swap_recv.at[0])
    arrived(qr_ref, swap_recv.at[1])
    for copy in started:
        copy.wait_send()


def exchange(inputs, kv_grad, query_pack, kv_pack):
    dma = pltpu.SemaphoreType.DMA
    quarter = (HALF, HD)
    return pl.pallas_call(
        exchange_kernel,
        name="exchange",
        out_shape=(
            jax.ShapeDtypeStruct((SENT * BLK, QH * HD), bf16),
            jax.ShapeDtypeStruct((SENT * BLK, KV), bf16),
            jax.ShapeDtypeStruct((SHARD, KV), bf16),
        ),
        in_specs=[VMEM] * 4,
        out_specs=(VMEM, VMEM, VMEM),
        scratch_shapes=[
            pltpu.VMEM((NF, SHARD, KV), bf16),
            pltpu.VMEM((NF, SHARD, 2 * HD), bf16),
            pltpu.VMEM((NF, SHARD, 2 * HD), bf16),
            pltpu.VMEM((2 * CH, 2) + quarter, bf16),
            pltpu.VMEM((2 * CH, 2) + quarter, bf16),
            pltpu.VMEM((2 * CH, 2) + quarter, bf16),
            pltpu.VMEM((2 * CH, 2) + quarter, bf16),
            pltpu.VMEM((NF,) + quarter, bf16),
            pltpu.VMEM((2 * (NZ - 1),) + quarter, bf16),
            pltpu.VMEM((2,) + quarter, bf16),
            pltpu.VMEM((4,) + quarter, bf16),
            pltpu.VMEM(quarter, bf16),
            dma((64,)),
            dma((2,)),
            dma((CH,)),
            dma((2 * CH,)),
            dma((2 * CH,)),
            dma((2 * CH,)),
            dma((2 * (NZ - 1),)),
            dma((3,)),
            dma((7,)),
        ],
        compiler_params=pltpu.CompilerParams(
            collective_id=1, has_side_effects=True, vmem_limit_bytes=LIMIT
        ),
    )(inputs, kv_grad, query_pack, kv_pack)


STEPS = 7


def finish_kernel(
    flags_ref, kvg_ref, kvr_ref, w_ref, qg_ref, qr_ref, gw_ref, gi_out, gq_out, gw_out, chosen
):
    flags = [flags_ref[0, b] for b in range(NB)]
    ranks = handed_blocks(flags)[0]

    def select(own, other, b):
        at = jnp.minimum(ranks[b], SENT - 1) * BLK
        taken = other[pl.ds(pl.multiple_of(at, BLK), BLK), :]
        return jnp.where(flags[b] == 1, taken, own[b * BLK : (b + 1) * BLK, :])

    @pl.when(pl.program_id(0) == 0)
    def _():
        for b in range(NB):
            chosen[b * BLK : (b + 1) * BLK, :] = select(kvg_ref, kvr_ref, b)

    gi_out[...] = dot(chosen[...], w_ref[...], (1, 1)).astype(bf16)
    for b in range(NB):
        gq_out[b * BLK : (b + 1) * BLK, :] = select(qg_ref, qr_ref, b)
    gw_out[...] = gw_ref[...].astype(f32)


def finish(flags, kv_grad, kv_recv, weight, query_grad, query_recv, grad_weight):
    def across(rows, width):
        return pl.BlockSpec((rows, width), lambda n, *_: (0, n))

    def down(rows, width):
        return pl.BlockSpec((rows, width), lambda n, *_: (n, 0))

    wide, q_wide, deep = D // STEPS, QH * HD // STEPS, SHARD // STEPS
    return pl.pallas_call(
        finish_kernel,
        name="place_blocks",
        out_shape=(
            jax.ShapeDtypeStruct((ROWS, D), bf16),
            jax.ShapeDtypeStruct((ROWS, QH * HD), bf16),
            jax.ShapeDtypeStruct((SHARD, KV), f32),
        ),
        grid_spec=pltpu.PrefetchScalarGridSpec(
            num_scalar_prefetch=1,
            grid=(STEPS,),
            in_specs=[
                whole(ROWS, KV),
                whole(SENT * BLK, KV),
                down(wide, KV),
                across(ROWS, q_wide),
                across(SENT * BLK, q_wide),
                down(deep, KV),
            ],
            out_specs=(across(ROWS, wide), across(ROWS, q_wide), down(deep, KV)),
            scratch_shapes=[pltpu.VMEM((ROWS, KV), bf16)],
        ),
        compiler_params=pltpu.CompilerParams(vmem_limit_bytes=LIMIT),
    )(flags, kv_grad, kv_recv, weight, query_grad, query_recv, grad_weight)


def shards(inputs, queries, out_grad, kv_weight, passage_blocks, handover):
    weight = gather_weight(kv_weight)
    query_grad, query_pack, kv_grad, kv_pack = attend(
        inputs, queries, out_grad, weight, passage_blocks, handover
    )
    query_recv, kv_recv, share = exchange(inputs, kv_grad, query_pack, kv_pack)
    return finish(handover, kv_grad, kv_recv, weight, query_grad, query_recv, share)


def solution(mesh):
    rows = P(("dp", "fsdp"), None)
    return jax.shard_map(
        shards,
        mesh=mesh,
        in_specs=(rows, rows, rows, P("fsdp", None), rows, rows),
        out_specs=(rows, rows, P("fsdp", None)),
        check_vma=False,
    )
```

```python
import jax
import jax.numpy as jnp
import numpy as np
from jax import lax
from jax.experimental import pallas as pl
from jax.experimental.pallas import tpu as pltpu
from jax.sharding import PartitionSpec as P

KVH = 2
GROUP = 7
HD = 128
QH = 14
NB = 6
BLK = 64
SENT = NB - 1
ROWS = NB * BLK
D = 3584
NX, NZ, NF = 4, 8, 16
SHARD = D // NF
HALF = SHARD // 2
CHUNK = 4 * SHARD
KV = 2 * KVH * HD
ROPE_BASE = 1000000.0
MESH = pl.DeviceIdType.MESH
VMEM = pl.BlockSpec(memory_space=pltpu.VMEM)
LIMIT = 56 * 1024 * 1024
f32, bf16 = jnp.float32, jnp.bfloat16


def place():
    d, f = lax.axis_index("dp"), lax.axis_index("fsdp")
    return d // 8, (d // 2) % NX, d % 2, f // NZ, f % NZ


def device(lo, x, c, hi, z):
    return (lo * 8 + x * 2 + c, hi * NZ + z)


def greet(peers):
    barrier = pltpu.get_barrier_semaphore()
    for peer in peers:
        pl.semaphore_signal(barrier, inc=1, device_id=peer, device_id_type=MESH)
    pl.semaphore_wait(barrier, len(peers))


def columns(index, width=HD):
    return pl.ds(pl.multiple_of(index * width, width), width)


def dot(a, b, dims):
    return lax.dot_general(a, b, ((dims[:1], dims[1:]), ((), ())), preferred_element_type=f32)


def handed_blocks(flags):
    rank, ranks = jnp.int32(0), []
    for b in range(NB):
        ranks.append(rank)
        rank = rank + flags[b]
    picks = []
    for r in range(SENT):
        pick = jnp.int32(0)
        for b in range(NB):
            pick = jnp.where((flags[b] == 1) & (ranks[b] == r), b, pick)
        picks.append(pick)
    return ranks, picks


HOPS = {1: 4, -1: 3}
WAYS = [(1, 1), (-1, 1), (1, 2), (-1, 2), (1, 3), (-1, 3), (1, 4)]


def kernel(
    ids_ref, flags_ref, w_ref, freq_ref, x_hbm, q_hbm, g_hbm,
    gi_hbm, gq_hbm, gw_hbm,
    x_ref, q_ref, g_ref, x_t, weight,
    keys, keys_t, vals, kacc, vacc, bias, cosine, sine, to_pack, from_pack, kept,
    qg, qp, qr, kvg, kvp, kvr, chosen, gi, gq, gw,
    part, sib, tot, relay_in, relay_out, direct, summed, after_x, z_in, after_z, y_in, final, shared,
    load, store, g_send, ring_recv, gy_recv, gx_recv, near_recv, far_recv,
    q_send, q_recv, kv_send, kv_recv,
    d_send, sib_recv, relay_recv, direct_recv, summed_recv, z_recv, y_recv, share_send, share_recv,
):
    lo, x, c, hi, z = place()
    y = 2 * hi + lo
    oth = 1 - hi
    sibling = device(lo, x, 1 - c, hi, z)
    partner = device(1 - lo, x, c, hi, z)
    cross = device(1 - lo, x, c, oth, z)
    across = device(lo, x, c, oth, z)
    x_side = ((x + 1) % NX, (x + NX - 1) % NX)
    x_peer = [device(lo, xs, c, hi, z) for xs in x_side]
    z_peer = [device(lo, x, c, hi, (z + s) % NZ) for s in range(1, NZ)]
    row_peer = [
        device(lo, (x + dx) % NX, (c + dc) % 2, hi, z)
        for dx in range(NX)
        for dc in range(2)
        if dx or dc
    ]
    loads = [
        pltpu.make_async_copy(src, dst, load.at[at])
        for at, (src, dst) in enumerate(((x_hbm, x_ref), (q_hbm, q_ref), (g_hbm, g_ref)))
    ]
    for copy in loads:
        copy.start()
    for q in range(2 * KVH):
        weight[q, hi, z] = w_ref[:, q * HD : (q + 1) * HD]
    greet(row_peer + z_peer + [partner, cross, across])

    def remote(src, dst, peer, sent, recv):
        return pltpu.make_async_remote_copy(
            src_ref=src,
            dst_ref=dst,
            send_sem=sent,
            recv_sem=recv,
            device_id=peer,
            device_id_type=MESH,
        )

    def pusher(sems):
        started = []

        def push(src, dst, peer, recv):
            copy = remote(src, dst, peer, sems.at[len(started)], recv)
            copy.start()
            started.append(copy)

        return push, started

    def arrived(dst, recv):
        remote(dst, dst, sibling, g_send.at[0], recv).wait_recv()

    ids = [ids_ref[0, b] for b in range(NB)]
    flags = [flags_ref[0, b] for b in range(NB)]
    ranks, picks = handed_blocks(flags)

    def set_masks():
        tall = lax.broadcasted_iota(jnp.int32, (ROWS, ROWS), 0)
        wide = lax.broadcasted_iota(jnp.int32, (ROWS, ROWS), 1)
        label_k = jnp.zeros((ROWS, ROWS), jnp.int32)
        label_q = jnp.zeros((ROWS, ROWS), jnp.int32)
        for b in range(NB):
            label_k = jnp.where(tall >= b * BLK, ids[b], label_k)
            label_q = jnp.where(wide >= b * BLK, ids[b], label_q)
        bias[...] = jnp.where(label_k == label_q, 0.0, -jnp.inf)

    def set_moves():
        tall = lax.broadcasted_iota(jnp.int32, (SENT * BLK, ROWS), 0)
        wide = lax.broadcasted_iota(jnp.int32, (SENT * BLK, ROWS), 1)
        shift = jnp.zeros((SENT * BLK, ROWS), jnp.int32)
        for r in range(SENT):
            shift = jnp.where(tall >= r * BLK, (picks[r] - r) * BLK, shift)
        to_pack[...] = jnp.where(tall + shift == wide, 1.0, 0.0).astype(bf16)
        tall = lax.broadcasted_iota(jnp.int32, (ROWS, SENT * BLK), 0)
        wide = lax.broadcasted_iota(jnp.int32, (ROWS, SENT * BLK), 1)
        shift = jnp.zeros((ROWS, SENT * BLK), jnp.int32)
        for b in range(NB):
            shift = jnp.where(tall >= b * BLK, (ranks[b] - b) * BLK, shift)
        from_pack[...] = jnp.where(tall + shift == wide, 1.0, 0.0).astype(bf16)
        row = lax.broadcasted_iota(jnp.int32, (ROWS, HD), 0)
        given = jnp.zeros((ROWS, HD), jnp.int32)
        for b in range(NB):
            given = jnp.where(row >= b * BLK, flags[b], given)
        kept[...] = (1 - given).astype(f32)

    def set_angles():
        first = [jnp.int32(0)]
        for b in range(1, NB):
            first.append(jnp.where(ids[b] == ids[b - 1], first[b - 1], b * BLK))
        row = lax.broadcasted_iota(jnp.int32, (ROWS, HD), 0)
        start = jnp.zeros((ROWS, HD), jnp.int32)
        for b in range(NB):
            start = jnp.where(row >= b * BLK, first[b], start)
        angle = (row - start).astype(f32) * freq_ref[...]
        cosine[...] = jnp.cos(angle)
        lane = lax.broadcasted_iota(jnp.int32, (ROWS, HD), 1)
        turn = jnp.sin(angle)
        sine[...] = jnp.where(lane < HD // 2, -turn, turn)

    def turn_inputs(first, count):
        @pl.loop(first, first + count)
        def _(n):
            x_t[pl.ds(pl.multiple_of(n * HD, HD), HD), :] = x_ref[:, columns(n)].T

    def piece_1():
        loads[0].wait()
        turn_inputs(0, 7)

    def piece_2():
        set_masks()
        turn_inputs(7, 7)

    def piece_3():
        set_angles()
        set_moves()

    def piece_4():
        turn_inputs(14, 14)

    pieces = {1: piece_1, 2: piece_2, 3: piece_3, 4: piece_4}

    near = 2 * (x % 2) + c
    far = 2 * (1 - x % 2) + c
    push, gather_started = pusher(g_send)

    def source(way, hop):
        return (z + NZ - way * hop) % NZ

    def slot(way, hop):
        return 7 if hop == 0 else WAYS.index((way, hop))

    def from_ring(way, hop):
        part = weight.at[near, hi, source(way, hop)]
        at = slot(way, hop)
        arrived(part, ring_recv.at[at])
        if hop < HOPS[way]:
            push(part, part, z_peer[0 if way == 1 else 6], ring_recv.at[slot(way, hop + 1)])
        push(part, part, cross, gy_recv.at[at])
        push(part, part, x_peer[0 if way == 1 else 1], gx_recv.at[at])
        push(part, part, sibling, near_recv.at[at])

    def from_y(way, hop):
        part = weight.at[near, oth, source(way, hop)]
        at = slot(way, hop)
        arrived(part, gy_recv.at[at])
        push(part, part, x_peer[1 if way == 1 and hop else 0], gx_recv.at[8 + at])
        push(part, part, sibling, near_recv.at[8 + at])

    def from_x(row, half, way, hop):
        part = weight.at[far, row, source(way, hop)]
        at = half * 8 + slot(way, hop)
        arrived(part, gx_recv.at[at])
        push(part, part, sibling, far_recv.at[at])

    own = weight.at[near, hi, z]
    push(own, own, z_peer[0], ring_recv.at[slot(1, 1)])
    push(own, own, z_peer[6], ring_recv.at[slot(-1, 1)])
    push(own, own, cross, gy_recv.at[slot(1, 0)])
    for time in range(1, 7):
        for way in (1, -1):
            if time <= HOPS[way]:
                from_ring(way, time)
        if time == 1:
            from_y(1, 0)
        for way in (1, -1):
            if 1 <= time - 1 <= HOPS[way]:
                from_y(way, time - 1)
        if time == 2:
            from_x(oth, 1, 1, 0)
        for way in (1, -1):
            if 1 <= time - 1 <= HOPS[way]:
                from_x(hi, 0, way, time - 1)
            if 1 <= time - 2 <= HOPS[way]:
                from_x(oth, 1, way, time - 2)
        if time in pieces:
            pieces[time]()
    for half, row in ((0, hi), (1, oth)):
        for way, hop in WAYS + [(1, 0)] * half:
            at = half * 8 + slot(way, hop)
            arrived(weight.at[2 * (x % 2) + 1 - c, row, source(way, hop)], near_recv.at[at])
            arrived(weight.at[2 * (1 - x % 2) + 1 - c, row, source(way, hop)], far_recv.at[at])

    def weight_rows(n):
        at = pl.ds((n % 2) * 4, 4)
        return jnp.concatenate(
            [weight[q, n // 2, at].reshape(CHUNK, HD) for q in range(2 * KVH)], axis=1
        )

    projected = jnp.zeros((ROWS, KV), f32)
    for n in range(4):
        projected += dot(x_ref[:, n * CHUNK : (n + 1) * CHUNK], weight_rows(n), (1, 0))
    for g in range(KVH):
        raw = projected[:, g * HD : (g + 1) * HD]
        key = raw * cosine[...] + pltpu.roll(raw, HD // 2, 1) * sine[...]
        keys[g] = key.astype(bf16)
        keys_t[g] = key.T.astype(bf16)
        vals[g] = projected[:, (KVH + g) * HD : (KVH + g + 1) * HD].astype(bf16)
    loads[1].wait()
    loads[2].wait()

    scale = 1.0 / HD**0.5

    def hand_over(h):
        return remote(qp.at[h], qr.at[h], partner, q_send.at[h], q_recv.at[h])

    def heads(g, first, last, send_now):
        @pl.loop(first, last)
        def _(h):
            query, grad = q_ref[:, columns(h)], g_ref[:, columns(h)]
            scores = dot(keys[g], query, (1, 1)) * scale + bias[...]
            weights = jnp.exp(scores - jnp.max(scores, axis=0, keepdims=True))
            probs = weights * (1.0 / jnp.sum(weights, axis=0, keepdims=True))
            probs_b = probs.astype(bf16)
            dprobs = dot(vals[g], grad, (1, 1))
            delta = jnp.sum(probs_b.astype(f32) * dprobs, axis=0, keepdims=True)
            dscores_b = (probs * (dprobs - delta)).astype(bf16)
            vacc[...] += dot(probs_b, grad, (1, 0))
            kacc[...] += dot(dscores_b, query, (1, 0))
            query_grad = dot(keys_t[g], dscores_b, (1, 0)) * scale
            own = query_grad.T.astype(bf16)
            qg[h] = own
            qp[h] = dot(to_pack[...], own, (1, 0)).astype(bf16)
            if send_now:
                hand_over(h).start()

    def clear():
        kacc[...] = jnp.zeros_like(kacc)
        vacc[...] = jnp.zeros_like(vacc)

    def hand_over_kv(g):
        return remote(kvp.at[g], kvr.at[g], partner, kv_send.at[g], kv_recv.at[g])

    def finish_group(g):
        grad_k = kacc[...] * scale
        raw = grad_k * cosine[...] - pltpu.roll(grad_k, HD // 2, 1) * sine[...]
        kvg[g, 0] = raw.astype(bf16)
        kvg[g, 1] = vacc[...].astype(bf16)
        for t in range(2):
            kvp[g, t] = dot(to_pack[...], kvg[g, t], (1, 0)).astype(bf16)
        hand_over_kv(g).start()

    push_d, d_started = pusher(d_send)

    def product(g):
        pair = jnp.concatenate([kvg[g, 0], kvg[g, 1]], axis=1)
        for n in range(4):
            result = dot(x_t[n * CHUNK : (n + 1) * CHUNK, :], pair, (1, 0)).astype(bf16)
            for t in range(2):
                half = result[:, t * HD : (t + 1) * HD]
                part[g, t, n * 4 : (n + 1) * 4] = half.reshape(4, SHARD, HD)
            four = pl.ds(n * 4, 4)
            push_d(part.at[g, 1 - c, four], sib.at[g, four], sibling, sib_recv.at[g * 4 + n])

    def box(xs, side):
        owners = pl.ds((xs % 2) * NZ + 4 * side, 4)
        return owners, pl.ds(pl.multiple_of((xs // 2) * HALF, HALF), HALF)

    def core_sum(g):
        for n in range(4):
            four = pl.ds(n * 4, 4)
            arrived(sib.at[g, four], sib_recv.at[g * 4 + n])
            total = part[g, c, four].astype(f32) + sib[g, four].astype(f32)
            tot[g, four] = total.astype(bf16)
        for side in range(2):
            at = 2 * g + side
            owners, rows = box((x + 2) % NX, side)
            push_d(tot.at[g, owners, rows], relay_in.at[at], x_peer[side], relay_recv.at[at])
        for side in range(2):
            at = 2 * g + side
            owners, rows = box(x_side[side], 1 - side)
            push_d(tot.at[g, owners, rows], direct.at[at], x_peer[side], direct_recv.at[at])

    def relay(g):
        for side in range(2):
            at = 2 * g + side
            owners, rows = box(x_side[side], side)
            arrived(relay_in.at[at], relay_recv.at[at])
            total = tot[g, owners, rows].astype(f32) + relay_in[at].astype(f32)
            relay_out[at] = total.astype(bf16)
            push_d(relay_out.at[at], summed.at[at], x_peer[side], summed_recv.at[at])

    def x_sum(g):
        for side in range(2):
            at, other = 2 * g + side, 2 * g + 1 - side
            owners, rows = box(x, side)
            arrived(direct.at[other], direct_recv.at[other])
            arrived(summed.at[at], summed_recv.at[at])
            got = summed[at].astype(f32) + direct[other].astype(f32)
            total = tot[g, owners, rows].astype(f32) + got
            after_x[g, side * 4 : (side + 1) * 4] = total.astype(bf16)
        for s in range(1, NZ):
            at = g * (NZ - 1) + s - 1
            push_d(after_x.at[g, (z + s) % NZ], z_in.at[at], z_peer[s - 1], z_recv.at[at])

    def z_sum(g):
        total = after_x[g, z].astype(f32)
        for s in range(1, NZ):
            at = g * (NZ - 1) + s - 1
            arrived(z_in.at[at], z_recv.at[at])
            total = total + z_in[at].astype(f32)
        after_z[g] = total.astype(bf16)
        y_in[g, y] = after_z[g]
        for n, peer in enumerate((partner, cross, across)):
            push_d(after_z.at[g], y_in.at[g, y], peer, y_recv.at[3 * g + n])

    def share(g):
        return [
            remote(
                final.at[g],
                shared.at[g, x // 2, c],
                peer,
                share_send.at[g * 7 + n],
                share_recv.at[g * 4 + (x // 2) * 2 + c],
            )
            for n, peer in enumerate(row_peer)
        ]

    def y_sum(g):
        arrived(y_in.at[g, 2 * hi + 1 - lo], y_recv.at[3 * g])
        arrived(y_in.at[g, 2 * oth + 1 - lo], y_recv.at[3 * g + 1])
        arrived(y_in.at[g, 2 * oth + lo], y_recv.at[3 * g + 2])
        total = y_in[g, 0].astype(f32)
        for at in range(1, 4):
            total = total + y_in[g, at].astype(f32)
        final[g] = total.astype(bf16)

        @pl.when(x % 2 == hi)
        def _():
            shared[g, x // 2, c] = final[g]
            for copy in share(g):
                copy.start()

    def collect(g):
        for half in range(2):
            for core in range(2):
                mine = (x % 2 == hi) & (x // 2 == half) & (c == core)

                @pl.when(jnp.logical_not(mine))
                def _():
                    at = g * 4 + half * 2 + core
                    arrived(shared.at[g, half, core], share_recv.at[at])

                gw[half * HALF : (half + 1) * HALF, (core * KVH + g) * HD : (core * KVH + g + 1) * HD] = (
                    shared[g, half, core].astype(f32)
                )

    stores = []

    def put(src, dst):
        copy = pltpu.make_async_copy(src, dst, store.at[len(stores)])
        copy.start()
        stores.append(copy)

    def pick(own, other):
        taken = dot(from_pack[...], other, (1, 0))
        return jnp.where(kept[...] > 0.5, own.astype(f32), taken).astype(bf16)

    def input_grad():
        for g in range(KVH):
            arrived(kvr.at[g], kv_recv.at[g])
        for g in range(KVH):
            for t in range(2):
                at = (t * KVH + g) * HD
                chosen[:, at : at + HD] = pick(kvg[g, t], kvr[g, t])
        for n in range(4):
            cols = slice(n * CHUNK, (n + 1) * CHUNK)
            gi[:, cols] = dot(chosen[...], weight_rows(n), (1, 1)).astype(bf16)
            put(gi.at[:, cols], gi_hbm.at[:, cols])

    def place_queries(first, last):
        @pl.loop(first, last)
        def _(h):
            arrived(qr.at[h], q_recv.at[h])
            gq[:, columns(h)] = pick(qg[h], qr[h])

        cols = slice(first * HD, last * HD)
        put(gq.at[:, cols], gq_hbm.at[:, cols])

    clear()
    heads(0, 0, 7, True)
    finish_group(0)
    clear()
    product(0)
    heads(1, 7, 9, True)
    core_sum(0)
    heads(1, 9, 11, False)
    relay(0)
    heads(1, 11, 13, False)
    x_sum(0)
    heads(1, 13, 14, False)
    finish_group(1)
    for h in range(9, 14):
        hand_over(h).start()
    product(1)
    core_sum(1)
    z_sum(0)
    relay(1)
    y_sum(0)
    x_sum(1)
    input_grad()
    z_sum(1)
    place_queries(0, 7)
    collect(0)
    y_sum(1)
    place_queries(7, 14)
    collect(1)
    put(gw, gw_hbm)
    for copy in gather_started + d_started:
        copy.wait_send()
    for h in range(QH):
        hand_over(h).wait_send()
    for g in range(KVH):
        hand_over_kv(g).wait_send()

        @pl.when(x % 2 == hi)
        def _():
            for copy in share(g):
                copy.wait_send()

    for copy in stores:
        copy.wait()


def shards(inputs, queries, out_grad, kv_weight, passage_blocks, handover):
    freq = ROPE_BASE ** (-(np.arange(HD // 2, dtype=np.float32) * 2.0) / HD)
    freq = jnp.asarray(np.concatenate([freq, freq])[None, :].astype(np.float32))
    dma = pltpu.SemaphoreType.DMA
    anywhere = pl.BlockSpec(memory_space=pl.ANY)
    scalars = pl.BlockSpec(memory_space=pltpu.SMEM)

    def vmem(*shape, kind=bf16):
        return pltpu.VMEM(shape, kind)

    packed = SENT * BLK
    return pl.pallas_call(
        kernel,
        name="grouped_attention_backward",
        out_shape=(
            jax.ShapeDtypeStruct((ROWS, D), bf16),
            jax.ShapeDtypeStruct((ROWS, QH * HD), bf16),
            jax.ShapeDtypeStruct((SHARD, KV), f32),
        ),
        in_specs=[scalars, scalars, VMEM, VMEM, anywhere, anywhere, anywhere],
        out_specs=(anywhere, anywhere, anywhere),
        scratch_shapes=[
            vmem(ROWS, D),
            vmem(ROWS, QH * HD),
            vmem(ROWS, QH * HD),
            vmem(D, ROWS),
            vmem(2 * KVH, 2, NZ, SHARD, HD),
            vmem(KVH, ROWS, HD),
            vmem(KVH, HD, ROWS),
            vmem(KVH, ROWS, HD),
            vmem(ROWS, HD, kind=f32),
            vmem(ROWS, HD, kind=f32),
            vmem(ROWS, ROWS, kind=f32),
            vmem(ROWS, HD, kind=f32),
            vmem(ROWS, HD, kind=f32),
            vmem(packed, ROWS),
            vmem(ROWS, packed),
            vmem(ROWS, HD, kind=f32),
            vmem(QH, ROWS, HD),
            vmem(QH, packed, HD),
            vmem(QH, packed, HD),
            vmem(KVH, 2, ROWS, HD),
            vmem(KVH, 2, packed, HD),
            vmem(KVH, 2, packed, HD),
            vmem(ROWS, KV),
            vmem(ROWS, D),
            vmem(ROWS, QH * HD),
            vmem(SHARD, KV, kind=f32),
            vmem(KVH, 2, NF, SHARD, HD),
            vmem(KVH, NF, SHARD, HD),
            vmem(KVH, NF, SHARD, HD),
            vmem(2 * KVH, 4, HALF, HD),
            vmem(2 * KVH, 4, HALF, HD),
            vmem(2 * KVH, 4, HALF, HD),
            vmem(2 * KVH, 4, HALF, HD),
            vmem(KVH, NZ, HALF, HD),
            vmem(KVH * (NZ - 1), HALF, HD),
            vmem(KVH, HALF, HD),
            vmem(KVH, 4, HALF, HD),
            vmem(KVH, HALF, HD),
            vmem(KVH, 2, 2, HALF, HD),
            dma((3,)),
            dma((8,)),
            dma((64,)),
            dma((8,)),
            dma((8,)),
            dma((16,)),
            dma((16,)),
            dma((16,)),
            dma((QH,)),
            dma((QH,)),
            dma((KVH,)),
            dma((KVH,)),
            dma((48,)),
            dma((8,)),
            dma((4,)),
            dma((4,)),
            dma((4,)),
            dma((KVH * (NZ - 1),)),
            dma((6,)),
            dma((14,)),
            dma((8,)),
        ],
        compiler_params=pltpu.CompilerParams(
            collective_id=0, has_side_effects=True, vmem_limit_bytes=LIMIT
        ),
    )(passage_blocks, handover, kv_weight, freq, inputs, queries, out_grad)

def solution(mesh):
    rows = P(("dp", "fsdp"), None)
    return jax.shard_map(
        shards,
        mesh=mesh,
        in_specs=(rows, rows, rows, P("fsdp", None), rows, rows),
        out_specs=(rows, rows, P("fsdp", None)),
        check_vma=False,
    )
```

```python
import jax
import jax.numpy as jnp
import numpy as np
from jax import lax
from jax.experimental import pallas as pl
from jax.experimental.pallas import tpu as pltpu
from jax.sharding import PartitionSpec as P

KVH = 2
GROUP = 7
HD = 128
QH = 14
NB = 6
BLK = 64
SENT = NB - 1
ROWS = NB * BLK
D = 3584
NX, NZ, NF = 4, 8, 16
SHARD = D // NF
HALF = SHARD // 2
CHUNK = 4 * SHARD
KV = 2 * KVH * HD
ROPE_BASE = 1000000.0
MESH = pl.DeviceIdType.MESH
VMEM = pl.BlockSpec(memory_space=pltpu.VMEM)
LIMIT = 56 * 1024 * 1024
f32, bf16 = jnp.float32, jnp.bfloat16


def place():
    d, f = lax.axis_index("dp"), lax.axis_index("fsdp")
    return d // 8, (d // 2) % NX, d % 2, f // NZ, f % NZ


def device(lo, x, c, hi, z):
    return (lo * 8 + x * 2 + c, hi * NZ + z)


def greet(peers):
    barrier = pltpu.get_barrier_semaphore()
    for peer in peers:
        pl.semaphore_signal(barrier, inc=1, device_id=peer, device_id_type=MESH)
    pl.semaphore_wait(barrier, len(peers))


def columns(index, width=HD):
    return pl.ds(pl.multiple_of(index * width, width), width)


def dot(a, b, dims):
    return lax.dot_general(a, b, ((dims[:1], dims[1:]), ((), ())), preferred_element_type=f32)


def handed_blocks(flags):
    rank, ranks = jnp.int32(0), []
    for b in range(NB):
        ranks.append(rank)
        rank = rank + flags[b]
    picks = []
    for r in range(SENT):
        pick = jnp.int32(0)
        for b in range(NB):
            pick = jnp.where((flags[b] == 1) & (ranks[b] == r), b, pick)
        picks.append(pick)
    return ranks, picks


HOPS = {1: 4, -1: 3}
ARRIVES = {1: 2, 2: 1, 3: 3, 4: 4}
WAYS = [(1, 1), (-1, 1), (1, 2), (-1, 2), (1, 3), (-1, 3), (1, 4)]


def kernel(
    ids_ref, flags_ref, w_ref, freq_ref, x_hbm, q_hbm, g_hbm,
    gi_hbm, gq_hbm, gw_hbm,
    x_ref, q_ref, g_ref, x_t, weight,
    keys, keys_t, vals, kacc, vacc, bias, cosine, sine, to_pack, from_pack, kept,
    qg, qp, qr, kvg, kvp, kvr, chosen, gi, gq, gw,
    part, sib, tot, relay_in, relay_out, direct, summed, after_x, z_in, after_z, y_in, final, shared,
    load, store, g_send, ring_recv, gy_recv, gx_recv, near_recv, far_recv,
    q_send, q_recv, kv_send, kv_recv,
    d_send, sib_recv, relay_recv, direct_recv, summed_recv, z_recv, y_recv, share_send, share_recv,
):
    lo, x, c, hi, z = place()
    y = 2 * hi + lo
    oth = 1 - hi
    sibling = device(lo, x, 1 - c, hi, z)
    partner = device(1 - lo, x, c, hi, z)
    cross = device(1 - lo, x, c, oth, z)
    across = device(lo, x, c, oth, z)
    x_side = ((x + 1) % NX, (x + NX - 1) % NX)
    x_peer = [device(lo, xs, c, hi, z) for xs in x_side]
    z_peer = [device(lo, x, c, hi, (z + s) % NZ) for s in range(1, NZ)]
    row_peer = [
        device(lo, (x + dx) % NX, (c + dc) % 2, hi, z)
        for dx in range(NX)
        for dc in range(2)
        if dx or dc
    ]
    loads = [
        pltpu.make_async_copy(src, dst, load.at[at])
        for at, (src, dst) in enumerate(((x_hbm, x_ref), (q_hbm, q_ref), (g_hbm, g_ref)))
    ]
    for copy in loads:
        copy.start()
    for q in range(2 * KVH):
        weight[q, hi, z] = w_ref[:, q * HD : (q + 1) * HD]
    greet(row_peer + z_peer + [partner, cross, across])

    def remote(src, dst, peer, sent, recv):
        return pltpu.make_async_remote_copy(
            src_ref=src,
            dst_ref=dst,
            send_sem=sent,
            recv_sem=recv,
            device_id=peer,
            device_id_type=MESH,
        )

    def pusher(sems):
        started = []

        def push(src, dst, peer, recv):
            copy = remote(src, dst, peer, sems.at[len(started)], recv)
            copy.start()
            started.append(copy)

        return push, started

    def arrived(dst, recv):
        remote(dst, dst, sibling, g_send.at[0], recv).wait_recv()

    ids = [ids_ref[0, b] for b in range(NB)]
    flags = [flags_ref[0, b] for b in range(NB)]
    ranks, picks = handed_blocks(flags)

    def set_masks():
        tall = lax.broadcasted_iota(jnp.int32, (ROWS, ROWS), 0)
        wide = lax.broadcasted_iota(jnp.int32, (ROWS, ROWS), 1)
        label_k = jnp.zeros((ROWS, ROWS), jnp.int32)
        label_q = jnp.zeros((ROWS, ROWS), jnp.int32)
        for b in range(NB):
            label_k = jnp.where(tall >= b * BLK, ids[b], label_k)
            label_q = jnp.where(wide >= b * BLK, ids[b], label_q)
        bias[...] = jnp.where(label_k == label_q, 0.0, -jnp.inf)

    def set_moves():
        tall = lax.broadcasted_iota(jnp.int32, (SENT * BLK, ROWS), 0)
        wide = lax.broadcasted_iota(jnp.int32, (SENT * BLK, ROWS), 1)
        shift = jnp.zeros((SENT * BLK, ROWS), jnp.int32)
        for r in range(SENT):
            shift = jnp.where(tall >= r * BLK, (picks[r] - r) * BLK, shift)
        to_pack[...] = jnp.where(tall + shift == wide, 1.0, 0.0).astype(bf16)
        tall = lax.broadcasted_iota(jnp.int32, (ROWS, SENT * BLK), 0)
        wide = lax.broadcasted_iota(jnp.int32, (ROWS, SENT * BLK), 1)
        shift = jnp.zeros((ROWS, SENT * BLK), jnp.int32)
        for b in range(NB):
            shift = jnp.where(tall >= b * BLK, (ranks[b] - b) * BLK, shift)
        from_pack[...] = jnp.where(tall + shift == wide, 1.0, 0.0).astype(bf16)
        row = lax.broadcasted_iota(jnp.int32, (ROWS, HD), 0)
        given = jnp.zeros((ROWS, HD), jnp.int32)
        for b in range(NB):
            given = jnp.where(row >= b * BLK, flags[b], given)
        kept[...] = (1 - given).astype(f32)

    def set_angles():
        first = [jnp.int32(0)]
        for b in range(1, NB):
            first.append(jnp.where(ids[b] == ids[b - 1], first[b - 1], b * BLK))
        row = lax.broadcasted_iota(jnp.int32, (ROWS, HD), 0)
        start = jnp.zeros((ROWS, HD), jnp.int32)
        for b in range(NB):
            start = jnp.where(row >= b * BLK, first[b], start)
        angle = (row - start).astype(f32) * freq_ref[...]
        cosine[...] = jnp.cos(angle)
        lane = lax.broadcasted_iota(jnp.int32, (ROWS, HD), 1)
        turn = jnp.sin(angle)
        sine[...] = jnp.where(lane < HD // 2, -turn, turn)

    def turn_inputs(first, count):
        @pl.loop(first, first + count)
        def _(n):
            x_t[pl.ds(pl.multiple_of(n * HD, HD), HD), :] = x_ref[:, columns(n)].T

    def piece_0():
        set_masks()
        set_moves()

    def piece_1():
        loads[0].wait()
        turn_inputs(0, 6)

    def piece_2():
        turn_inputs(6, 6)

    def piece_3():
        set_angles()

    def piece_4():
        turn_inputs(12, 16)

    pieces = {1: piece_1, 2: piece_2, 3: piece_3, 4: piece_4}

    near = 2 * (x % 2) + c
    far = 2 * (1 - x % 2) + c
    push, gather_started = pusher(g_send)

    def source(way, hop):
        return (z + NZ - way * hop) % NZ

    def slot(way, hop):
        return 7 if hop == 0 else WAYS.index((way, hop))

    def from_ring(way, hop):
        part = weight.at[near, hi, source(way, hop)]
        at = slot(way, hop)
        arrived(part, ring_recv.at[at])
        if hop == 2:
            push(part, part, z_peer[0 if way == 1 else 6], ring_recv.at[slot(way, 3)])
            if way == 1:
                push(part, part, z_peer[1], ring_recv.at[slot(way, 4)])
        push(part, part, cross, gy_recv.at[at])
        push(part, part, x_peer[0 if way == 1 else 1], gx_recv.at[at])
        push(part, part, sibling, near_recv.at[at])

    def from_y(way, hop):
        part = weight.at[near, oth, source(way, hop)]
        at = slot(way, hop)
        arrived(part, gy_recv.at[at])
        push(part, part, x_peer[1 if way == 1 and hop else 0], gx_recv.at[8 + at])
        push(part, part, sibling, near_recv.at[8 + at])

    def from_x(row, half, way, hop):
        part = weight.at[far, row, source(way, hop)]
        at = half * 8 + slot(way, hop)
        arrived(part, gx_recv.at[at])
        push(part, part, sibling, far_recv.at[at])

    own = weight.at[near, hi, z]
    push(own, own, z_peer[1], ring_recv.at[slot(1, 2)])
    push(own, own, z_peer[5], ring_recv.at[slot(-1, 2)])
    push(own, own, z_peer[0], ring_recv.at[slot(1, 1)])
    push(own, own, z_peer[6], ring_recv.at[slot(-1, 1)])
    push(own, own, cross, gy_recv.at[slot(1, 0)])
    piece_0()
    for time in range(1, 7):
        for way in (1, -1):
            if time in ARRIVES and ARRIVES[time] <= HOPS[way]:
                from_ring(way, ARRIVES[time])
        if time == 2:
            from_y(1, 0)
        for way in (1, -1):
            if time - 1 in ARRIVES and ARRIVES[time - 1] <= HOPS[way]:
                from_y(way, ARRIVES[time - 1])
        if time == 3:
            from_x(oth, 1, 1, 0)
        for way in (1, -1):
            if time - 1 in ARRIVES and ARRIVES[time - 1] <= HOPS[way]:
                from_x(hi, 0, way, ARRIVES[time - 1])
            if time - 2 in ARRIVES and ARRIVES[time - 2] <= HOPS[way]:
                from_x(oth, 1, way, ARRIVES[time - 2])
        if time in pieces:
            pieces[time]()
    for half, row in ((0, hi), (1, oth)):
        for way, hop in WAYS + [(1, 0)] * half:
            at = half * 8 + slot(way, hop)
            arrived(weight.at[2 * (x % 2) + 1 - c, row, source(way, hop)], near_recv.at[at])
            arrived(weight.at[2 * (1 - x % 2) + 1 - c, row, source(way, hop)], far_recv.at[at])

    def weight_rows(n):
        at = pl.ds((n % 2) * 4, 4)
        return jnp.concatenate(
            [weight[q, n // 2, at].reshape(CHUNK, HD) for q in range(2 * KVH)], axis=1
        )

    projected = jnp.zeros((ROWS, KV), f32)
    for n in range(4):
        projected += dot(x_ref[:, n * CHUNK : (n + 1) * CHUNK], weight_rows(n), (1, 0))
    for g in range(KVH):
        raw = projected[:, g * HD : (g + 1) * HD]
        key = raw * cosine[...] + pltpu.roll(raw, HD // 2, 1) * sine[...]
        keys[g] = key.astype(bf16)
        keys_t[g] = key.T.astype(bf16)
        vals[g] = projected[:, (KVH + g) * HD : (KVH + g + 1) * HD].astype(bf16)
    loads[1].wait()
    loads[2].wait()

    scale = 1.0 / HD**0.5

    def hand_over(h):
        return remote(qp.at[h], qr.at[h], partner, q_send.at[h], q_recv.at[h])

    def heads(g, first, last, send_now):
        for h in range(first, last):
            query, grad = q_ref[:, h * HD : (h + 1) * HD], g_ref[:, h * HD : (h + 1) * HD]
            scores = dot(keys[g], query, (1, 1)) * scale + bias[...]
            weights = jnp.exp(scores - jnp.max(scores, axis=0, keepdims=True))
            probs = weights * (1.0 / jnp.sum(weights, axis=0, keepdims=True))
            probs_b = probs.astype(bf16)
            dprobs = dot(vals[g], grad, (1, 1))
            delta = jnp.sum(probs_b.astype(f32) * dprobs, axis=0, keepdims=True)
            dscores_b = (probs * (dprobs - delta)).astype(bf16)
            vacc[...] += dot(probs_b, grad, (1, 0))
            kacc[...] += dot(dscores_b, query, (1, 0))
            query_grad = dot(keys_t[g], dscores_b, (1, 0)) * scale
            own = query_grad.T.astype(bf16)
            qg[h] = own
            qp[h] = dot(to_pack[...], own, (1, 0)).astype(bf16)
            if send_now:
                hand_over(h).start()

    def clear():
        kacc[...] = jnp.zeros_like(kacc)
        vacc[...] = jnp.zeros_like(vacc)

    def hand_over_kv(g):
        return remote(kvp.at[g], kvr.at[g], partner, kv_send.at[g], kv_recv.at[g])

    def finish_group(g):
        grad_k = kacc[...] * scale
        raw = grad_k * cosine[...] - pltpu.roll(grad_k, HD // 2, 1) * sine[...]
        kvg[g, 0] = raw.astype(bf16)
        kvg[g, 1] = vacc[...].astype(bf16)
        for t in range(2):
            kvp[g, t] = dot(to_pack[...], kvg[g, t], (1, 0)).astype(bf16)
        hand_over_kv(g).start()

    push_d, d_started = pusher(d_send)

    def chunk(i):
        return 2 * (x % 2 if i < 2 else 1 - x % 2) + i % 2

    def product(g, i):
        n = chunk(i)
        pair = jnp.concatenate([kvg[g, 0], kvg[g, 1]], axis=1)
        rows = pl.ds(pl.multiple_of(n * CHUNK, CHUNK), CHUNK)
        result = dot(x_t[rows, :], pair, (1, 0)).astype(bf16)
        four = pl.ds(n * 4, 4)
        for t in range(2):
            part[g, t, four] = result[:, t * HD : (t + 1) * HD].reshape(4, SHARD, HD)
        push_d(part.at[g, 1 - c, four], sib.at[g, four], sibling, sib_recv.at[g * 4 + i])

    def box(xs, side):
        owners = pl.ds((xs % 2) * NZ + 4 * side, 4)
        return owners, pl.ds(pl.multiple_of((xs // 2) * HALF, HALF), HALF)

    def core_sum(g, i):
        four = pl.ds(chunk(i) * 4, 4)
        arrived(sib.at[g, four], sib_recv.at[g * 4 + i])
        total = part[g, c, four].astype(f32) + sib[g, four].astype(f32)
        tot[g, four] = total.astype(bf16)
        if i < 2:
            side, at = i, 2 * g + i
            owners, rows = box((x + 2) % NX, side)
            push_d(tot.at[g, owners, rows], relay_in.at[at], x_peer[side], relay_recv.at[at])
        else:
            side, at = 3 - i, 2 * g + 3 - i
            owners, rows = box(x_side[side], 1 - side)
            push_d(tot.at[g, owners, rows], direct.at[at], x_peer[side], direct_recv.at[at])

    def relay(g):
        for side in range(2):
            at = 2 * g + side
            owners, rows = box(x_side[side], side)
            arrived(relay_in.at[at], relay_recv.at[at])
            total = tot[g, owners, rows].astype(f32) + relay_in[at].astype(f32)
            relay_out[at] = total.astype(bf16)
            push_d(relay_out.at[at], summed.at[at], x_peer[side], summed_recv.at[at])

    def x_sum(g):
        for side in range(2):
            at, other = 2 * g + side, 2 * g + 1 - side
            owners, rows = box(x, side)
            arrived(direct.at[other], direct_recv.at[other])
            arrived(summed.at[at], summed_recv.at[at])
            got = summed[at].astype(f32) + direct[other].astype(f32)
            total = tot[g, owners, rows].astype(f32) + got
            after_x[g, side * 4 : (side + 1) * 4] = total.astype(bf16)
        for s in range(1, NZ):
            at = g * (NZ - 1) + s - 1
            push_d(after_x.at[g, (z + s) % NZ], z_in.at[at], z_peer[s - 1], z_recv.at[at])

    def z_sum(g):
        total = after_x[g, z].astype(f32)
        for s in range(1, NZ):
            at = g * (NZ - 1) + s - 1
            arrived(z_in.at[at], z_recv.at[at])
            total = total + z_in[at].astype(f32)
        after_z[g] = total.astype(bf16)
        y_in[g, y] = after_z[g]
        for n, peer in enumerate((partner, cross, across)):
            push_d(after_z.at[g], y_in.at[g, y], peer, y_recv.at[3 * g + n])

    def share(g):
        return [
            remote(
                final.at[g],
                shared.at[g, x // 2, c],
                peer,
                share_send.at[g * 7 + n],
                share_recv.at[g * 4 + (x // 2) * 2 + c],
            )
            for n, peer in enumerate(row_peer)
        ]

    def y_sum(g):
        arrived(y_in.at[g, 2 * hi + 1 - lo], y_recv.at[3 * g])
        arrived(y_in.at[g, 2 * oth + 1 - lo], y_recv.at[3 * g + 1])
        arrived(y_in.at[g, 2 * oth + lo], y_recv.at[3 * g + 2])
        total = y_in[g, 0].astype(f32)
        for at in range(1, 4):
            total = total + y_in[g, at].astype(f32)
        final[g] = total.astype(bf16)

        @pl.when(x % 2 == hi)
        def _():
            shared[g, x // 2, c] = final[g]
            for copy in share(g):
                copy.start()

    def collect(g):
        for half in range(2):
            for core in range(2):
                mine = (x % 2 == hi) & (x // 2 == half) & (c == core)

                @pl.when(jnp.logical_not(mine))
                def _():
                    at = g * 4 + half * 2 + core
                    arrived(shared.at[g, half, core], share_recv.at[at])

                gw[half * HALF : (half + 1) * HALF, (core * KVH + g) * HD : (core * KVH + g + 1) * HD] = (
                    shared[g, half, core].astype(f32)
                )

    stores = []

    def put(src, dst):
        copy = pltpu.make_async_copy(src, dst, store.at[len(stores)])
        copy.start()
        stores.append(copy)

    def pick(own, other):
        taken = dot(from_pack[...], other, (1, 0))
        return jnp.where(kept[...] > 0.5, own.astype(f32), taken).astype(bf16)

    def input_grad():
        for g in range(KVH):
            arrived(kvr.at[g], kv_recv.at[g])
        for g in range(KVH):
            for t in range(2):
                at = (t * KVH + g) * HD
                chosen[:, at : at + HD] = pick(kvg[g, t], kvr[g, t])
        for n in range(4):
            cols = slice(n * CHUNK, (n + 1) * CHUNK)
            gi[:, cols] = dot(chosen[...], weight_rows(n), (1, 1)).astype(bf16)
            put(gi.at[:, cols], gi_hbm.at[:, cols])

    def place_queries(first, last):
        @pl.loop(first, last)
        def _(h):
            arrived(qr.at[h], q_recv.at[h])
            gq[:, columns(h)] = pick(qg[h], qr[h])

        cols = slice(first * HD, last * HD)
        put(gq.at[:, cols], gq_hbm.at[:, cols])

    clear()
    heads(0, 0, 7, True)
    finish_group(0)
    clear()
    for i in range(4):
        product(0, i)
    heads(1, 7, 8, True)
    for i in range(4):
        core_sum(0, i)
    heads(1, 8, 9, True)
    heads(1, 9, 12, False)
    relay(0)
    heads(1, 12, 14, False)
    finish_group(1)
    product(1, 0)
    product(1, 1)
    core_sum(1, 0)
    product(1, 2)
    core_sum(1, 1)
    product(1, 3)
    core_sum(1, 2)
    core_sum(1, 3)
    for h in range(9, 14):
        hand_over(h).start()
    x_sum(0)
    relay(1)
    z_sum(0)
    x_sum(1)
    input_grad()
    y_sum(0)
    z_sum(1)
    place_queries(0, 7)
    y_sum(1)
    collect(0)
    place_queries(7, 14)
    collect(1)
    put(gw, gw_hbm)
    for copy in gather_started + d_started:
        copy.wait_send()
    for h in range(QH):
        hand_over(h).wait_send()
    for g in range(KVH):
        hand_over_kv(g).wait_send()

        @pl.when(x % 2 == hi)
        def _():
            for copy in share(g):
                copy.wait_send()

    for copy in stores:
        copy.wait()


def write_kernel(*refs):
    sems, copies = refs[6], []
    for src, dst, parts in zip(refs[:3], refs[3:6], (6, 3, 2)):
        rows = src.shape[0] // parts
        for n in range(parts):
            at = pl.ds(n * rows, rows)
            copies.append(pltpu.make_async_copy(src.at[at], dst.at[at], sems.at[len(copies)]))
    for copy in copies:
        copy.start()
    for copy in copies:
        copy.wait()


def shards(inputs, queries, out_grad, kv_weight, passage_blocks, handover):
    freq = ROPE_BASE ** (-(np.arange(HD // 2, dtype=np.float32) * 2.0) / HD)
    freq = jnp.asarray(np.concatenate([freq, freq])[None, :].astype(np.float32))
    dma = pltpu.SemaphoreType.DMA
    anywhere = pl.BlockSpec(memory_space=pl.ANY)
    scalars = pl.BlockSpec(memory_space=pltpu.SMEM)

    def vmem(*shape, kind=bf16):
        return pltpu.VMEM(shape, kind)

    packed = SENT * BLK
    shapes = (
        jax.ShapeDtypeStruct((ROWS, D), bf16),
        jax.ShapeDtypeStruct((ROWS, QH * HD), bf16),
        jax.ShapeDtypeStruct((SHARD, KV), f32),
    )
    results = pl.pallas_call(
        kernel,
        name="grouped_attention_backward",
        out_shape=shapes,
        in_specs=[scalars, scalars, VMEM, VMEM, anywhere, anywhere, anywhere],
        out_specs=(anywhere, anywhere, anywhere),
        scratch_shapes=[
            vmem(ROWS, D),
            vmem(ROWS, QH * HD),
            vmem(ROWS, QH * HD),
            vmem(D, ROWS),
            vmem(2 * KVH, 2, NZ, SHARD, HD),
            vmem(KVH, ROWS, HD),
            vmem(KVH, HD, ROWS),
            vmem(KVH, ROWS, HD),
            vmem(ROWS, HD, kind=f32),
            vmem(ROWS, HD, kind=f32),
            vmem(ROWS, ROWS, kind=f32),
            vmem(ROWS, HD, kind=f32),
            vmem(ROWS, HD, kind=f32),
            vmem(packed, ROWS),
            vmem(ROWS, packed),
            vmem(ROWS, HD, kind=f32),
            vmem(QH, ROWS, HD),
            vmem(QH, packed, HD),
            vmem(QH, packed, HD),
            vmem(KVH, 2, ROWS, HD),
            vmem(KVH, 2, packed, HD),
            vmem(KVH, 2, packed, HD),
            vmem(ROWS, KV),
            vmem(ROWS, D),
            vmem(ROWS, QH * HD),
            vmem(SHARD, KV, kind=f32),
            vmem(KVH, 2, NF, SHARD, HD),
            vmem(KVH, NF, SHARD, HD),
            vmem(KVH, NF, SHARD, HD),
            vmem(2 * KVH, 4, HALF, HD),
            vmem(2 * KVH, 4, HALF, HD),
            vmem(2 * KVH, 4, HALF, HD),
            vmem(2 * KVH, 4, HALF, HD),
            vmem(KVH, NZ, HALF, HD),
            vmem(KVH * (NZ - 1), HALF, HD),
            vmem(KVH, HALF, HD),
            vmem(KVH, 4, HALF, HD),
            vmem(KVH, HALF, HD),
            vmem(KVH, 2, 2, HALF, HD),
            dma((3,)),
            dma((8,)),
            dma((64,)),
            dma((8,)),
            dma((8,)),
            dma((16,)),
            dma((16,)),
            dma((16,)),
            dma((QH,)),
            dma((QH,)),
            dma((KVH,)),
            dma((KVH,)),
            dma((48,)),
            dma((8,)),
            dma((4,)),
            dma((4,)),
            dma((4,)),
            dma((KVH * (NZ - 1),)),
            dma((6,)),
            dma((14,)),
            dma((8,)),
        ],
        compiler_params=pltpu.CompilerParams(
            collective_id=0, has_side_effects=True, vmem_limit_bytes=LIMIT
        ),
    )(passage_blocks, handover, kv_weight, freq, inputs, queries, out_grad)
    return pl.pallas_call(
        write_kernel,
        name="write_results",
        out_shape=shapes,
        in_specs=[anywhere] * 3,
        out_specs=(anywhere,) * 3,
        scratch_shapes=[dma((16,))],
    )(*results)

def solution(mesh):
    rows = P(("dp", "fsdp"), None)
    return jax.shard_map(
        shards,
        mesh=mesh,
        in_specs=(rows, rows, rows, P("fsdp", None), rows, rows),
        out_specs=(rows, rows, P("fsdp", None)),
        check_vma=False,
    )
```

```python
import jax
import jax.numpy as jnp
import numpy as np
from jax import lax
from jax.experimental import pallas as pl
from jax.experimental.pallas import tpu as pltpu
from jax.sharding import PartitionSpec as P

KVH = 2
GROUP = 7
HD = 128
QH = 14
NB = 6
BLK = 64
SENT = NB - 1
ROWS = NB * BLK
D = 3584
NX, NZ, NF = 4, 8, 16
SHARD = D // NF
HALF = SHARD // 2
CHUNK = 4 * SHARD
KV = 2 * KVH * HD
ROPE_BASE = 1000000.0
MESH = pl.DeviceIdType.MESH
VMEM = pl.BlockSpec(memory_space=pltpu.VMEM)
LIMIT = 56 * 1024 * 1024
f32, bf16 = jnp.float32, jnp.bfloat16


def place():
    d, f = lax.axis_index("dp"), lax.axis_index("fsdp")
    return d // 8, (d // 2) % NX, d % 2, f // NZ, f % NZ


def device(lo, x, c, hi, z):
    return (lo * 8 + x * 2 + c, hi * NZ + z)


def greet(peers):
    barrier = pltpu.get_barrier_semaphore()
    for peer in peers:
        pl.semaphore_signal(barrier, inc=1, device_id=peer, device_id_type=MESH)
    pl.semaphore_wait(barrier, len(peers))


def columns(index, width=HD):
    return pl.ds(pl.multiple_of(index * width, width), width)


def dot(a, b, dims):
    return lax.dot_general(a, b, ((dims[:1], dims[1:]), ((), ())), preferred_element_type=f32)


def handed_blocks(flags):
    rank, ranks = jnp.int32(0), []
    for b in range(NB):
        ranks.append(rank)
        rank = rank + flags[b]
    picks = []
    for r in range(SENT):
        pick = jnp.int32(0)
        for b in range(NB):
            pick = jnp.where((flags[b] == 1) & (ranks[b] == r), b, pick)
        picks.append(pick)
    return ranks, picks


HOPS = {1: 4, -1: 3}
LATE = 9
ARRIVES = {1: 2, 2: 1, 3: 3, 4: 4}
WAYS = [(1, 1), (-1, 1), (1, 2), (-1, 2), (1, 3), (-1, 3), (1, 4)]


def kernel(
    ids_ref, flags_ref, w_ref, freq_ref, x_hbm, q_hbm, g_hbm,
    gi, gq, gw,
    x_ref, q_ref, g_ref, x_t, weight,
    keys, keys_t, vals, kacc, vacc, bias, cosine, sine, to_pack, from_pack, kept,
    held, qg, qp, qr, kvg, kvp, kvr, chosen,
    part, sib, tot, relay_in, relay_out, direct, summed, after_x, z_in, after_z, y_in, final, shared,
    load, g_send, ring_recv, gy_recv, gx_recv, near_recv, far_recv,
    q_send, q_recv, kv_send, kv_recv,
    d_send, sib_recv, relay_recv, direct_recv, summed_recv, z_recv, y_recv, share_send, share_recv,
):
    lo, x, c, hi, z = place()
    y = 2 * hi + lo
    oth = 1 - hi
    sibling = device(lo, x, 1 - c, hi, z)
    partner = device(1 - lo, x, c, hi, z)
    cross = device(1 - lo, x, c, oth, z)
    across = device(lo, x, c, oth, z)
    x_side = ((x + 1) % NX, (x + NX - 1) % NX)
    x_peer = [device(lo, xs, c, hi, z) for xs in x_side]
    z_peer = [device(lo, x, c, hi, (z + s) % NZ) for s in range(1, NZ)]
    row_peer = [
        device(lo, (x + dx) % NX, (c + dc) % 2, hi, z)
        for dx in range(NX)
        for dc in range(2)
        if dx or dc
    ]
    loads = [
        pltpu.make_async_copy(src, dst, load.at[at])
        for at, (src, dst) in enumerate(((x_hbm, x_ref), (q_hbm, q_ref), (g_hbm, g_ref)))
    ]
    for copy in loads:
        copy.start()
    for q in range(2 * KVH):
        weight[q, hi, z] = w_ref[:, q * HD : (q + 1) * HD]
    greet(row_peer + z_peer + [partner, cross, across])

    def remote(src, dst, peer, sent, recv):
        return pltpu.make_async_remote_copy(
            src_ref=src,
            dst_ref=dst,
            send_sem=sent,
            recv_sem=recv,
            device_id=peer,
            device_id_type=MESH,
        )

    def pusher(sems):
        started = []

        def push(src, dst, peer, recv):
            copy = remote(src, dst, peer, sems.at[len(started)], recv)
            copy.start()
            started.append(copy)

        return push, started

    def arrived(dst, recv):
        remote(dst, dst, sibling, g_send.at[0], recv).wait_recv()

    ids = [ids_ref[0, b] for b in range(NB)]
    flags = [flags_ref[0, b] for b in range(NB)]
    ranks, picks = handed_blocks(flags)

    def set_masks():
        tall = lax.broadcasted_iota(jnp.int32, (ROWS, ROWS), 0)
        wide = lax.broadcasted_iota(jnp.int32, (ROWS, ROWS), 1)
        label_k = jnp.zeros((ROWS, ROWS), jnp.int32)
        label_q = jnp.zeros((ROWS, ROWS), jnp.int32)
        for b in range(NB):
            label_k = jnp.where(tall >= b * BLK, ids[b], label_k)
            label_q = jnp.where(wide >= b * BLK, ids[b], label_q)
        bias[...] = jnp.where(label_k == label_q, 0.0, -jnp.inf)

    def set_moves():
        tall = lax.broadcasted_iota(jnp.int32, (SENT * BLK, ROWS), 0)
        wide = lax.broadcasted_iota(jnp.int32, (SENT * BLK, ROWS), 1)
        shift = jnp.zeros((SENT * BLK, ROWS), jnp.int32)
        for r in range(SENT):
            shift = jnp.where(tall >= r * BLK, (picks[r] - r) * BLK, shift)
        to_pack[...] = jnp.where(tall + shift == wide, 1.0, 0.0).astype(bf16)
        tall = lax.broadcasted_iota(jnp.int32, (ROWS, SENT * BLK), 0)
        wide = lax.broadcasted_iota(jnp.int32, (ROWS, SENT * BLK), 1)
        shift = jnp.zeros((ROWS, SENT * BLK), jnp.int32)
        for b in range(NB):
            shift = jnp.where(tall >= b * BLK, (ranks[b] - b) * BLK, shift)
        from_pack[...] = jnp.where(tall + shift == wide, 1.0, 0.0).astype(bf16)
        row = lax.broadcasted_iota(jnp.int32, (ROWS, HD), 0)
        given = jnp.zeros((ROWS, HD), jnp.int32)
        for b in range(NB):
            given = jnp.where(row >= b * BLK, flags[b], given)
        kept[...] = (1 - given).astype(f32)

    def set_angles():
        first = [jnp.int32(0)]
        for b in range(1, NB):
            first.append(jnp.where(ids[b] == ids[b - 1], first[b - 1], b * BLK))
        row = lax.broadcasted_iota(jnp.int32, (ROWS, HD), 0)
        start = jnp.zeros((ROWS, HD), jnp.int32)
        for b in range(NB):
            start = jnp.where(row >= b * BLK, first[b], start)
        angle = (row - start).astype(f32) * freq_ref[...]
        cosine[...] = jnp.cos(angle)
        lane = lax.broadcasted_iota(jnp.int32, (ROWS, HD), 1)
        turn = jnp.sin(angle)
        sine[...] = jnp.where(lane < HD // 2, -turn, turn)

    def turn_inputs(first, count):
        @pl.loop(first, first + count)
        def _(n):
            x_t[pl.ds(pl.multiple_of(n * HD, HD), HD), :] = x_ref[:, columns(n)].T

    def piece_0():
        set_masks()
        set_moves()

    def piece_1():
        loads[0].wait()
        turn_inputs(0, 6)

    def piece_2():
        turn_inputs(6, 6)

    def piece_3():
        set_angles()

    def piece_4():
        turn_inputs(12, 16)

    pieces = {1: piece_1, 2: piece_2, 3: piece_3, 4: piece_4}

    push, gather_started = pusher(g_send)

    def source(way, hop):
        return (z + NZ - way * hop) % NZ

    def slot(way, hop):
        return 7 if hop == 0 else WAYS.index((way, hop))

    def piece(p, kind, row, zs, core):
        rows = pl.ds(pl.multiple_of(core * HALF, HALF), HALF)
        return weight.at[KVH * kind + p, row, zs, rows]

    near, far = x % 2, 1 - x % 2

    def gather_start(p):
        own = piece(p, near, hi, z, c)
        push(own, own, z_peer[1], ring_recv.at[p * 8 + slot(1, 2)])
        push(own, own, z_peer[5], ring_recv.at[p * 8 + slot(-1, 2)])
        push(own, own, z_peer[0], ring_recv.at[p * 8 + slot(1, 1)])
        push(own, own, z_peer[6], ring_recv.at[p * 8 + slot(-1, 1)])
        push(own, own, cross, gy_recv.at[p * 8 + slot(1, 0)])

    def from_ring(p, way, hop):
        part = piece(p, near, hi, source(way, hop), c)
        at = slot(way, hop)
        arrived(part, ring_recv.at[p * 8 + at])
        if hop == 2:
            push(part, part, z_peer[0 if way == 1 else 6], ring_recv.at[p * 8 + slot(way, 3)])
            if way == 1:
                push(part, part, z_peer[1], ring_recv.at[p * 8 + slot(way, 4)])
        push(part, part, cross, gy_recv.at[p * 8 + at])
        push(part, part, x_peer[0 if way == 1 else 1], gx_recv.at[p * 16 + at])
        push(part, part, sibling, near_recv.at[p * 16 + at])

    def from_y(p, way, hop):
        part = piece(p, near, oth, source(way, hop), c)
        at = slot(way, hop)
        arrived(part, gy_recv.at[p * 8 + at])
        push(part, part, x_peer[1 if way == 1 and hop else 0], gx_recv.at[p * 16 + 8 + at])
        push(part, part, sibling, near_recv.at[p * 16 + 8 + at])

    def from_x(p, row, half, way, hop):
        part = piece(p, far, row, source(way, hop), c)
        at = p * 16 + half * 8 + slot(way, hop)
        arrived(part, gx_recv.at[at])
        push(part, part, sibling, far_recv.at[at])

    def gather_step(p, time):
        for way in (1, -1):
            if time in ARRIVES and ARRIVES[time] <= HOPS[way]:
                from_ring(p, way, ARRIVES[time])
        if time == 2:
            from_y(p, 1, 0)
        for way in (1, -1):
            if time - 1 in ARRIVES and ARRIVES[time - 1] <= HOPS[way]:
                from_y(p, way, ARRIVES[time - 1])
        if time == 3:
            from_x(p, oth, 1, 1, 0)
        for way in (1, -1):
            if time - 1 in ARRIVES and ARRIVES[time - 1] <= HOPS[way]:
                from_x(p, hi, 0, way, ARRIVES[time - 1])
            if time - 2 in ARRIVES and ARRIVES[time - 2] <= HOPS[way]:
                from_x(p, oth, 1, way, ARRIVES[time - 2])

    def gather_end(p):
        for half, row in ((0, hi), (1, oth)):
            for way, hop in WAYS + [(1, 0)] * half:
                at = p * 16 + half * 8 + slot(way, hop)
                arrived(piece(p, near, row, source(way, hop), 1 - c), near_recv.at[at])
                arrived(piece(p, far, row, source(way, hop), 1 - c), far_recv.at[at])

    def weight_rows(n, blocks=range(2 * KVH)):
        at = pl.ds((n % 2) * 4, 4)
        return jnp.concatenate([weight[q, n // 2, at].reshape(CHUNK, HD) for q in blocks], axis=1)

    def project(g):
        projected = jnp.zeros((ROWS, 2 * HD), f32)
        for n in range(4):
            rows = weight_rows(n, (g, KVH + g))
            projected += dot(x_ref[:, n * CHUNK : (n + 1) * CHUNK], rows, (1, 0))
        raw = projected[:, :HD]
        key = raw * cosine[...] + pltpu.roll(raw, HD // 2, 1) * sine[...]
        keys[g] = key.astype(bf16)
        keys_t[g] = key.T.astype(bf16)
        vals[g] = projected[:, HD:].astype(bf16)

    gather_start(0)
    piece_0()
    for time in range(1, 7):
        gather_step(0, time)
        if time == 4:
            gather_start(1)
        if time in pieces:
            pieces[time]()
    gather_end(0)
    project(0)
    loads[1].wait()
    loads[2].wait()

    scale = 1.0 / HD**0.5

    def hand_over(h):
        return remote(qp.at[h], qr.at[h], partner, q_send.at[h], q_recv.at[h])

    def query_part(g, h, dscores_b):
        own = (dot(keys_t[g], dscores_b, (1, 0)) * scale).T.astype(bf16)
        qg[h] = own
        qp[h] = dot(to_pack[...], own, (1, 0)).astype(bf16)
        hand_over(h).start()

    def late_queries(first, last):
        for h in range(first, last):
            query_part(1, h, held[h - LATE])

    def heads(g, first, last):
        for h in range(first, last):
            query, grad = q_ref[:, h * HD : (h + 1) * HD], g_ref[:, h * HD : (h + 1) * HD]
            scores = dot(keys[g], query, (1, 1)) * scale + bias[...]
            weights = jnp.exp(scores - jnp.max(scores, axis=0, keepdims=True))
            probs = weights * (1.0 / jnp.sum(weights, axis=0, keepdims=True))
            probs_b = probs.astype(bf16)
            dprobs = dot(vals[g], grad, (1, 1))
            delta = jnp.sum(probs_b.astype(f32) * dprobs, axis=0, keepdims=True)
            dscores_b = (probs * (dprobs - delta)).astype(bf16)
            vacc[...] += dot(probs_b, grad, (1, 0))
            kacc[...] += dot(dscores_b, query, (1, 0))
            if h < LATE:
                query_part(g, h, dscores_b)
            else:
                held[h - LATE] = dscores_b

    def clear():
        kacc[...] = jnp.zeros_like(kacc)
        vacc[...] = jnp.zeros_like(vacc)

    def hand_over_kv(g):
        return remote(kvp.at[g], kvr.at[g], partner, kv_send.at[g], kv_recv.at[g])

    def finish_group(g):
        grad_k = kacc[...] * scale
        raw = grad_k * cosine[...] - pltpu.roll(grad_k, HD // 2, 1) * sine[...]
        kvg[g, 0] = raw.astype(bf16)
        kvg[g, 1] = vacc[...].astype(bf16)
        for t in range(2):
            kvp[g, t] = dot(to_pack[...], kvg[g, t], (1, 0)).astype(bf16)
        hand_over_kv(g).start()

    push_d, d_started = pusher(d_send)

    def chunk(i):
        return 2 * (x % 2 if i < 2 else 1 - x % 2) + i % 2

    def product(g, i):
        n = chunk(i)
        pair = jnp.concatenate([kvg[g, 0], kvg[g, 1]], axis=1)
        rows = pl.ds(pl.multiple_of(n * CHUNK, CHUNK), CHUNK)
        result = dot(x_t[rows, :], pair, (1, 0)).astype(bf16)
        four = pl.ds(n * 4, 4)
        for t in range(2):
            part[g, t, four] = result[:, t * HD : (t + 1) * HD].reshape(4, SHARD, HD)
        push_d(part.at[g, 1 - c, four], sib.at[g, four], sibling, sib_recv.at[g * 4 + i])

    def box(xs, side):
        owners = pl.ds((xs % 2) * NZ + 4 * side, 4)
        return owners, pl.ds(pl.multiple_of((xs // 2) * HALF, HALF), HALF)

    def core_sum(g, i):
        four = pl.ds(chunk(i) * 4, 4)
        arrived(sib.at[g, four], sib_recv.at[g * 4 + i])
        total = part[g, c, four].astype(f32) + sib[g, four].astype(f32)
        tot[g, four] = total.astype(bf16)
        if i < 2:
            side, at = i, 2 * g + i
            owners, rows = box((x + 2) % NX, side)
            push_d(tot.at[g, owners, rows], relay_in.at[at], x_peer[side], relay_recv.at[at])
        else:
            side, at = 3 - i, 2 * g + 3 - i
            owners, rows = box(x_side[side], 1 - side)
            push_d(tot.at[g, owners, rows], direct.at[at], x_peer[side], direct_recv.at[at])

    def relay(g):
        for side in range(2):
            at = 2 * g + side
            owners, rows = box(x_side[side], side)
            arrived(relay_in.at[at], relay_recv.at[at])
            total = tot[g, owners, rows].astype(f32) + relay_in[at].astype(f32)
            relay_out[at] = total.astype(bf16)
            push_d(relay_out.at[at], summed.at[at], x_peer[side], summed_recv.at[at])

    def x_sum(g):
        for side in range(2):
            at, other = 2 * g + side, 2 * g + 1 - side
            owners, rows = box(x, side)
            arrived(direct.at[other], direct_recv.at[other])
            arrived(summed.at[at], summed_recv.at[at])
            got = summed[at].astype(f32) + direct[other].astype(f32)
            total = tot[g, owners, rows].astype(f32) + got
            after_x[g, side * 4 : (side + 1) * 4] = total.astype(bf16)
        for s in range(1, NZ):
            at = g * (NZ - 1) + s - 1
            push_d(after_x.at[g, (z + s) % NZ], z_in.at[at], z_peer[s - 1], z_recv.at[at])

    def z_sum(g):
        total = after_x[g, z].astype(f32)
        for s in range(1, NZ):
            at = g * (NZ - 1) + s - 1
            arrived(z_in.at[at], z_recv.at[at])
            total = total + z_in[at].astype(f32)
        after_z[g] = total.astype(bf16)
        y_in[g, y] = after_z[g]
        for n, peer in enumerate((partner, cross, across)):
            push_d(after_z.at[g], y_in.at[g, y], peer, y_recv.at[3 * g + n])

    def share(g):
        return [
            remote(
                final.at[g],
                shared.at[g, x // 2, c],
                peer,
                share_send.at[g * 7 + n],
                share_recv.at[g * 4 + (x // 2) * 2 + c],
            )
            for n, peer in enumerate(row_peer)
        ]

    def y_sum(g):
        arrived(y_in.at[g, 2 * hi + 1 - lo], y_recv.at[3 * g])
        arrived(y_in.at[g, 2 * oth + 1 - lo], y_recv.at[3 * g + 1])
        arrived(y_in.at[g, 2 * oth + lo], y_recv.at[3 * g + 2])
        total = y_in[g, 0].astype(f32)
        for at in range(1, 4):
            total = total + y_in[g, at].astype(f32)
        final[g] = total.astype(bf16)

        @pl.when(x % 2 == hi)
        def _():
            shared[g, x // 2, c] = final[g]
            for copy in share(g):
                copy.start()

    def collect(g):
        for half in range(2):
            for core in range(2):
                mine = (x % 2 == hi) & (x // 2 == half) & (c == core)

                @pl.when(jnp.logical_not(mine))
                def _():
                    at = g * 4 + half * 2 + core
                    arrived(shared.at[g, half, core], share_recv.at[at])

                gw[half * HALF : (half + 1) * HALF, (core * KVH + g) * HD : (core * KVH + g + 1) * HD] = (
                    shared[g, half, core].astype(f32)
                )

    def pick(own, other):
        taken = dot(from_pack[...], other, (1, 0))
        return jnp.where(kept[...] > 0.5, own.astype(f32), taken).astype(bf16)

    def input_grad():
        for g in range(KVH):
            arrived(kvr.at[g], kv_recv.at[g])
        for g in range(KVH):
            for t in range(2):
                at = (t * KVH + g) * HD
                chosen[:, at : at + HD] = pick(kvg[g, t], kvr[g, t])
        for n in range(4):
            cols = slice(n * CHUNK, (n + 1) * CHUNK)
            gi[:, cols] = dot(chosen[...], weight_rows(n), (1, 1)).astype(bf16)

    def place_queries(first, last):
        @pl.loop(first, last)
        def _(h):
            arrived(qr.at[h], q_recv.at[h])
            gq[:, columns(h)] = pick(qg[h], qr[h])

    clear()
    for h in range(GROUP):
        heads(0, h, h + 1)
        if h < 6:
            gather_step(1, h + 1)
    finish_group(0)
    clear()
    for i in range(4):
        product(0, i)
    gather_end(1)
    project(1)
    for i in range(4):
        core_sum(0, i)
    heads(1, 7, 11)
    relay(0)
    heads(1, 11, 14)
    finish_group(1)
    product(1, 0)
    product(1, 1)
    core_sum(1, 0)
    product(1, 2)
    core_sum(1, 1)
    product(1, 3)
    core_sum(1, 2)
    core_sum(1, 3)
    x_sum(0)
    late_queries(9, 12)
    relay(1)
    z_sum(0)
    late_queries(12, 14)
    x_sum(1)
    y_sum(0)
    input_grad()
    z_sum(1)
    place_queries(0, 7)
    y_sum(1)
    collect(0)
    place_queries(7, 14)
    collect(1)
    for copy in gather_started + d_started:
        copy.wait_send()
    for h in range(QH):
        hand_over(h).wait_send()
    for g in range(KVH):
        hand_over_kv(g).wait_send()

        @pl.when(x % 2 == hi)
        def _():
            for copy in share(g):
                copy.wait_send()


def shards(inputs, queries, out_grad, kv_weight, passage_blocks, handover):
    freq = ROPE_BASE ** (-(np.arange(HD // 2, dtype=np.float32) * 2.0) / HD)
    freq = jnp.asarray(np.concatenate([freq, freq])[None, :].astype(np.float32))
    dma = pltpu.SemaphoreType.DMA
    anywhere = pl.BlockSpec(memory_space=pl.ANY)
    scalars = pl.BlockSpec(memory_space=pltpu.SMEM)

    def vmem(*shape, kind=bf16):
        return pltpu.VMEM(shape, kind)

    packed = SENT * BLK
    shapes = (
        jax.ShapeDtypeStruct((ROWS, D), bf16),
        jax.ShapeDtypeStruct((ROWS, QH * HD), bf16),
        jax.ShapeDtypeStruct((SHARD, KV), f32),
    )
    return pl.pallas_call(
        kernel,
        name="grouped_attention_backward",
        out_shape=tuple(pltpu.VMEM(shape.shape, shape.dtype) for shape in shapes),
        in_specs=[scalars, scalars, VMEM, VMEM, anywhere, anywhere, anywhere],
        out_specs=(VMEM, VMEM, VMEM),
        scratch_shapes=[
            vmem(ROWS, D),
            vmem(ROWS, QH * HD),
            vmem(ROWS, QH * HD),
            vmem(D, ROWS),
            vmem(2 * KVH, 2, NZ, SHARD, HD),
            vmem(KVH, ROWS, HD),
            vmem(KVH, HD, ROWS),
            vmem(KVH, ROWS, HD),
            vmem(ROWS, HD, kind=f32),
            vmem(ROWS, HD, kind=f32),
            vmem(ROWS, ROWS, kind=f32),
            vmem(ROWS, HD, kind=f32),
            vmem(ROWS, HD, kind=f32),
            vmem(packed, ROWS),
            vmem(ROWS, packed),
            vmem(ROWS, HD, kind=f32),
            vmem(QH - LATE, ROWS, ROWS),
            vmem(QH, ROWS, HD),
            vmem(QH, packed, HD),
            vmem(QH, packed, HD),
            vmem(KVH, 2, ROWS, HD),
            vmem(KVH, 2, packed, HD),
            vmem(KVH, 2, packed, HD),
            vmem(ROWS, KV),
            vmem(KVH, 2, NF, SHARD, HD),
            vmem(KVH, NF, SHARD, HD),
            vmem(KVH, NF, SHARD, HD),
            vmem(2 * KVH, 4, HALF, HD),
            vmem(2 * KVH, 4, HALF, HD),
            vmem(2 * KVH, 4, HALF, HD),
            vmem(2 * KVH, 4, HALF, HD),
            vmem(KVH, NZ, HALF, HD),
            vmem(KVH * (NZ - 1), HALF, HD),
            vmem(KVH, HALF, HD),
            vmem(KVH, 4, HALF, HD),
            vmem(KVH, HALF, HD),
            vmem(KVH, 2, 2, HALF, HD),
            dma((3,)),
            dma((128,)),
            dma((16,)),
            dma((16,)),
            dma((32,)),
            dma((32,)),
            dma((32,)),
            dma((QH,)),
            dma((QH,)),
            dma((KVH,)),
            dma((KVH,)),
            dma((48,)),
            dma((8,)),
            dma((4,)),
            dma((4,)),
            dma((4,)),
            dma((KVH * (NZ - 1),)),
            dma((6,)),
            dma((14,)),
            dma((8,)),
        ],
        compiler_params=pltpu.CompilerParams(
            collective_id=0, has_side_effects=True, vmem_limit_bytes=LIMIT
        ),
    )(passage_blocks, handover, kv_weight, freq, inputs, queries, out_grad)


def solution(mesh):
    rows = P(("dp", "fsdp"), None)
    return jax.shard_map(
        shards,
        mesh=mesh,
        in_specs=(rows, rows, rows, P("fsdp", None), rows, rows),
        out_specs=(rows, rows, P("fsdp", None)),
        check_vma=False,
    )
```

```python
import jax
import jax.numpy as jnp
import numpy as np
from jax import lax
from jax.experimental import pallas as pl
from jax.experimental.pallas import tpu as pltpu
from jax.sharding import PartitionSpec as P

KVH = 2
GROUP = 7
HD = 128
QH = 14
NB = 6
BLK = 64
SENT = NB - 1
ROWS = NB * BLK
D = 3584
NX, NZ, NF = 4, 8, 16
SHARD = D // NF
HALF = SHARD // 2
CHUNK = 4 * SHARD
KV = 2 * KVH * HD
ROPE_BASE = 1000000.0
MESH = pl.DeviceIdType.MESH
VMEM = pl.BlockSpec(memory_space=pltpu.VMEM)
LIMIT = 56 * 1024 * 1024
f32, bf16 = jnp.float32, jnp.bfloat16


def place():
    d, f = lax.axis_index("dp"), lax.axis_index("fsdp")
    return d // 8, (d // 2) % NX, d % 2, f // NZ, f % NZ


def device(lo, x, c, hi, z):
    return (lo * 8 + x * 2 + c, hi * NZ + z)


def greet(peers):
    barrier = pltpu.get_barrier_semaphore()
    for peer in peers:
        pl.semaphore_signal(barrier, inc=1, device_id=peer, device_id_type=MESH)
    pl.semaphore_wait(barrier, len(peers))


def columns(index, width=HD):
    return pl.ds(pl.multiple_of(index * width, width), width)


def dot(a, b, dims):
    return lax.dot_general(a, b, ((dims[:1], dims[1:]), ((), ())), preferred_element_type=f32)


def handed_blocks(flags):
    rank, ranks = jnp.int32(0), []
    for b in range(NB):
        ranks.append(rank)
        rank = rank + flags[b]
    picks = []
    for r in range(SENT):
        pick = jnp.int32(0)
        for b in range(NB):
            pick = jnp.where((flags[b] == 1) & (ranks[b] == r), b, pick)
        picks.append(pick)
    return ranks, picks


HOPS = {1: 4, -1: 3}
LATE = 9
ARRIVES = {1: 2, 2: 1, 3: 3, 4: 4}
WAYS = [(1, 1), (-1, 1), (1, 2), (-1, 2), (1, 3), (-1, 3), (1, 4)]


def kernel(
    ids_ref, flags_ref, w_ref, freq_ref, x_hbm, q_hbm, g_hbm,
    gi, gq, gw,
    x_ref, q_ref, g_ref, x_t, weight,
    keys, keys_t, vals, kacc, vacc, bias, cosine, sine, to_pack, from_pack, kept,
    held, qg, qp, qr, kvg, kvp, kvr, chosen,
    part, sib, tot, relay_in, relay_out, direct, summed, after_x, z_in, after_z, y_in, final, shared,
    load, g_send, ring_recv, gy_recv, gx_recv, near_recv, far_recv,
    q_send, q_recv, kv_send, kv_recv,
    d_send, sib_recv, relay_recv, direct_recv, summed_recv, z_recv, y_recv, share_send, share_recv,
):
    lo, x, c, hi, z = place()
    y = 2 * hi + lo
    oth = 1 - hi
    sibling = device(lo, x, 1 - c, hi, z)
    partner = device(1 - lo, x, c, hi, z)
    cross = device(1 - lo, x, c, oth, z)
    across = device(lo, x, c, oth, z)
    x_side = ((x + 1) % NX, (x + NX - 1) % NX)
    x_peer = [device(lo, xs, c, hi, z) for xs in x_side]
    z_peer = [device(lo, x, c, hi, (z + s) % NZ) for s in range(1, NZ)]
    row_peer = [
        device(lo, (x + dx) % NX, (c + dc) % 2, hi, z)
        for dx in range(NX)
        for dc in range(2)
        if dx or dc
    ]
    loads = [
        pltpu.make_async_copy(src, dst, load.at[at])
        for at, (src, dst) in enumerate(((x_hbm, x_ref), (q_hbm, q_ref), (g_hbm, g_ref)))
    ]
    for copy in loads:
        copy.start()
    for q in range(2 * KVH):
        weight[q, hi, z] = w_ref[:, q * HD : (q + 1) * HD]
    greet(row_peer + z_peer + [partner, cross, across])

    def remote(src, dst, peer, sent, recv):
        return pltpu.make_async_remote_copy(
            src_ref=src,
            dst_ref=dst,
            send_sem=sent,
            recv_sem=recv,
            device_id=peer,
            device_id_type=MESH,
        )

    def pusher(sems):
        started = []

        def push(src, dst, peer, recv):
            copy = remote(src, dst, peer, sems.at[len(started)], recv)
            copy.start()
            started.append(copy)

        return push, started

    def arrived(dst, recv):
        remote(dst, dst, sibling, g_send.at[0], recv).wait_recv()

    ids = [ids_ref[0, b] for b in range(NB)]
    flags = [flags_ref[0, b] for b in range(NB)]
    ranks, picks = handed_blocks(flags)

    def set_masks():
        tall = lax.broadcasted_iota(jnp.int32, (ROWS, ROWS), 0)
        wide = lax.broadcasted_iota(jnp.int32, (ROWS, ROWS), 1)
        label_k = jnp.zeros((ROWS, ROWS), jnp.int32)
        label_q = jnp.zeros((ROWS, ROWS), jnp.int32)
        for b in range(NB):
            label_k = jnp.where(tall >= b * BLK, ids[b], label_k)
            label_q = jnp.where(wide >= b * BLK, ids[b], label_q)
        bias[...] = jnp.where(label_k == label_q, 0.0, -jnp.inf)

    def set_moves():
        tall = lax.broadcasted_iota(jnp.int32, (SENT * BLK, ROWS), 0)
        wide = lax.broadcasted_iota(jnp.int32, (SENT * BLK, ROWS), 1)
        shift = jnp.zeros((SENT * BLK, ROWS), jnp.int32)
        for r in range(SENT):
            shift = jnp.where(tall >= r * BLK, (picks[r] - r) * BLK, shift)
        to_pack[...] = jnp.where(tall + shift == wide, 1.0, 0.0).astype(bf16)
        tall = lax.broadcasted_iota(jnp.int32, (ROWS, SENT * BLK), 0)
        wide = lax.broadcasted_iota(jnp.int32, (ROWS, SENT * BLK), 1)
        shift = jnp.zeros((ROWS, SENT * BLK), jnp.int32)
        for b in range(NB):
            shift = jnp.where(tall >= b * BLK, (ranks[b] - b) * BLK, shift)
        from_pack[...] = jnp.where(tall + shift == wide, 1.0, 0.0).astype(bf16)
        row = lax.broadcasted_iota(jnp.int32, (ROWS, HD), 0)
        given = jnp.zeros((ROWS, HD), jnp.int32)
        for b in range(NB):
            given = jnp.where(row >= b * BLK, flags[b], given)
        kept[...] = (1 - given).astype(f32)

    def set_angles():
        first = [jnp.int32(0)]
        for b in range(1, NB):
            first.append(jnp.where(ids[b] == ids[b - 1], first[b - 1], b * BLK))
        row = lax.broadcasted_iota(jnp.int32, (ROWS, HD), 0)
        start = jnp.zeros((ROWS, HD), jnp.int32)
        for b in range(NB):
            start = jnp.where(row >= b * BLK, first[b], start)
        angle = (row - start).astype(f32) * freq_ref[...]
        cosine[...] = jnp.cos(angle)
        lane = lax.broadcasted_iota(jnp.int32, (ROWS, HD), 1)
        turn = jnp.sin(angle)
        sine[...] = jnp.where(lane < HD // 2, -turn, turn)

    def turn_inputs(first, count):
        @pl.loop(first, first + count)
        def _(n):
            x_t[pl.ds(pl.multiple_of(n * HD, HD), HD), :] = x_ref[:, columns(n)].T

    def piece_0():
        set_masks()
        set_moves()

    def piece_1():
        loads[0].wait()
        turn_inputs(0, 6)

    def piece_2():
        turn_inputs(6, 6)

    def piece_3():
        set_angles()

    def piece_4():
        turn_inputs(12, 16)

    pieces = {1: piece_1, 2: piece_2, 3: piece_3, 4: piece_4}

    push, gather_started = pusher(g_send)

    def source(way, hop):
        return (z + NZ - way * hop) % NZ

    def slot(way, hop):
        return 7 if hop == 0 else WAYS.index((way, hop))

    def piece(p, kind, row, zs, core):
        rows = pl.ds(pl.multiple_of(core * HALF, HALF), HALF)
        return weight.at[KVH * kind + p, row, zs, rows]

    near, far = x % 2, 1 - x % 2

    def gather_start(p):
        own = piece(p, near, hi, z, c)
        push(own, own, z_peer[1], ring_recv.at[p * 8 + slot(1, 2)])
        push(own, own, z_peer[5], ring_recv.at[p * 8 + slot(-1, 2)])
        push(own, own, z_peer[0], ring_recv.at[p * 8 + slot(1, 1)])
        push(own, own, z_peer[6], ring_recv.at[p * 8 + slot(-1, 1)])
        push(own, own, cross, gy_recv.at[p * 8 + slot(1, 0)])

    def from_ring(p, way, hop):
        part = piece(p, near, hi, source(way, hop), c)
        at = slot(way, hop)
        arrived(part, ring_recv.at[p * 8 + at])
        if hop == 2:
            push(part, part, z_peer[0 if way == 1 else 6], ring_recv.at[p * 8 + slot(way, 3)])
            if way == 1:
                push(part, part, z_peer[1], ring_recv.at[p * 8 + slot(way, 4)])
        push(part, part, cross, gy_recv.at[p * 8 + at])
        push(part, part, x_peer[0 if way == 1 else 1], gx_recv.at[p * 16 + at])
        push(part, part, sibling, near_recv.at[p * 16 + at])

    def from_y(p, way, hop):
        part = piece(p, near, oth, source(way, hop), c)
        at = slot(way, hop)
        arrived(part, gy_recv.at[p * 8 + at])
        push(part, part, x_peer[1 if way == 1 and hop else 0], gx_recv.at[p * 16 + 8 + at])
        push(part, part, sibling, near_recv.at[p * 16 + 8 + at])

    def from_x(p, row, half, way, hop):
        part = piece(p, far, row, source(way, hop), c)
        at = p * 16 + half * 8 + slot(way, hop)
        arrived(part, gx_recv.at[at])
        push(part, part, sibling, far_recv.at[at])

    def gather_step(p, time):
        for way in (1, -1):
            if time in ARRIVES and ARRIVES[time] <= HOPS[way]:
                from_ring(p, way, ARRIVES[time])
        if time == 2:
            from_y(p, 1, 0)
        for way in (1, -1):
            if time - 1 in ARRIVES and ARRIVES[time - 1] <= HOPS[way]:
                from_y(p, way, ARRIVES[time - 1])
        if time == 3:
            from_x(p, oth, 1, 1, 0)
        for way in (1, -1):
            if time - 1 in ARRIVES and ARRIVES[time - 1] <= HOPS[way]:
                from_x(p, hi, 0, way, ARRIVES[time - 1])
            if time - 2 in ARRIVES and ARRIVES[time - 2] <= HOPS[way]:
                from_x(p, oth, 1, way, ARRIVES[time - 2])

    def gather_end(p):
        for half, row in ((0, hi), (1, oth)):
            for way, hop in WAYS + [(1, 0)] * half:
                at = p * 16 + half * 8 + slot(way, hop)
                arrived(piece(p, near, row, source(way, hop), 1 - c), near_recv.at[at])
                arrived(piece(p, far, row, source(way, hop), 1 - c), far_recv.at[at])

    def weight_rows(n, blocks=range(2 * KVH)):
        at = pl.ds((n % 2) * 4, 4)
        return jnp.concatenate([weight[q, n // 2, at].reshape(CHUNK, HD) for q in blocks], axis=1)

    def project(g):
        projected = jnp.zeros((ROWS, 2 * HD), f32)
        for n in range(4):
            rows = weight_rows(n, (g, KVH + g))
            projected += dot(x_ref[:, n * CHUNK : (n + 1) * CHUNK], rows, (1, 0))
        raw = projected[:, :HD]
        key = raw * cosine[...] + pltpu.roll(raw, HD // 2, 1) * sine[...]
        keys[g] = key.astype(bf16)
        keys_t[g] = key.T.astype(bf16)
        vals[g] = projected[:, HD:].astype(bf16)

    gather_start(0)
    piece_0()
    for time in range(1, 7):
        gather_step(0, time)
        if time == 2:
            gather_start(1)
        if time in pieces:
            pieces[time]()
    gather_step(1, 1)
    gather_end(0)
    project(0)
    gather_step(1, 2)
    loads[1].wait()
    loads[2].wait()

    scale = 1.0 / HD**0.5

    def hand_over(h):
        return remote(qp.at[h], qr.at[h], partner, q_send.at[h], q_recv.at[h])

    def query_part(g, h, dscores_b):
        own = (dot(keys_t[g], dscores_b, (1, 0)) * scale).T.astype(bf16)
        qg[h] = own
        qp[h] = dot(to_pack[...], own, (1, 0)).astype(bf16)
        hand_over(h).start()

    def late_queries(first, last):
        for h in range(first, last):
            query_part(1, h, held[h - LATE])

    def heads(g, first, last):
        for h in range(first, last):
            query, grad = q_ref[:, h * HD : (h + 1) * HD], g_ref[:, h * HD : (h + 1) * HD]
            scores = dot(keys[g], query, (1, 1)) * scale + bias[...]
            weights = jnp.exp(scores - jnp.max(scores, axis=0, keepdims=True))
            probs = weights * (1.0 / jnp.sum(weights, axis=0, keepdims=True))
            probs_b = probs.astype(bf16)
            dprobs = dot(vals[g], grad, (1, 1))
            delta = jnp.sum(probs_b.astype(f32) * dprobs, axis=0, keepdims=True)
            dscores_b = (probs * (dprobs - delta)).astype(bf16)
            vacc[...] += dot(probs_b, grad, (1, 0))
            kacc[...] += dot(dscores_b, query, (1, 0))
            if h < LATE:
                query_part(g, h, dscores_b)
            else:
                held[h - LATE] = dscores_b

    def clear():
        kacc[...] = jnp.zeros_like(kacc)
        vacc[...] = jnp.zeros_like(vacc)

    def hand_over_kv(g):
        return remote(kvp.at[g], kvr.at[g], partner, kv_send.at[g], kv_recv.at[g])

    def finish_group(g):
        grad_k = kacc[...] * scale
        raw = grad_k * cosine[...] - pltpu.roll(grad_k, HD // 2, 1) * sine[...]
        kvg[g, 0] = raw.astype(bf16)
        kvg[g, 1] = vacc[...].astype(bf16)
        for t in range(2):
            kvp[g, t] = dot(to_pack[...], kvg[g, t], (1, 0)).astype(bf16)
        hand_over_kv(g).start()

    push_d, d_started = pusher(d_send)

    def chunk(i):
        return 2 * (x % 2 if i < 2 else 1 - x % 2) + i % 2

    def product(g, i):
        n = chunk(i)
        pair = jnp.concatenate([kvg[g, 0], kvg[g, 1]], axis=1)
        rows = pl.ds(pl.multiple_of(n * CHUNK, CHUNK), CHUNK)
        result = dot(x_t[rows, :], pair, (1, 0)).astype(bf16)
        four = pl.ds(n * 4, 4)
        for t in range(2):
            part[g, t, four] = result[:, t * HD : (t + 1) * HD].reshape(4, SHARD, HD)
        push_d(part.at[g, 1 - c, four], sib.at[g, four], sibling, sib_recv.at[g * 4 + i])

    def box(xs, side):
        owners = pl.ds((xs % 2) * NZ + 4 * side, 4)
        return owners, pl.ds(pl.multiple_of((xs // 2) * HALF, HALF), HALF)

    def core_sum(g, i):
        four = pl.ds(chunk(i) * 4, 4)
        arrived(sib.at[g, four], sib_recv.at[g * 4 + i])
        total = part[g, c, four].astype(f32) + sib[g, four].astype(f32)
        tot[g, four] = total.astype(bf16)
        if i < 2:
            side, at = i, 2 * g + i
            owners, rows = box((x + 2) % NX, side)
            push_d(tot.at[g, owners, rows], relay_in.at[at], x_peer[side], relay_recv.at[at])
        else:
            side, at = 3 - i, 2 * g + 3 - i
            owners, rows = box(x_side[side], 1 - side)
            push_d(tot.at[g, owners, rows], direct.at[at], x_peer[side], direct_recv.at[at])

    def relay(g):
        for side in range(2):
            at = 2 * g + side
            owners, rows = box(x_side[side], side)
            arrived(relay_in.at[at], relay_recv.at[at])
            total = tot[g, owners, rows].astype(f32) + relay_in[at].astype(f32)
            relay_out[at] = total.astype(bf16)
            push_d(relay_out.at[at], summed.at[at], x_peer[side], summed_recv.at[at])

    def x_sum(g):
        for side in range(2):
            at, other = 2 * g + side, 2 * g + 1 - side
            owners, rows = box(x, side)
            arrived(direct.at[other], direct_recv.at[other])
            arrived(summed.at[at], summed_recv.at[at])
            got = summed[at].astype(f32) + direct[other].astype(f32)
            total = tot[g, owners, rows].astype(f32) + got
            after_x[g, side * 4 : (side + 1) * 4] = total.astype(bf16)
        for s in range(1, NZ):
            at = g * (NZ - 1) + s - 1
            push_d(after_x.at[g, (z + s) % NZ], z_in.at[at], z_peer[s - 1], z_recv.at[at])

    def z_sum(g):
        total = after_x[g, z].astype(f32)
        for s in range(1, NZ):
            at = g * (NZ - 1) + s - 1
            arrived(z_in.at[at], z_recv.at[at])
            total = total + z_in[at].astype(f32)
        after_z[g] = total.astype(bf16)
        y_in[g, y] = after_z[g]
        for n, peer in enumerate((partner, cross, across)):
            push_d(after_z.at[g], y_in.at[g, y], peer, y_recv.at[3 * g + n])

    def share(g):
        return [
            remote(
                final.at[g],
                shared.at[g, x // 2, c],
                peer,
                share_send.at[g * 7 + n],
                share_recv.at[g * 4 + (x // 2) * 2 + c],
            )
            for n, peer in enumerate(row_peer)
        ]

    def y_sum(g):
        arrived(y_in.at[g, 2 * hi + 1 - lo], y_recv.at[3 * g])
        arrived(y_in.at[g, 2 * oth + 1 - lo], y_recv.at[3 * g + 1])
        arrived(y_in.at[g, 2 * oth + lo], y_recv.at[3 * g + 2])
        total = y_in[g, 0].astype(f32)
        for at in range(1, 4):
            total = total + y_in[g, at].astype(f32)
        final[g] = total.astype(bf16)

        @pl.when(x % 2 == hi)
        def _():
            shared[g, x // 2, c] = final[g]
            for copy in share(g):
                copy.start()

    def collect(g):
        for half in range(2):
            for core in range(2):
                mine = (x % 2 == hi) & (x // 2 == half) & (c == core)

                @pl.when(jnp.logical_not(mine))
                def _():
                    at = g * 4 + half * 2 + core
                    arrived(shared.at[g, half, core], share_recv.at[at])

                gw[half * HALF : (half + 1) * HALF, (core * KVH + g) * HD : (core * KVH + g + 1) * HD] = (
                    shared[g, half, core].astype(f32)
                )

    def pick(own, other):
        taken = dot(from_pack[...], other, (1, 0))
        return jnp.where(kept[...] > 0.5, own.astype(f32), taken).astype(bf16)

    def input_grad():
        for g in range(KVH):
            arrived(kvr.at[g], kv_recv.at[g])
        for g in range(KVH):
            for t in range(2):
                at = (t * KVH + g) * HD
                chosen[:, at : at + HD] = pick(kvg[g, t], kvr[g, t])
        for n in range(4):
            cols = slice(n * CHUNK, (n + 1) * CHUNK)
            gi[:, cols] = dot(chosen[...], weight_rows(n), (1, 1)).astype(bf16)

    def place_queries(first, last):
        @pl.loop(first, last)
        def _(h):
            arrived(qr.at[h], q_recv.at[h])
            gq[:, columns(h)] = pick(qg[h], qr[h])

    clear()
    for h in range(GROUP):
        heads(0, h, h + 1)
        if h in (1, 3, 5):
            gather_step(1, 3 + h // 2)
    finish_group(0)
    clear()
    for i in range(4):
        product(0, i)
    gather_step(1, 6)
    for i in range(4):
        core_sum(0, i)
    gather_end(1)
    project(1)
    heads(1, 7, 13)
    relay(0)
    heads(1, 13, 14)
    finish_group(1)
    product(1, 0)
    product(1, 1)
    core_sum(1, 0)
    product(1, 2)
    core_sum(1, 1)
    product(1, 3)
    core_sum(1, 2)
    core_sum(1, 3)
    x_sum(0)
    late_queries(9, 12)
    relay(1)
    z_sum(0)
    late_queries(12, 14)
    x_sum(1)
    y_sum(0)
    input_grad()
    z_sum(1)
    place_queries(0, 7)
    y_sum(1)
    collect(0)
    place_queries(7, 14)
    collect(1)
    for copy in gather_started + d_started:
        copy.wait_send()
    for h in range(QH):
        hand_over(h).wait_send()
    for g in range(KVH):
        hand_over_kv(g).wait_send()

        @pl.when(x % 2 == hi)
        def _():
            for copy in share(g):
                copy.wait_send()


def shards(inputs, queries, out_grad, kv_weight, passage_blocks, handover):
    freq = ROPE_BASE ** (-(np.arange(HD // 2, dtype=np.float32) * 2.0) / HD)
    freq = jnp.asarray(np.concatenate([freq, freq])[None, :].astype(np.float32))
    dma = pltpu.SemaphoreType.DMA
    anywhere = pl.BlockSpec(memory_space=pl.ANY)
    scalars = pl.BlockSpec(memory_space=pltpu.SMEM)

    def vmem(*shape, kind=bf16):
        return pltpu.VMEM(shape, kind)

    packed = SENT * BLK
    shapes = (
        jax.ShapeDtypeStruct((ROWS, D), bf16),
        jax.ShapeDtypeStruct((ROWS, QH * HD), bf16),
        jax.ShapeDtypeStruct((SHARD, KV), f32),
    )
    return pl.pallas_call(
        kernel,
        name="grouped_attention_backward",
        out_shape=tuple(pltpu.VMEM(shape.shape, shape.dtype) for shape in shapes),
        in_specs=[scalars, scalars, VMEM, VMEM, anywhere, anywhere, anywhere],
        out_specs=(VMEM, VMEM, VMEM),
        scratch_shapes=[
            vmem(ROWS, D),
            vmem(ROWS, QH * HD),
            vmem(ROWS, QH * HD),
            vmem(D, ROWS),
            vmem(2 * KVH, 2, NZ, SHARD, HD),
            vmem(KVH, ROWS, HD),
            vmem(KVH, HD, ROWS),
            vmem(KVH, ROWS, HD),
            vmem(ROWS, HD, kind=f32),
            vmem(ROWS, HD, kind=f32),
            vmem(ROWS, ROWS, kind=f32),
            vmem(ROWS, HD, kind=f32),
            vmem(ROWS, HD, kind=f32),
            vmem(packed, ROWS),
            vmem(ROWS, packed),
            vmem(ROWS, HD, kind=f32),
            vmem(QH - LATE, ROWS, ROWS),
            vmem(QH, ROWS, HD),
            vmem(QH, packed, HD),
            vmem(QH, packed, HD),
            vmem(KVH, 2, ROWS, HD),
            vmem(KVH, 2, packed, HD),
            vmem(KVH, 2, packed, HD),
            vmem(ROWS, KV),
            vmem(KVH, 2, NF, SHARD, HD),
            vmem(KVH, NF, SHARD, HD),
            vmem(KVH, NF, SHARD, HD),
            vmem(2 * KVH, 4, HALF, HD),
            vmem(2 * KVH, 4, HALF, HD),
            vmem(2 * KVH, 4, HALF, HD),
            vmem(2 * KVH, 4, HALF, HD),
            vmem(KVH, NZ, HALF, HD),
            vmem(KVH * (NZ - 1), HALF, HD),
            vmem(KVH, HALF, HD),
            vmem(KVH, 4, HALF, HD),
            vmem(KVH, HALF, HD),
            vmem(KVH, 2, 2, HALF, HD),
            dma((3,)),
            dma((128,)),
            dma((16,)),
            dma((16,)),
            dma((32,)),
            dma((32,)),
            dma((32,)),
            dma((QH,)),
            dma((QH,)),
            dma((KVH,)),
            dma((KVH,)),
            dma((48,)),
            dma((8,)),
            dma((4,)),
            dma((4,)),
            dma((4,)),
            dma((KVH * (NZ - 1),)),
            dma((6,)),
            dma((14,)),
            dma((8,)),
        ],
        compiler_params=pltpu.CompilerParams(
            collective_id=0, has_side_effects=True, vmem_limit_bytes=LIMIT
        ),
    )(passage_blocks, handover, kv_weight, freq, inputs, queries, out_grad)


def solution(mesh):
    rows = P(("dp", "fsdp"), None)
    return jax.shard_map(
        shards,
        mesh=mesh,
        in_specs=(rows, rows, rows, P("fsdp", None), rows, rows),
        out_specs=(rows, rows, P("fsdp", None)),
        check_vma=False,
    )
```

```python
import jax
import jax.numpy as jnp
import numpy as np
from jax import lax
from jax.experimental import pallas as pl
from jax.experimental.pallas import tpu as pltpu
from jax.sharding import PartitionSpec as P

KVH = 2
GROUP = 7
HD = 128
QH = 14
NB = 6
BLK = 64
SENT = NB - 1
ROWS = NB * BLK
D = 3584
NX, NZ, NF = 4, 8, 16
SHARD = D // NF
HALF = SHARD // 2
CHUNK = 4 * SHARD
KV = 2 * KVH * HD
ROPE_BASE = 1000000.0
LOG2E = 1.4426950408889634
MESH = pl.DeviceIdType.MESH
VMEM = pl.BlockSpec(memory_space=pltpu.VMEM)
LIMIT = 56 * 1024 * 1024
f32, bf16 = jnp.float32, jnp.bfloat16


def place():
    d, f = lax.axis_index("dp"), lax.axis_index("fsdp")
    return d // 8, (d // 2) % NX, d % 2, f // NZ, f % NZ


def device(lo, x, c, hi, z):
    return (lo * 8 + x * 2 + c, hi * NZ + z)


def greet(peers):
    barrier = pltpu.get_barrier_semaphore()
    for peer in peers:
        pl.semaphore_signal(barrier, inc=1, device_id=peer, device_id_type=MESH)
    pl.semaphore_wait(barrier, len(peers))


def columns(index, width=HD):
    return pl.ds(pl.multiple_of(index * width, width), width)


def dot(a, b, dims):
    return lax.dot_general(a, b, ((dims[:1], dims[1:]), ((), ())), preferred_element_type=f32)


def handed_blocks(flags):
    rank, ranks = jnp.int32(0), []
    for b in range(NB):
        ranks.append(rank)
        rank = rank + flags[b]
    picks = []
    for r in range(SENT):
        pick = jnp.int32(0)
        for b in range(NB):
            pick = jnp.where((flags[b] == 1) & (ranks[b] == r), b, pick)
        picks.append(pick)
    return ranks, picks


HOPS = {1: 4, -1: 3}
LATE = 6
ARRIVES = {1: 1, 2: 2, 3: 3, 4: 4}
WAYS = [(1, 1), (-1, 1), (1, 2), (-1, 2), (1, 3), (-1, 3), (1, 4)]


def kernel(
    ids_ref, flags_ref, w_ref, freq_ref, x_hbm, q_hbm, g_hbm,
    gi, gq, gw,
    x_ref, q_ref, g_ref, x_t, weight,
    keys, keys_t, vals, kacc, vacc, bias, cosine, sine, to_pack, from_pack, kept,
    held, qg, qp, qr, kvg, kvp, kvr, chosen,
    part, sib, tot, relay_in, relay_out, direct, summed, after_x, z_in, after_z, y_in, final, shared,
    load, g_send, ring_recv, gy_recv, gx_recv, near_recv, far_recv,
    q_send, q_recv, kv_send, kv_recv,
    d_send, sib_recv, relay_recv, direct_recv, summed_recv, z_recv, y_recv, share_send, share_recv,
):
    lo, x, c, hi, z = place()
    y = 2 * hi + lo
    oth = 1 - hi
    sibling = device(lo, x, 1 - c, hi, z)
    partner = device(1 - lo, x, c, hi, z)
    cross = device(1 - lo, x, c, oth, z)
    across = device(lo, x, c, oth, z)
    x_side = ((x + 1) % NX, (x + NX - 1) % NX)
    x_peer = [device(lo, xs, c, hi, z) for xs in x_side]
    z_peer = [device(lo, x, c, hi, (z + s) % NZ) for s in range(1, NZ)]
    row_peer = [
        device(lo, (x + dx) % NX, (c + dc) % 2, hi, z)
        for dx in range(NX)
        for dc in range(2)
        if dx or dc
    ]
    loads = [
        pltpu.make_async_copy(src, dst, load.at[at])
        for at, (src, dst) in enumerate(((x_hbm, x_ref), (q_hbm, q_ref), (g_hbm, g_ref)))
    ]
    for copy in loads:
        copy.start()
    for q in range(2 * KVH):
        weight[q, hi, z] = w_ref[:, q * HD : (q + 1) * HD]
    greet(row_peer + z_peer + [partner, cross, across])

    def remote(src, dst, peer, sent, recv):
        return pltpu.make_async_remote_copy(
            src_ref=src,
            dst_ref=dst,
            send_sem=sent,
            recv_sem=recv,
            device_id=peer,
            device_id_type=MESH,
        )

    def pusher(sems):
        started = []

        def push(src, dst, peer, recv):
            copy = remote(src, dst, peer, sems.at[len(started)], recv)
            copy.start()
            started.append(copy)

        return push, started

    def arrived(dst, recv):
        remote(dst, dst, sibling, g_send.at[0], recv).wait_recv()

    ids = [ids_ref[0, b] for b in range(NB)]
    flags = [flags_ref[0, b] for b in range(NB)]
    ranks, picks = handed_blocks(flags)

    def set_masks():
        tall = lax.broadcasted_iota(jnp.int32, (ROWS, ROWS), 0)
        wide = lax.broadcasted_iota(jnp.int32, (ROWS, ROWS), 1)
        label_k = jnp.zeros((ROWS, ROWS), jnp.int32)
        label_q = jnp.zeros((ROWS, ROWS), jnp.int32)
        for b in range(NB):
            label_k = jnp.where(tall >= b * BLK, ids[b], label_k)
            label_q = jnp.where(wide >= b * BLK, ids[b], label_q)
        bias[...] = jnp.where(label_k == label_q, 0.0, -jnp.inf)

    def set_moves():
        tall = lax.broadcasted_iota(jnp.int32, (SENT * BLK, ROWS), 0)
        wide = lax.broadcasted_iota(jnp.int32, (SENT * BLK, ROWS), 1)
        shift = jnp.zeros((SENT * BLK, ROWS), jnp.int32)
        for r in range(SENT):
            shift = jnp.where(tall >= r * BLK, (picks[r] - r) * BLK, shift)
        to_pack[...] = jnp.where(tall + shift == wide, 1.0, 0.0).astype(bf16)
        tall = lax.broadcasted_iota(jnp.int32, (ROWS, SENT * BLK), 0)
        wide = lax.broadcasted_iota(jnp.int32, (ROWS, SENT * BLK), 1)
        shift = jnp.zeros((ROWS, SENT * BLK), jnp.int32)
        for b in range(NB):
            shift = jnp.where(tall >= b * BLK, (ranks[b] - b) * BLK, shift)
        from_pack[...] = jnp.where(tall + shift == wide, 1.0, 0.0).astype(bf16)
        row = lax.broadcasted_iota(jnp.int32, (ROWS, HD), 0)
        given = jnp.zeros((ROWS, HD), jnp.int32)
        for b in range(NB):
            given = jnp.where(row >= b * BLK, flags[b], given)
        kept[...] = (1 - given).astype(f32)

    def set_angles():
        first = [jnp.int32(0)]
        for b in range(1, NB):
            first.append(jnp.where(ids[b] == ids[b - 1], first[b - 1], b * BLK))
        row = lax.broadcasted_iota(jnp.int32, (ROWS, HD), 0)
        start = jnp.zeros((ROWS, HD), jnp.int32)
        for b in range(NB):
            start = jnp.where(row >= b * BLK, first[b], start)
        angle = (row - start).astype(f32) * freq_ref[...]
        cosine[...] = jnp.cos(angle)
        lane = lax.broadcasted_iota(jnp.int32, (ROWS, HD), 1)
        turn = jnp.sin(angle)
        sine[...] = jnp.where(lane < HD // 2, -turn, turn)

    def turn_inputs(first, count):
        @pl.loop(first, first + count)
        def _(n):
            x_t[pl.ds(pl.multiple_of(n * HD, HD), HD), :] = x_ref[:, columns(n)].T

    def piece_0():
        set_masks()
        set_moves()

    def piece_1():
        loads[0].wait()
        turn_inputs(0, 6)

    def piece_2():
        turn_inputs(6, 6)

    def piece_3():
        set_angles()

    def piece_4():
        turn_inputs(12, 16)

    pieces = {1: piece_1, 2: piece_2, 3: piece_3, 4: piece_4}

    push, gather_started = pusher(g_send)

    def source(way, hop):
        return (z + NZ - way * hop) % NZ

    def slot(way, hop):
        return 7 if hop == 0 else WAYS.index((way, hop))

    def piece(p, kind, row, zs, core):
        rows = pl.ds(pl.multiple_of(core * HALF, HALF), HALF)
        return weight.at[KVH * kind + p, row, zs, rows]

    near, far = x % 2, 1 - x % 2

    def gather_start(p):
        own = piece(p, near, hi, z, c)
        for way, hop in WAYS:
            peer = z_peer[(hop if way == 1 else NZ - hop) - 1]
            push(own, own, peer, ring_recv.at[p * 8 + slot(way, hop)])
            if (way, hop) == (-1, 1):
                push(own, own, cross, gy_recv.at[p * 8 + slot(1, 0)])

    def from_ring(p, way, hop):
        part = piece(p, near, hi, source(way, hop), c)
        at = slot(way, hop)
        arrived(part, ring_recv.at[p * 8 + at])
        push(part, part, cross, gy_recv.at[p * 8 + at])
        push(part, part, x_peer[0 if way == 1 else 1], gx_recv.at[p * 16 + at])
        push(part, part, sibling, near_recv.at[p * 16 + at])

    def from_y(p, way, hop):
        part = piece(p, near, oth, source(way, hop), c)
        at = slot(way, hop)
        arrived(part, gy_recv.at[p * 8 + at])
        push(part, part, x_peer[1 if way == 1 and hop else 0], gx_recv.at[p * 16 + 8 + at])
        push(part, part, sibling, near_recv.at[p * 16 + 8 + at])

    def from_x(p, row, half, way, hop):
        part = piece(p, far, row, source(way, hop), c)
        at = p * 16 + half * 8 + slot(way, hop)
        arrived(part, gx_recv.at[at])
        push(part, part, sibling, far_recv.at[at])

    def gather_step(p, time):
        for way in (1, -1):
            if time in ARRIVES and ARRIVES[time] <= HOPS[way]:
                from_ring(p, way, ARRIVES[time])
        if time == 2:
            from_y(p, 1, 0)
        for way in (1, -1):
            if time - 1 in ARRIVES and ARRIVES[time - 1] <= HOPS[way]:
                from_y(p, way, ARRIVES[time - 1])
        if time == 3:
            from_x(p, oth, 1, 1, 0)
        for way in (1, -1):
            if time - 1 in ARRIVES and ARRIVES[time - 1] <= HOPS[way]:
                from_x(p, hi, 0, way, ARRIVES[time - 1])
            if time - 2 in ARRIVES and ARRIVES[time - 2] <= HOPS[way]:
                from_x(p, oth, 1, way, ARRIVES[time - 2])

    def gather_end(p):
        for half, row in ((0, hi), (1, oth)):
            for way, hop in WAYS + [(1, 0)] * half:
                at = p * 16 + half * 8 + slot(way, hop)
                arrived(piece(p, near, row, source(way, hop), 1 - c), near_recv.at[at])
                arrived(piece(p, far, row, source(way, hop), 1 - c), far_recv.at[at])

    def weight_rows(n, blocks=range(2 * KVH)):
        at = pl.ds((n % 2) * 4, 4)
        return jnp.concatenate([weight[q, n // 2, at].reshape(CHUNK, HD) for q in blocks], axis=1)

    def project(g):
        projected = jnp.zeros((ROWS, 2 * HD), f32)
        for n in range(4):
            rows = weight_rows(n, (g, KVH + g))
            projected += dot(x_ref[:, n * CHUNK : (n + 1) * CHUNK], rows, (1, 0))
        raw = projected[:, :HD]
        key = raw * cosine[...] + pltpu.roll(raw, HD // 2, 1) * sine[...]
        keys[g] = key.astype(bf16)
        keys_t[g] = key.T.astype(bf16)
        vals[g] = projected[:, HD:].astype(bf16)

    gather_start(0)
    piece_0()
    for time in range(1, 7):
        gather_step(0, time)
        if time == 2:
            gather_start(1)
        if time in pieces:
            pieces[time]()
    gather_step(1, 1)
    gather_end(0)
    project(0)
    gather_step(1, 2)
    loads[1].wait()
    loads[2].wait()

    scale = 1.0 / HD**0.5

    def hand_over(h):
        return remote(qp.at[h], qr.at[h], partner, q_send.at[h], q_recv.at[h])

    def query_part(h, dscores_b):
        own = (dot(keys_t[h // GROUP], dscores_b, (1, 0)) * scale).T.astype(bf16)
        qg[h] = own
        qp[h] = dot(to_pack[...], own, (1, 0)).astype(bf16)
        hand_over(h).start()

    def late_queries(first, last):
        for h in range(first, last):
            query_part(h, held[h - LATE])

    def heads(g, first, last):
        for h in range(first, last):
            query, grad = q_ref[:, h * HD : (h + 1) * HD], g_ref[:, h * HD : (h + 1) * HD]
            scores = dot(keys[g], query, (1, 1)) * (scale * LOG2E) + bias[...]
            weights = jnp.exp2(scores - jnp.max(scores, axis=0, keepdims=True))
            probs = weights * (1.0 / jnp.sum(weights, axis=0, keepdims=True))
            probs_b = probs.astype(bf16)
            dprobs = dot(vals[g], grad, (1, 1))
            delta = jnp.sum(probs_b.astype(f32) * dprobs, axis=0, keepdims=True)
            dscores_b = (probs * (dprobs - delta)).astype(bf16)
            vacc[...] += dot(probs_b, grad, (1, 0))
            kacc[...] += dot(dscores_b, query, (1, 0))
            if h < LATE:
                query_part(h, dscores_b)
            else:
                held[h - LATE] = dscores_b

    def clear():
        kacc[...] = jnp.zeros_like(kacc)
        vacc[...] = jnp.zeros_like(vacc)

    def hand_over_kv(g):
        return remote(kvp.at[g], kvr.at[g], partner, kv_send.at[g], kv_recv.at[g])

    def finish_group(g):
        grad_k = kacc[...] * scale
        raw = grad_k * cosine[...] - pltpu.roll(grad_k, HD // 2, 1) * sine[...]
        kvg[g, 0] = raw.astype(bf16)
        kvg[g, 1] = vacc[...].astype(bf16)
        for t in range(2):
            kvp[g, t] = dot(to_pack[...], kvg[g, t], (1, 0)).astype(bf16)
        hand_over_kv(g).start()

    push_d, d_started = pusher(d_send)

    def chunk(i):
        return 2 * (x % 2 if i < 2 else 1 - x % 2) + i % 2

    def product(g, i):
        n = chunk(i)
        pair = jnp.concatenate([kvg[g, 0], kvg[g, 1]], axis=1)
        rows = pl.ds(pl.multiple_of(n * CHUNK, CHUNK), CHUNK)
        result = dot(x_t[rows, :], pair, (1, 0)).astype(bf16)
        four = pl.ds(n * 4, 4)
        for t in range(2):
            part[g, t, four] = result[:, t * HD : (t + 1) * HD].reshape(4, SHARD, HD)
        push_d(part.at[g, 1 - c, four], sib.at[g, four], sibling, sib_recv.at[g * 4 + i])

    def box(xs, side):
        owners = pl.ds((xs % 2) * NZ + 4 * side, 4)
        return owners, pl.ds(pl.multiple_of((xs // 2) * HALF, HALF), HALF)

    def core_sum(g, i):
        four = pl.ds(chunk(i) * 4, 4)
        arrived(sib.at[g, four], sib_recv.at[g * 4 + i])
        total = part[g, c, four].astype(f32) + sib[g, four].astype(f32)
        tot[g, four] = total.astype(bf16)
        if i < 2:
            side, at = i, 2 * g + i
            owners, rows = box((x + 2) % NX, side)
            push_d(tot.at[g, owners, rows], relay_in.at[at], x_peer[side], relay_recv.at[at])
        else:
            side, at = 3 - i, 2 * g + 3 - i
            owners, rows = box(x_side[side], 1 - side)
            push_d(tot.at[g, owners, rows], direct.at[at], x_peer[side], direct_recv.at[at])

    def relay(g):
        for side in range(2):
            at = 2 * g + side
            owners, rows = box(x_side[side], side)
            arrived(relay_in.at[at], relay_recv.at[at])
            total = tot[g, owners, rows].astype(f32) + relay_in[at].astype(f32)
            relay_out[at] = total.astype(bf16)
            push_d(relay_out.at[at], summed.at[at], x_peer[side], summed_recv.at[at])

    def x_sum(g):
        for side in range(2):
            at, other = 2 * g + side, 2 * g + 1 - side
            owners, rows = box(x, side)
            arrived(direct.at[other], direct_recv.at[other])
            arrived(summed.at[at], summed_recv.at[at])
            got = summed[at].astype(f32) + direct[other].astype(f32)
            total = tot[g, owners, rows].astype(f32) + got
            after_x[g, side * 4 : (side + 1) * 4] = total.astype(bf16)
        for s in range(1, NZ):
            at = g * (NZ - 1) + s - 1
            push_d(after_x.at[g, (z + s) % NZ], z_in.at[at], z_peer[s - 1], z_recv.at[at])

    def z_sum(g):
        total = after_x[g, z].astype(f32)
        for s in range(1, NZ):
            at = g * (NZ - 1) + s - 1
            arrived(z_in.at[at], z_recv.at[at])
            total = total + z_in[at].astype(f32)
        after_z[g] = total.astype(bf16)
        y_in[g, y] = after_z[g]
        for n, peer in enumerate((partner, cross, across)):
            push_d(after_z.at[g], y_in.at[g, y], peer, y_recv.at[3 * g + n])

    def share(g):
        return [
            remote(
                final.at[g],
                shared.at[g, x // 2, c],
                peer,
                share_send.at[g * 7 + n],
                share_recv.at[g * 4 + (x // 2) * 2 + c],
            )
            for n, peer in enumerate(row_peer)
        ]

    def y_sum(g):
        arrived(y_in.at[g, 2 * hi + 1 - lo], y_recv.at[3 * g])
        arrived(y_in.at[g, 2 * oth + 1 - lo], y_recv.at[3 * g + 1])
        arrived(y_in.at[g, 2 * oth + lo], y_recv.at[3 * g + 2])
        total = y_in[g, 0].astype(f32)
        for at in range(1, 4):
            total = total + y_in[g, at].astype(f32)
        final[g] = total.astype(bf16)

        @pl.when(x % 2 == hi)
        def _():
            shared[g, x // 2, c] = final[g]
            for copy in share(g):
                copy.start()

    def collect(g):
        for half in range(2):
            for core in range(2):
                mine = (x % 2 == hi) & (x // 2 == half) & (c == core)

                @pl.when(jnp.logical_not(mine))
                def _():
                    at = g * 4 + half * 2 + core
                    arrived(shared.at[g, half, core], share_recv.at[at])

                gw[half * HALF : (half + 1) * HALF, (core * KVH + g) * HD : (core * KVH + g + 1) * HD] = (
                    shared[g, half, core].astype(f32)
                )

    def pick(own, other):
        taken = dot(from_pack[...], other, (1, 0))
        return jnp.where(kept[...] > 0.5, own.astype(f32), taken).astype(bf16)

    def input_grad():
        for g in range(KVH):
            arrived(kvr.at[g], kv_recv.at[g])
        for g in range(KVH):
            for t in range(2):
                at = (t * KVH + g) * HD
                chosen[:, at : at + HD] = pick(kvg[g, t], kvr[g, t])
        for n in range(4):
            cols = slice(n * CHUNK, (n + 1) * CHUNK)
            gi[:, cols] = dot(chosen[...], weight_rows(n), (1, 1)).astype(bf16)

    def place_queries(first, last):
        @pl.loop(first, last)
        def _(h):
            arrived(qr.at[h], q_recv.at[h])
            gq[:, columns(h)] = pick(qg[h], qr[h])

    clear()
    for h in range(GROUP):
        heads(0, h, h + 1)
        if h in (1, 3, 5):
            gather_step(1, 3 + h // 2)
    finish_group(0)
    clear()
    for i in range(4):
        product(0, i)
    gather_step(1, 6)
    for i in range(4):
        core_sum(0, i)
    gather_end(1)
    project(1)
    heads(1, 7, 13)
    relay(0)
    heads(1, 13, 14)
    finish_group(1)
    product(1, 0)
    product(1, 1)
    core_sum(1, 0)
    product(1, 2)
    core_sum(1, 1)
    product(1, 3)
    core_sum(1, 2)
    core_sum(1, 3)
    x_sum(0)
    late_queries(6, 11)
    relay(1)
    z_sum(0)
    late_queries(11, 14)
    x_sum(1)
    y_sum(0)
    input_grad()
    z_sum(1)
    place_queries(0, 7)
    y_sum(1)
    collect(0)
    place_queries(7, 14)
    collect(1)
    for copy in gather_started + d_started:
        copy.wait_send()
    for h in range(QH):
        hand_over(h).wait_send()
    for g in range(KVH):
        hand_over_kv(g).wait_send()

        @pl.when(x % 2 == hi)
        def _():
            for copy in share(g):
                copy.wait_send()


def shards(inputs, queries, out_grad, kv_weight, passage_blocks, handover):
    freq = ROPE_BASE ** (-(np.arange(HD // 2, dtype=np.float32) * 2.0) / HD)
    freq = jnp.asarray(np.concatenate([freq, freq])[None, :].astype(np.float32))
    dma = pltpu.SemaphoreType.DMA
    anywhere = pl.BlockSpec(memory_space=pl.ANY)
    scalars = pl.BlockSpec(memory_space=pltpu.SMEM)

    def vmem(*shape, kind=bf16):
        return pltpu.VMEM(shape, kind)

    packed = SENT * BLK
    shapes = (
        jax.ShapeDtypeStruct((ROWS, D), bf16),
        jax.ShapeDtypeStruct((ROWS, QH * HD), bf16),
        jax.ShapeDtypeStruct((SHARD, KV), f32),
    )
    return pl.pallas_call(
        kernel,
        name="grouped_attention_backward",
        out_shape=tuple(pltpu.VMEM(shape.shape, shape.dtype) for shape in shapes),
        in_specs=[scalars, scalars, VMEM, VMEM, anywhere, anywhere, anywhere],
        out_specs=(VMEM, VMEM, VMEM),
        scratch_shapes=[
            vmem(ROWS, D),
            vmem(ROWS, QH * HD),
            vmem(ROWS, QH * HD),
            vmem(D, ROWS),
            vmem(2 * KVH, 2, NZ, SHARD, HD),
            vmem(KVH, ROWS, HD),
            vmem(KVH, HD, ROWS),
            vmem(KVH, ROWS, HD),
            vmem(ROWS, HD, kind=f32),
            vmem(ROWS, HD, kind=f32),
            vmem(ROWS, ROWS, kind=f32),
            vmem(ROWS, HD, kind=f32),
            vmem(ROWS, HD, kind=f32),
            vmem(packed, ROWS),
            vmem(ROWS, packed),
            vmem(ROWS, HD, kind=f32),
            vmem(QH - LATE, ROWS, ROWS),
            vmem(QH, ROWS, HD),
            vmem(QH, packed, HD),
            vmem(QH, packed, HD),
            vmem(KVH, 2, ROWS, HD),
            vmem(KVH, 2, packed, HD),
            vmem(KVH, 2, packed, HD),
            vmem(ROWS, KV),
            vmem(KVH, 2, NF, SHARD, HD),
            vmem(KVH, NF, SHARD, HD),
            vmem(KVH, NF, SHARD, HD),
            vmem(2 * KVH, 4, HALF, HD),
            vmem(2 * KVH, 4, HALF, HD),
            vmem(2 * KVH, 4, HALF, HD),
            vmem(2 * KVH, 4, HALF, HD),
            vmem(KVH, NZ, HALF, HD),
            vmem(KVH * (NZ - 1), HALF, HD),
            vmem(KVH, HALF, HD),
            vmem(KVH, 4, HALF, HD),
            vmem(KVH, HALF, HD),
            vmem(KVH, 2, 2, HALF, HD),
            dma((3,)),
            dma((128,)),
            dma((16,)),
            dma((16,)),
            dma((32,)),
            dma((32,)),
            dma((32,)),
            dma((QH,)),
            dma((QH,)),
            dma((KVH,)),
            dma((KVH,)),
            dma((48,)),
            dma((8,)),
            dma((4,)),
            dma((4,)),
            dma((4,)),
            dma((KVH * (NZ - 1),)),
            dma((6,)),
            dma((14,)),
            dma((8,)),
        ],
        compiler_params=pltpu.CompilerParams(
            collective_id=0, has_side_effects=True, vmem_limit_bytes=LIMIT
        ),
    )(passage_blocks, handover, kv_weight, freq, inputs, queries, out_grad)


def solution(mesh):
    rows = P(("dp", "fsdp"), None)
    return jax.shard_map(
        shards,
        mesh=mesh,
        in_specs=(rows, rows, rows, P("fsdp", None), rows, rows),
        out_specs=(rows, rows, P("fsdp", None)),
        check_vma=False,
    )
```

```python
import jax
import jax.numpy as jnp
import numpy as np
from jax import lax
from jax.experimental import pallas as pl
from jax.experimental.pallas import tpu as pltpu
from jax.sharding import PartitionSpec as P

KVH = 2
GROUP = 7
HD = 128
QH = 14
NB = 6
BLK = 64
SENT = NB - 1
ROWS = NB * BLK
D = 3584
NX, NZ, NF = 4, 8, 16
SHARD = D // NF
HALF = SHARD // 2
CHUNK = 4 * SHARD
KV = 2 * KVH * HD
ROPE_BASE = 1000000.0
LOG2E = 1.4426950408889634
MESH = pl.DeviceIdType.MESH
VMEM = pl.BlockSpec(memory_space=pltpu.VMEM)
LIMIT = 56 * 1024 * 1024
f32, bf16 = jnp.float32, jnp.bfloat16


def place():
    d, f = lax.axis_index("dp"), lax.axis_index("fsdp")
    return d // 8, (d // 2) % NX, d % 2, f // NZ, f % NZ


def device(lo, x, c, hi, z):
    return (lo * 8 + x * 2 + c, hi * NZ + z)


def greet(peers):
    barrier = pltpu.get_barrier_semaphore()
    for peer in peers:
        pl.semaphore_signal(barrier, inc=1, device_id=peer, device_id_type=MESH)
    pl.semaphore_wait(barrier, len(peers))


def columns(index, width=HD):
    return pl.ds(pl.multiple_of(index * width, width), width)


def dot(a, b, dims):
    return lax.dot_general(a, b, ((dims[:1], dims[1:]), ((), ())), preferred_element_type=f32)


def handed_blocks(flags):
    rank, ranks = jnp.int32(0), []
    for b in range(NB):
        ranks.append(rank)
        rank = rank + flags[b]
    picks = []
    for r in range(SENT):
        pick = jnp.int32(0)
        for b in range(NB):
            pick = jnp.where((flags[b] == 1) & (ranks[b] == r), b, pick)
        picks.append(pick)
    return ranks, picks


HOPS = {1: 4, -1: 3}
LATE = 6
ARRIVES = {1: 1, 2: 2, 3: 3, 4: 4}
WAYS = [(1, 1), (-1, 1), (1, 2), (-1, 2), (1, 3), (-1, 3), (1, 4)]


def kernel(
    ids_ref, flags_ref, w_ref, freq_ref, x_hbm, q_hbm, g_hbm,
    gi, gq, gw,
    x_ref, q_ref, g_ref, x_t, weight,
    keys, keys_t, vals, kacc, vacc, bias, cosine, sine, to_pack, from_pack, kept,
    held, qg, qp, qr, kvg, kvp, kvr, chosen,
    part, sib, tot, relay_in, relay_out, direct, summed, after_x, z_in, after_z, y_in, final, shared,
    load, g_send, ring_recv, gy_recv, gx_recv, near_recv, far_recv,
    q_send, q_recv, kv_send, kv_recv,
    d_send, sib_recv, relay_recv, direct_recv, summed_recv, z_recv, y_recv, share_send, share_recv,
):
    lo, x, c, hi, z = place()
    y = 2 * hi + lo
    oth = 1 - hi
    sibling = device(lo, x, 1 - c, hi, z)
    partner = device(1 - lo, x, c, hi, z)
    cross = device(1 - lo, x, c, oth, z)
    across = device(lo, x, c, oth, z)
    x_side = ((x + 1) % NX, (x + NX - 1) % NX)
    x_peer = [device(lo, xs, c, hi, z) for xs in x_side]
    z_peer = [device(lo, x, c, hi, (z + s) % NZ) for s in range(1, NZ)]
    row_peer = [
        device(lo, (x + dx) % NX, (c + dc) % 2, hi, z)
        for dx in range(NX)
        for dc in range(2)
        if dx or dc
    ]
    loads = [
        pltpu.make_async_copy(src, dst, load.at[at])
        for at, (src, dst) in enumerate(((x_hbm, x_ref), (q_hbm, q_ref), (g_hbm, g_ref)))
    ]
    for copy in loads:
        copy.start()
    for q in range(2 * KVH):
        weight[q, hi, z] = w_ref[:, q * HD : (q + 1) * HD]
    greet(row_peer + z_peer + [partner, cross, across])

    def remote(src, dst, peer, sent, recv):
        return pltpu.make_async_remote_copy(
            src_ref=src,
            dst_ref=dst,
            send_sem=sent,
            recv_sem=recv,
            device_id=peer,
            device_id_type=MESH,
        )

    def pusher(sems):
        started = []

        def push(src, dst, peer, recv):
            copy = remote(src, dst, peer, sems.at[len(started)], recv)
            copy.start()
            started.append(copy)

        return push, started

    def arrived(dst, recv):
        remote(dst, dst, sibling, g_send.at[0], recv).wait_recv()

    ids = [ids_ref[0, b] for b in range(NB)]
    flags = [flags_ref[0, b] for b in range(NB)]
    ranks, picks = handed_blocks(flags)

    def set_masks():
        tall = lax.broadcasted_iota(jnp.int32, (ROWS, ROWS), 0)
        wide = lax.broadcasted_iota(jnp.int32, (ROWS, ROWS), 1)
        label_k = jnp.zeros((ROWS, ROWS), jnp.int32)
        label_q = jnp.zeros((ROWS, ROWS), jnp.int32)
        for b in range(NB):
            label_k = jnp.where(tall >= b * BLK, ids[b], label_k)
            label_q = jnp.where(wide >= b * BLK, ids[b], label_q)
        bias[...] = jnp.where(label_k == label_q, 0.0, -jnp.inf)

    def set_moves():
        tall = lax.broadcasted_iota(jnp.int32, (SENT * BLK, ROWS), 0)
        wide = lax.broadcasted_iota(jnp.int32, (SENT * BLK, ROWS), 1)
        shift = jnp.zeros((SENT * BLK, ROWS), jnp.int32)
        for r in range(SENT):
            shift = jnp.where(tall >= r * BLK, (picks[r] - r) * BLK, shift)
        to_pack[...] = jnp.where(tall + shift == wide, 1.0, 0.0).astype(bf16)
        tall = lax.broadcasted_iota(jnp.int32, (ROWS, SENT * BLK), 0)
        wide = lax.broadcasted_iota(jnp.int32, (ROWS, SENT * BLK), 1)
        shift = jnp.zeros((ROWS, SENT * BLK), jnp.int32)
        for b in range(NB):
            shift = jnp.where(tall >= b * BLK, (ranks[b] - b) * BLK, shift)
        from_pack[...] = jnp.where(tall + shift == wide, 1.0, 0.0).astype(bf16)
        row = lax.broadcasted_iota(jnp.int32, (ROWS, HD), 0)
        given = jnp.zeros((ROWS, HD), jnp.int32)
        for b in range(NB):
            given = jnp.where(row >= b * BLK, flags[b], given)
        kept[...] = (1 - given).astype(f32)

    def set_angles():
        first = [jnp.int32(0)]
        for b in range(1, NB):
            first.append(jnp.where(ids[b] == ids[b - 1], first[b - 1], b * BLK))
        row = lax.broadcasted_iota(jnp.int32, (ROWS, HD), 0)
        start = jnp.zeros((ROWS, HD), jnp.int32)
        for b in range(NB):
            start = jnp.where(row >= b * BLK, first[b], start)
        angle = (row - start).astype(f32) * freq_ref[...]
        cosine[...] = jnp.cos(angle)
        lane = lax.broadcasted_iota(jnp.int32, (ROWS, HD), 1)
        turn = jnp.sin(angle)
        sine[...] = jnp.where(lane < HD // 2, -turn, turn)

    def turn_inputs(first, count):
        @pl.loop(first, first + count)
        def _(n):
            x_t[pl.ds(pl.multiple_of(n * HD, HD), HD), :] = x_ref[:, columns(n)].T

    def piece_0():
        set_masks()
        set_moves()

    def piece_1():
        loads[0].wait()
        turn_inputs(0, 6)

    def piece_2():
        turn_inputs(6, 6)

    def piece_3():
        set_angles()

    def piece_4():
        turn_inputs(12, 16)

    pieces = {1: piece_1, 2: piece_2, 3: piece_3, 4: piece_4}

    push, gather_started = pusher(g_send)

    def source(way, hop):
        return (z + NZ - way * hop) % NZ

    def slot(way, hop):
        return 7 if hop == 0 else WAYS.index((way, hop))

    def piece(p, kind, row, zs, core):
        rows = pl.ds(pl.multiple_of(core * HALF, HALF), HALF)
        return weight.at[KVH * kind + p, row, zs, rows]

    near, far = x % 2, 1 - x % 2

    def gather_start(p):
        own = piece(p, near, hi, z, c)
        for way, hop in WAYS:
            peer = z_peer[(hop if way == 1 else NZ - hop) - 1]
            push(own, own, peer, ring_recv.at[p * 8 + slot(way, hop)])
            if (way, hop) == (-1, 1):
                push(own, own, cross, gy_recv.at[p * 8 + slot(1, 0)])

    def from_ring(p, way, hop):
        part = piece(p, near, hi, source(way, hop), c)
        at = slot(way, hop)
        arrived(part, ring_recv.at[p * 8 + at])
        push(part, part, cross, gy_recv.at[p * 8 + at])
        push(part, part, x_peer[0 if way == 1 else 1], gx_recv.at[p * 16 + at])
        push(part, part, sibling, near_recv.at[p * 16 + at])

    def from_y(p, way, hop):
        part = piece(p, near, oth, source(way, hop), c)
        at = slot(way, hop)
        arrived(part, gy_recv.at[p * 8 + at])
        push(part, part, x_peer[1 if way == 1 and hop else 0], gx_recv.at[p * 16 + 8 + at])
        push(part, part, sibling, near_recv.at[p * 16 + 8 + at])

    def from_x(p, row, half, way, hop):
        part = piece(p, far, row, source(way, hop), c)
        at = p * 16 + half * 8 + slot(way, hop)
        arrived(part, gx_recv.at[at])
        push(part, part, sibling, far_recv.at[at])

    def gather_step(p, time):
        for way in (1, -1):
            if time in ARRIVES and ARRIVES[time] <= HOPS[way]:
                from_ring(p, way, ARRIVES[time])
        if time == 2:
            from_y(p, 1, 0)
        for way in (1, -1):
            if time - 1 in ARRIVES and ARRIVES[time - 1] <= HOPS[way]:
                from_y(p, way, ARRIVES[time - 1])
        if time == 3:
            from_x(p, oth, 1, 1, 0)
        for way in (1, -1):
            if time - 1 in ARRIVES and ARRIVES[time - 1] <= HOPS[way]:
                from_x(p, hi, 0, way, ARRIVES[time - 1])
            if time - 2 in ARRIVES and ARRIVES[time - 2] <= HOPS[way]:
                from_x(p, oth, 1, way, ARRIVES[time - 2])

    def gather_end(p):
        for half, row in ((0, hi), (1, oth)):
            for way, hop in WAYS + [(1, 0)] * half:
                at = p * 16 + half * 8 + slot(way, hop)
                arrived(piece(p, near, row, source(way, hop), 1 - c), near_recv.at[at])
                arrived(piece(p, far, row, source(way, hop), 1 - c), far_recv.at[at])

    def weight_rows(n, blocks=range(2 * KVH)):
        at = pl.ds((n % 2) * 4, 4)
        return jnp.concatenate([weight[q, n // 2, at].reshape(CHUNK, HD) for q in blocks], axis=1)

    def project(g):
        projected = jnp.zeros((ROWS, 2 * HD), f32)
        for n in range(4):
            rows = weight_rows(n, (g, KVH + g))
            projected += dot(x_ref[:, n * CHUNK : (n + 1) * CHUNK], rows, (1, 0))
        raw = projected[:, :HD]
        key = raw * cosine[...] + pltpu.roll(raw, HD // 2, 1) * sine[...]
        keys[g] = key.astype(bf16)
        keys_t[g] = key.T.astype(bf16)
        vals[g] = projected[:, HD:].astype(bf16)

    gather_start(0)
    piece_0()
    for time in range(1, 7):
        gather_step(0, time)
        if time == 2:
            gather_start(1)
        if time in pieces:
            pieces[time]()
    gather_step(1, 1)
    gather_end(0)
    project(0)
    gather_step(1, 2)
    loads[1].wait()
    loads[2].wait()

    scale = 1.0 / HD**0.5

    def hand_over(h):
        return remote(qp.at[h], qr.at[h], partner, q_send.at[h], q_recv.at[h])

    def query_part(h, dscores_b):
        own = (dot(keys_t[h // GROUP], dscores_b, (1, 0)) * scale).astype(bf16).T
        qg[h] = own
        qp[h] = dot(to_pack[...], own, (1, 0)).astype(bf16)

    def late_queries(first, last):
        for h in range(first, last):
            query_part(h, held[h - LATE])
        for h in range(first, last):
            hand_over(h).start()

    def heads(g, first, last):
        for h in range(first, last):
            query, grad = q_ref[:, h * HD : (h + 1) * HD], g_ref[:, h * HD : (h + 1) * HD]
            scores = dot(keys[g], query, (1, 1)) * (scale * LOG2E) + bias[...]
            weights = jnp.exp2(scores - jnp.max(scores, axis=0, keepdims=True))
            probs = weights * (1.0 / jnp.sum(weights, axis=0, keepdims=True))
            probs_b = probs.astype(bf16)
            dprobs = dot(vals[g], grad, (1, 1))
            delta = jnp.sum(probs_b.astype(f32) * dprobs, axis=0, keepdims=True)
            dscores_b = (probs * (dprobs - delta)).astype(bf16)
            vacc[...] += dot(probs_b, grad, (1, 0))
            kacc[...] += dot(dscores_b, query, (1, 0))
            if h < LATE:
                query_part(h, dscores_b)
            else:
                held[h - LATE] = dscores_b
        for h in range(first, min(last, LATE)):
            hand_over(h).start()

    def clear():
        kacc[...] = jnp.zeros_like(kacc)
        vacc[...] = jnp.zeros_like(vacc)

    def hand_over_kv(g):
        return remote(kvp.at[g], kvr.at[g], partner, kv_send.at[g], kv_recv.at[g])

    def finish_group(g):
        grad_k = kacc[...] * scale
        raw = grad_k * cosine[...] - pltpu.roll(grad_k, HD // 2, 1) * sine[...]
        kvg[g, 0] = raw.astype(bf16)
        kvg[g, 1] = vacc[...].astype(bf16)

    def send_group(g):
        for t in range(2):
            kvp[g, t] = dot(to_pack[...], kvg[g, t], (1, 0)).astype(bf16)
        hand_over_kv(g).start()

    push_d, d_started = pusher(d_send)

    def chunk(i):
        return 2 * (x % 2 if i < 2 else 1 - x % 2) + i % 2

    def product(g, i):
        n = chunk(i)
        pair = jnp.concatenate([kvg[g, 0], kvg[g, 1]], axis=1)
        rows = pl.ds(pl.multiple_of(n * CHUNK, CHUNK), CHUNK)
        result = dot(x_t[rows, :], pair, (1, 0)).astype(bf16)
        four = pl.ds(n * 4, 4)
        for t in range(2):
            part[g, t, four] = result[:, t * HD : (t + 1) * HD].reshape(4, SHARD, HD)
        push_d(part.at[g, 1 - c, four], sib.at[g, four], sibling, sib_recv.at[g * 4 + i])

    def box(xs, side):
        owners = pl.ds((xs % 2) * NZ + 4 * side, 4)
        return owners, pl.ds(pl.multiple_of((xs // 2) * HALF, HALF), HALF)

    def core_sum(g, i):
        four = pl.ds(chunk(i) * 4, 4)
        arrived(sib.at[g, four], sib_recv.at[g * 4 + i])
        total = part[g, c, four].astype(f32) + sib[g, four].astype(f32)
        tot[g, four] = total.astype(bf16)
        if i < 2:
            side, at = i, 2 * g + i
            owners, rows = box((x + 2) % NX, side)
            push_d(tot.at[g, owners, rows], relay_in.at[at], x_peer[side], relay_recv.at[at])
        else:
            side, at = 3 - i, 2 * g + 3 - i
            owners, rows = box(x_side[side], 1 - side)
            push_d(tot.at[g, owners, rows], direct.at[at], x_peer[side], direct_recv.at[at])

    def relay(g):
        for side in range(2):
            at = 2 * g + side
            owners, rows = box(x_side[side], side)
            arrived(relay_in.at[at], relay_recv.at[at])
            total = tot[g, owners, rows].astype(f32) + relay_in[at].astype(f32)
            relay_out[at] = total.astype(bf16)
            push_d(relay_out.at[at], summed.at[at], x_peer[side], summed_recv.at[at])

    def x_sum(g):
        for side in range(2):
            at, other = 2 * g + side, 2 * g + 1 - side
            owners, rows = box(x, side)
            arrived(direct.at[other], direct_recv.at[other])
            arrived(summed.at[at], summed_recv.at[at])
            got = summed[at].astype(f32) + direct[other].astype(f32)
            total = tot[g, owners, rows].astype(f32) + got
            after_x[g, side * 4 : (side + 1) * 4] = total.astype(bf16)
        for s in range(1, NZ):
            at = g * (NZ - 1) + s - 1
            push_d(after_x.at[g, (z + s) % NZ], z_in.at[at], z_peer[s - 1], z_recv.at[at])

    def z_sum(g):
        total = after_x[g, z].astype(f32)
        for s in range(1, NZ):
            at = g * (NZ - 1) + s - 1
            arrived(z_in.at[at], z_recv.at[at])
            total = total + z_in[at].astype(f32)
        after_z[g] = total.astype(bf16)
        y_in[g, y] = after_z[g]
        for n, peer in enumerate((partner, cross, across)):
            push_d(after_z.at[g], y_in.at[g, y], peer, y_recv.at[3 * g + n])

    def share(g):
        return [
            remote(
                final.at[g],
                shared.at[g, x // 2, c],
                peer,
                share_send.at[g * 7 + n],
                share_recv.at[g * 4 + (x // 2) * 2 + c],
            )
            for n, peer in enumerate(row_peer)
        ]

    def y_sum(g):
        arrived(y_in.at[g, 2 * hi + 1 - lo], y_recv.at[3 * g])
        arrived(y_in.at[g, 2 * oth + 1 - lo], y_recv.at[3 * g + 1])
        arrived(y_in.at[g, 2 * oth + lo], y_recv.at[3 * g + 2])
        total = y_in[g, 0].astype(f32)
        for at in range(1, 4):
            total = total + y_in[g, at].astype(f32)
        final[g] = total.astype(bf16)

        @pl.when(x % 2 == hi)
        def _():
            shared[g, x // 2, c] = final[g]
            for copy in share(g):
                copy.start()

    def collect(g):
        for half in range(2):
            for core in range(2):
                mine = (x % 2 == hi) & (x // 2 == half) & (c == core)

                @pl.when(jnp.logical_not(mine))
                def _():
                    at = g * 4 + half * 2 + core
                    arrived(shared.at[g, half, core], share_recv.at[at])

                gw[half * HALF : (half + 1) * HALF, (core * KVH + g) * HD : (core * KVH + g + 1) * HD] = (
                    shared[g, half, core].astype(f32)
                )

    def pick(own, other):
        taken = dot(from_pack[...], other, (1, 0))
        return jnp.where(kept[...] > 0.5, own.astype(f32), taken).astype(bf16)

    def input_grad():
        for g in range(KVH):
            arrived(kvr.at[g], kv_recv.at[g])
        for g in range(KVH):
            for t in range(2):
                at = (t * KVH + g) * HD
                chosen[:, at : at + HD] = pick(kvg[g, t], kvr[g, t])
        for n in range(4):
            cols = slice(n * CHUNK, (n + 1) * CHUNK)
            gi[:, cols] = dot(chosen[...], weight_rows(n), (1, 1)).astype(bf16)

    def place_queries(first, last):
        @pl.loop(first, last)
        def _(h):
            arrived(qr.at[h], q_recv.at[h])
            gq[:, columns(h)] = pick(qg[h], qr[h])

    clear()
    for pair in range(3):
        heads(0, 2 * pair, 2 * pair + 2)
        gather_step(1, 3 + pair)
    heads(0, 6, 7)
    finish_group(0)
    clear()
    for i in range(4):
        product(0, i)
    gather_step(1, 6)
    send_group(0)
    for i in range(4):
        core_sum(0, i)
    gather_end(1)
    project(1)
    heads(1, 7, 13)
    relay(0)
    heads(1, 13, 14)
    finish_group(1)
    product(1, 0)
    product(1, 1)
    core_sum(1, 0)
    product(1, 2)
    core_sum(1, 1)
    product(1, 3)
    core_sum(1, 2)
    core_sum(1, 3)
    send_group(1)
    x_sum(0)
    late_queries(6, 8)
    late_queries(8, 11)
    relay(1)
    z_sum(0)
    late_queries(11, 14)
    x_sum(1)
    y_sum(0)
    input_grad()
    z_sum(1)
    place_queries(0, 7)
    y_sum(1)
    collect(0)
    place_queries(7, 14)
    collect(1)
    for copy in gather_started + d_started:
        copy.wait_send()
    for h in range(QH):
        hand_over(h).wait_send()
    for g in range(KVH):
        hand_over_kv(g).wait_send()

        @pl.when(x % 2 == hi)
        def _():
            for copy in share(g):
                copy.wait_send()


def shards(inputs, queries, out_grad, kv_weight, passage_blocks, handover):
    freq = ROPE_BASE ** (-(np.arange(HD // 2, dtype=np.float32) * 2.0) / HD)
    freq = jnp.asarray(np.concatenate([freq, freq])[None, :].astype(np.float32))
    dma = pltpu.SemaphoreType.DMA
    anywhere = pl.BlockSpec(memory_space=pl.ANY)
    scalars = pl.BlockSpec(memory_space=pltpu.SMEM)

    def vmem(*shape, kind=bf16):
        return pltpu.VMEM(shape, kind)

    packed = SENT * BLK
    shapes = (
        jax.ShapeDtypeStruct((ROWS, D), bf16),
        jax.ShapeDtypeStruct((ROWS, QH * HD), bf16),
        jax.ShapeDtypeStruct((SHARD, KV), f32),
    )
    return pl.pallas_call(
        kernel,
        name="grouped_attention_backward",
        out_shape=tuple(pltpu.VMEM(shape.shape, shape.dtype) for shape in shapes),
        in_specs=[scalars, scalars, VMEM, VMEM, anywhere, anywhere, anywhere],
        out_specs=(VMEM, VMEM, VMEM),
        scratch_shapes=[
            vmem(ROWS, D),
            vmem(ROWS, QH * HD),
            vmem(ROWS, QH * HD),
            vmem(D, ROWS),
            vmem(2 * KVH, 2, NZ, SHARD, HD),
            vmem(KVH, ROWS, HD),
            vmem(KVH, HD, ROWS),
            vmem(KVH, ROWS, HD),
            vmem(ROWS, HD, kind=f32),
            vmem(ROWS, HD, kind=f32),
            vmem(ROWS, ROWS, kind=f32),
            vmem(ROWS, HD, kind=f32),
            vmem(ROWS, HD, kind=f32),
            vmem(packed, ROWS),
            vmem(ROWS, packed),
            vmem(ROWS, HD, kind=f32),
            vmem(QH - LATE, ROWS, ROWS),
            vmem(QH, ROWS, HD),
            vmem(QH, packed, HD),
            vmem(QH, packed, HD),
            vmem(KVH, 2, ROWS, HD),
            vmem(KVH, 2, packed, HD),
            vmem(KVH, 2, packed, HD),
            vmem(ROWS, KV),
            vmem(KVH, 2, NF, SHARD, HD),
            vmem(KVH, NF, SHARD, HD),
            vmem(KVH, NF, SHARD, HD),
            vmem(2 * KVH, 4, HALF, HD),
            vmem(2 * KVH, 4, HALF, HD),
            vmem(2 * KVH, 4, HALF, HD),
            vmem(2 * KVH, 4, HALF, HD),
            vmem(KVH, NZ, HALF, HD),
            vmem(KVH * (NZ - 1), HALF, HD),
            vmem(KVH, HALF, HD),
            vmem(KVH, 4, HALF, HD),
            vmem(KVH, HALF, HD),
            vmem(KVH, 2, 2, HALF, HD),
            dma((3,)),
            dma((128,)),
            dma((16,)),
            dma((16,)),
            dma((32,)),
            dma((32,)),
            dma((32,)),
            dma((QH,)),
            dma((QH,)),
            dma((KVH,)),
            dma((KVH,)),
            dma((48,)),
            dma((8,)),
            dma((4,)),
            dma((4,)),
            dma((4,)),
            dma((KVH * (NZ - 1),)),
            dma((6,)),
            dma((14,)),
            dma((8,)),
        ],
        compiler_params=pltpu.CompilerParams(
            collective_id=0, has_side_effects=True, vmem_limit_bytes=LIMIT
        ),
    )(passage_blocks, handover, kv_weight, freq, inputs, queries, out_grad)


def solution(mesh):
    rows = P(("dp", "fsdp"), None)
    return jax.shard_map(
        shards,
        mesh=mesh,
        in_specs=(rows, rows, rows, P("fsdp", None), rows, rows),
        out_specs=(rows, rows, P("fsdp", None)),
        check_vma=False,
    )
```

```python
import jax
import jax.numpy as jnp
import numpy as np
from jax import lax
from jax.experimental import pallas as pl
from jax.experimental.pallas import tpu as pltpu
from jax.sharding import PartitionSpec as P

KVH = 2
GROUP = 7
HD = 128
QH = 14
NB = 6
BLK = 64
SENT = NB - 1
ROWS = NB * BLK
D = 3584
NX, NZ, NF = 4, 8, 16
SHARD = D // NF
HALF = SHARD // 2
CHUNK = 4 * SHARD
KV = 2 * KVH * HD
ROPE_BASE = 1000000.0
LOG2E = 1.4426950408889634
MESH = pl.DeviceIdType.MESH
VMEM = pl.BlockSpec(memory_space=pltpu.VMEM)
LIMIT = 56 * 1024 * 1024
f32, bf16 = jnp.float32, jnp.bfloat16


def place():
    d, f = lax.axis_index("dp"), lax.axis_index("fsdp")
    return d // 8, (d // 2) % NX, d % 2, f // NZ, f % NZ


def device(lo, x, c, hi, z):
    return (lo * 8 + x * 2 + c, hi * NZ + z)


def greet(peers):
    barrier = pltpu.get_barrier_semaphore()
    for peer in peers:
        pl.semaphore_signal(barrier, inc=1, device_id=peer, device_id_type=MESH)
    pl.semaphore_wait(barrier, len(peers))


def columns(index, width=HD):
    return pl.ds(pl.multiple_of(index * width, width), width)


def dot(a, b, dims):
    return lax.dot_general(a, b, ((dims[:1], dims[1:]), ((), ())), preferred_element_type=f32)


def handed_blocks(flags):
    rank, ranks = jnp.int32(0), []
    for b in range(NB):
        ranks.append(rank)
        rank = rank + flags[b]
    picks = []
    for r in range(SENT):
        pick = jnp.int32(0)
        for b in range(NB):
            pick = jnp.where((flags[b] == 1) & (ranks[b] == r), b, pick)
        picks.append(pick)
    return ranks, picks


HOPS = {1: 4, -1: 3}
LATE = 6
ARRIVES = {1: 1, 2: 2, 3: 3, 4: 4}
WAYS = [(1, 1), (-1, 1), (1, 2), (-1, 2), (1, 3), (-1, 3), (1, 4)]


def kernel(
    ids_ref, flags_ref, w_ref, freq_ref, x_hbm, q_hbm, g_hbm,
    gi, gq, gw,
    x_ref, q_ref, g_ref, x_t, weight,
    keys, keys_t, vals, kacc, vacc, bias, cosine, sine, to_pack, from_pack, kept,
    held, qg, qp, qr, kvg, kvp, kvr, chosen,
    part, sib, tot, relay_in, relay_out, direct, summed, after_x, z_in, after_z, y_in, final, shared,
    load, g_send, ring_recv, gy_recv, gx_recv, near_recv, far_recv,
    q_send, q_recv, kv_send, kv_recv,
    d_send, sib_recv, relay_recv, direct_recv, summed_recv, z_recv, y_recv, share_send, share_recv,
):
    lo, x, c, hi, z = place()
    y = 2 * hi + lo
    oth = 1 - hi
    sibling = device(lo, x, 1 - c, hi, z)
    partner = device(1 - lo, x, c, hi, z)
    cross = device(1 - lo, x, c, oth, z)
    across = device(lo, x, c, oth, z)
    x_side = ((x + 1) % NX, (x + NX - 1) % NX)
    x_peer = [device(lo, xs, c, hi, z) for xs in x_side]
    z_peer = [device(lo, x, c, hi, (z + s) % NZ) for s in range(1, NZ)]
    row_peer = [
        device(lo, (x + dx) % NX, (c + dc) % 2, hi, z)
        for dx in range(NX)
        for dc in range(2)
        if dx or dc
    ]
    loads = [
        pltpu.make_async_copy(src, dst, load.at[at])
        for at, (src, dst) in enumerate(((x_hbm, x_ref), (q_hbm, q_ref), (g_hbm, g_ref)))
    ]
    for copy in loads:
        copy.start()
    for q in range(2 * KVH):
        weight[q, hi, z] = w_ref[:, q * HD : (q + 1) * HD]
    greet(row_peer + z_peer + [partner, cross, across])

    def remote(src, dst, peer, sent, recv):
        return pltpu.make_async_remote_copy(
            src_ref=src,
            dst_ref=dst,
            send_sem=sent,
            recv_sem=recv,
            device_id=peer,
            device_id_type=MESH,
        )

    def pusher(sems):
        started = []

        def push(src, dst, peer, recv):
            copy = remote(src, dst, peer, sems.at[len(started)], recv)
            copy.start()
            started.append(copy)

        return push, started

    def arrived(dst, recv):
        remote(dst, dst, sibling, g_send.at[0], recv).wait_recv()

    ids = [ids_ref[0, b] for b in range(NB)]
    flags = [flags_ref[0, b] for b in range(NB)]
    ranks, picks = handed_blocks(flags)

    def set_masks():
        tall = lax.broadcasted_iota(jnp.int32, (ROWS, ROWS), 0)
        wide = lax.broadcasted_iota(jnp.int32, (ROWS, ROWS), 1)
        label_k = jnp.zeros((ROWS, ROWS), jnp.int32)
        label_q = jnp.zeros((ROWS, ROWS), jnp.int32)
        for b in range(NB):
            label_k = jnp.where(tall >= b * BLK, ids[b], label_k)
            label_q = jnp.where(wide >= b * BLK, ids[b], label_q)
        bias[...] = jnp.where(label_k == label_q, 0.0, -jnp.inf)

    def set_moves():
        tall = lax.broadcasted_iota(jnp.int32, (SENT * BLK, ROWS), 0)
        wide = lax.broadcasted_iota(jnp.int32, (SENT * BLK, ROWS), 1)
        shift = jnp.zeros((SENT * BLK, ROWS), jnp.int32)
        for r in range(SENT):
            shift = jnp.where(tall >= r * BLK, (picks[r] - r) * BLK, shift)
        to_pack[...] = jnp.where(tall + shift == wide, 1.0, 0.0).astype(bf16)
        tall = lax.broadcasted_iota(jnp.int32, (ROWS, SENT * BLK), 0)
        wide = lax.broadcasted_iota(jnp.int32, (ROWS, SENT * BLK), 1)
        shift = jnp.zeros((ROWS, SENT * BLK), jnp.int32)
        for b in range(NB):
            shift = jnp.where(tall >= b * BLK, (ranks[b] - b) * BLK, shift)
        from_pack[...] = jnp.where(tall + shift == wide, 1.0, 0.0).astype(bf16)
        row = lax.broadcasted_iota(jnp.int32, (ROWS, HD), 0)
        given = jnp.zeros((ROWS, HD), jnp.int32)
        for b in range(NB):
            given = jnp.where(row >= b * BLK, flags[b], given)
        kept[...] = (1 - given).astype(f32)

    def set_angles():
        first = [jnp.int32(0)]
        for b in range(1, NB):
            first.append(jnp.where(ids[b] == ids[b - 1], first[b - 1], b * BLK))
        row = lax.broadcasted_iota(jnp.int32, (ROWS, HD), 0)
        start = jnp.zeros((ROWS, HD), jnp.int32)
        for b in range(NB):
            start = jnp.where(row >= b * BLK, first[b], start)
        angle = (row - start).astype(f32) * freq_ref[...]
        cosine[...] = jnp.cos(angle)
        lane = lax.broadcasted_iota(jnp.int32, (ROWS, HD), 1)
        turn = jnp.sin(angle)
        sine[...] = jnp.where(lane < HD // 2, -turn, turn)

    def turn_inputs(first, count):
        @pl.loop(first, first + count)
        def _(n):
            x_t[pl.ds(pl.multiple_of(n * HD, HD), HD), :] = x_ref[:, columns(n)].T

    def piece_0():
        set_masks()
        set_moves()

    def piece_1():
        loads[0].wait()
        turn_inputs(0, 6)

    def piece_2():
        turn_inputs(6, 6)

    def piece_3():
        set_angles()

    def piece_4():
        turn_inputs(12, 16)

    pieces = {1: piece_1, 2: piece_2, 3: piece_3, 4: piece_4}

    push, gather_started = pusher(g_send)

    def source(way, hop):
        return (z + NZ - way * hop) % NZ

    def slot(way, hop):
        return 7 if hop == 0 else WAYS.index((way, hop))

    def piece(p, kind, row, zs, core):
        rows = pl.ds(pl.multiple_of(core * HALF, HALF), HALF)
        return weight.at[KVH * kind + p, row, zs, rows]

    near, far = x % 2, 1 - x % 2

    def gather_start(p):
        own = piece(p, near, hi, z, c)
        for way, hop in WAYS:
            peer = z_peer[(hop if way == 1 else NZ - hop) - 1]
            push(own, own, peer, ring_recv.at[p * 8 + slot(way, hop)])
            if (way, hop) == (-1, 1):
                push(own, own, cross, gy_recv.at[p * 8 + slot(1, 0)])

    def from_ring(p, way, hop):
        part = piece(p, near, hi, source(way, hop), c)
        at = slot(way, hop)
        arrived(part, ring_recv.at[p * 8 + at])
        push(part, part, cross, gy_recv.at[p * 8 + at])
        push(part, part, x_peer[0 if way == 1 else 1], gx_recv.at[p * 16 + at])
        push(part, part, sibling, near_recv.at[p * 16 + at])

    def from_y(p, way, hop):
        part = piece(p, near, oth, source(way, hop), c)
        at = slot(way, hop)
        arrived(part, gy_recv.at[p * 8 + at])
        push(part, part, x_peer[1 if way == 1 and hop else 0], gx_recv.at[p * 16 + 8 + at])
        push(part, part, sibling, near_recv.at[p * 16 + 8 + at])

    def from_x(p, row, half, way, hop):
        part = piece(p, far, row, source(way, hop), c)
        at = p * 16 + half * 8 + slot(way, hop)
        arrived(part, gx_recv.at[at])
        push(part, part, sibling, far_recv.at[at])

    def gather_step(p, time):
        for way in (1, -1):
            if time in ARRIVES and ARRIVES[time] <= HOPS[way]:
                from_ring(p, way, ARRIVES[time])
        if time == 2:
            from_y(p, 1, 0)
        for way in (1, -1):
            if time - 1 in ARRIVES and ARRIVES[time - 1] <= HOPS[way]:
                from_y(p, way, ARRIVES[time - 1])
        if time == 3:
            from_x(p, oth, 1, 1, 0)
        for way in (1, -1):
            if time - 1 in ARRIVES and ARRIVES[time - 1] <= HOPS[way]:
                from_x(p, hi, 0, way, ARRIVES[time - 1])
            if time - 2 in ARRIVES and ARRIVES[time - 2] <= HOPS[way]:
                from_x(p, oth, 1, way, ARRIVES[time - 2])

    def gather_end(p):
        for half, row in ((0, hi), (1, oth)):
            for way, hop in WAYS + [(1, 0)] * half:
                at = p * 16 + half * 8 + slot(way, hop)
                arrived(piece(p, near, row, source(way, hop), 1 - c), near_recv.at[at])
                arrived(piece(p, far, row, source(way, hop), 1 - c), far_recv.at[at])

    def weight_rows(n, blocks=range(2 * KVH)):
        at = pl.ds((n % 2) * 4, 4)
        return jnp.concatenate([weight[q, n // 2, at].reshape(CHUNK, HD) for q in blocks], axis=1)

    def project(g):
        projected = jnp.zeros((ROWS, 2 * HD), f32)
        for n in range(4):
            rows = weight_rows(n, (g, KVH + g))
            projected += dot(x_ref[:, n * CHUNK : (n + 1) * CHUNK], rows, (1, 0))
        raw = projected[:, :HD]
        key = raw * cosine[...] + pltpu.roll(raw, HD // 2, 1) * sine[...]
        keys[g] = key.astype(bf16)
        keys_t[g] = key.T.astype(bf16)
        vals[g] = projected[:, HD:].astype(bf16)

    gather_start(0)
    piece_0()
    for time in range(1, 7):
        gather_step(0, time)
        if time == 2:
            gather_start(1)
        if time in pieces:
            pieces[time]()
    gather_step(1, 1)
    gather_end(0)
    project(0)
    gather_step(1, 2)
    loads[1].wait()
    loads[2].wait()

    scale = 1.0 / HD**0.5

    def hand_over(h):
        return remote(qp.at[h], qr.at[h], partner, q_send.at[h], q_recv.at[h])

    def query_part(h, dscores_b):
        own = (dot(keys_t[h // GROUP], dscores_b, (1, 0)) * scale).T.astype(bf16)
        qg[h] = own
        qp[h] = dot(to_pack[...], own, (1, 0)).astype(bf16)
        hand_over(h).start()

    def late_queries(first, last):
        for h in range(first, last):
            query_part(h, held[h - LATE])

    def heads(g, first, last):
        for h in range(first, last):
            query, grad = q_ref[:, h * HD : (h + 1) * HD], g_ref[:, h * HD : (h + 1) * HD]
            scores = dot(keys[g], query, (1, 1)) * (scale * LOG2E) + bias[...]
            weights = jnp.exp2(scores - jnp.max(scores, axis=0, keepdims=True))
            probs = weights * (1.0 / jnp.sum(weights, axis=0, keepdims=True))
            probs_b = probs.astype(bf16)
            dprobs = dot(vals[g], grad, (1, 1))
            delta = jnp.sum(probs_b.astype(f32) * dprobs, axis=0, keepdims=True)
            dscores_b = (probs * (dprobs - delta)).astype(bf16)
            vacc[...] += dot(probs_b, grad, (1, 0))
            kacc[...] += dot(dscores_b, query, (1, 0))
            if h < LATE:
                query_part(h, dscores_b)
            else:
                held[h - LATE] = dscores_b

    def clear():
        kacc[...] = jnp.zeros_like(kacc)
        vacc[...] = jnp.zeros_like(vacc)

    def hand_over_kv(g):
        return remote(kvp.at[g], kvr.at[g], partner, kv_send.at[g], kv_recv.at[g])

    def finish_group(g):
        grad_k = kacc[...] * scale
        raw = grad_k * cosine[...] - pltpu.roll(grad_k, HD // 2, 1) * sine[...]
        kvg[g, 0] = raw.astype(bf16)
        kvg[g, 1] = vacc[...].astype(bf16)
        for t in range(2):
            kvp[g, t] = dot(to_pack[...], kvg[g, t], (1, 0)).astype(bf16)
        hand_over_kv(g).start()

    push_d, d_started = pusher(d_send)

    def chunk(i):
        return 2 * (x % 2 if i < 2 else 1 - x % 2) + i % 2

    def product(g, i):
        n = chunk(i)
        pair = jnp.concatenate([kvg[g, 0], kvg[g, 1]], axis=1)
        rows = pl.ds(pl.multiple_of(n * CHUNK, CHUNK), CHUNK)
        result = dot(x_t[rows, :], pair, (1, 0)).astype(bf16)
        four = pl.ds(n * 4, 4)
        for t in range(2):
            part[g, t, four] = result[:, t * HD : (t + 1) * HD].reshape(4, SHARD, HD)
        push_d(part.at[g, 1 - c, four], sib.at[g, four], sibling, sib_recv.at[g * 4 + i])

    def box(xs, side):
        owners = pl.ds((xs % 2) * NZ + 4 * side, 4)
        return owners, pl.ds(pl.multiple_of((xs // 2) * HALF, HALF), HALF)

    def core_sum(g, i):
        four = pl.ds(chunk(i) * 4, 4)
        arrived(sib.at[g, four], sib_recv.at[g * 4 + i])
        total = part[g, c, four].astype(f32) + sib[g, four].astype(f32)
        tot[g, four] = total.astype(bf16)
        if i < 2:
            side, at = i, 2 * g + i
            owners, rows = box((x + 2) % NX, side)
            push_d(tot.at[g, owners, rows], relay_in.at[at], x_peer[side], relay_recv.at[at])
        else:
            side, at = 3 - i, 2 * g + 3 - i
            owners, rows = box(x_side[side], 1 - side)
            push_d(tot.at[g, owners, rows], direct.at[at], x_peer[side], direct_recv.at[at])

    def relay(g):
        for side in range(2):
            at = 2 * g + side
            owners, rows = box(x_side[side], side)
            arrived(relay_in.at[at], relay_recv.at[at])
            total = tot[g, owners, rows].astype(f32) + relay_in[at].astype(f32)
            relay_out[at] = total.astype(bf16)
            push_d(relay_out.at[at], summed.at[at], x_peer[side], summed_recv.at[at])

    def x_sum(g):
        for side in range(2):
            at, other = 2 * g + side, 2 * g + 1 - side
            owners, rows = box(x, side)
            arrived(direct.at[other], direct_recv.at[other])
            arrived(summed.at[at], summed_recv.at[at])
            got = summed[at].astype(f32) + direct[other].astype(f32)
            total = tot[g, owners, rows].astype(f32) + got
            after_x[g, side * 4 : (side + 1) * 4] = total.astype(bf16)
        for s in range(1, NZ):
            at = g * (NZ - 1) + s - 1
            push_d(after_x.at[g, (z + s) % NZ], z_in.at[at], z_peer[s - 1], z_recv.at[at])

    def z_sum(g):
        total = after_x[g, z].astype(f32)
        for s in range(1, NZ):
            at = g * (NZ - 1) + s - 1
            arrived(z_in.at[at], z_recv.at[at])
            total = total + z_in[at].astype(f32)
        after_z[g] = total.astype(bf16)
        y_in[g, y] = after_z[g]
        for n, peer in enumerate((partner, cross, across)):
            push_d(after_z.at[g], y_in.at[g, y], peer, y_recv.at[3 * g + n])

    def share(g):
        return [
            remote(
                final.at[g],
                shared.at[g, x // 2, c],
                peer,
                share_send.at[g * 7 + n],
                share_recv.at[g * 4 + (x // 2) * 2 + c],
            )
            for n, peer in enumerate(row_peer)
        ]

    def y_sum(g):
        arrived(y_in.at[g, 2 * hi + 1 - lo], y_recv.at[3 * g])
        arrived(y_in.at[g, 2 * oth + 1 - lo], y_recv.at[3 * g + 1])
        arrived(y_in.at[g, 2 * oth + lo], y_recv.at[3 * g + 2])
        total = y_in[g, 0].astype(f32)
        for at in range(1, 4):
            total = total + y_in[g, at].astype(f32)
        final[g] = total.astype(bf16)

        @pl.when(x % 2 == hi)
        def _():
            shared[g, x // 2, c] = final[g]
            for copy in share(g):
                copy.start()

    def collect(g):
        for half in range(2):
            for core in range(2):
                mine = (x % 2 == hi) & (x // 2 == half) & (c == core)

                @pl.when(jnp.logical_not(mine))
                def _():
                    at = g * 4 + half * 2 + core
                    arrived(shared.at[g, half, core], share_recv.at[at])

                gw[half * HALF : (half + 1) * HALF, (core * KVH + g) * HD : (core * KVH + g + 1) * HD] = (
                    shared[g, half, core].astype(f32)
                )

    def pick(own, other):
        taken = dot(from_pack[...], other, (1, 0))
        return jnp.where(kept[...] > 0.5, own.astype(f32), taken).astype(bf16)

    def input_grad():
        for g in range(KVH):
            arrived(kvr.at[g], kv_recv.at[g])
        for g in range(KVH):
            for t in range(2):
                at = (t * KVH + g) * HD
                chosen[:, at : at + HD] = pick(kvg[g, t], kvr[g, t])
        for n in range(4):
            cols = slice(n * CHUNK, (n + 1) * CHUNK)
            gi[:, cols] = dot(chosen[...], weight_rows(n), (1, 1)).astype(bf16)

    def place_queries(first, last):
        @pl.loop(first, last)
        def _(h):
            arrived(qr.at[h], q_recv.at[h])
            gq[:, columns(h)] = pick(qg[h], qr[h])

    clear()
    for h in range(GROUP):
        heads(0, h, h + 1)
        if h in (1, 3, 5):
            gather_step(1, 3 + h // 2)
    finish_group(0)
    clear()
    for i in range(4):
        product(0, i)
    gather_step(1, 6)
    for i in range(4):
        core_sum(0, i)
    gather_end(1)
    project(1)
    heads(1, 7, 13)
    relay(0)
    heads(1, 13, 14)
    finish_group(1)
    product(1, 0)
    product(1, 1)
    core_sum(1, 0)
    product(1, 2)
    core_sum(1, 1)
    product(1, 3)
    core_sum(1, 2)
    core_sum(1, 3)
    x_sum(0)
    late_queries(6, 11)
    relay(1)
    z_sum(0)
    late_queries(11, 14)
    x_sum(1)
    input_grad()
    z_sum(1)
    y_sum(0)
    place_queries(0, 7)
    y_sum(1)
    collect(0)
    place_queries(7, 14)
    collect(1)
    for copy in gather_started + d_started:
        copy.wait_send()
    for h in range(QH):
        hand_over(h).wait_send()
    for g in range(KVH):
        hand_over_kv(g).wait_send()

        @pl.when(x % 2 == hi)
        def _():
            for copy in share(g):
                copy.wait_send()


def shards(inputs, queries, out_grad, kv_weight, passage_blocks, handover):
    freq = ROPE_BASE ** (-(np.arange(HD // 2, dtype=np.float32) * 2.0) / HD)
    freq = jnp.asarray(np.concatenate([freq, freq])[None, :].astype(np.float32))
    dma = pltpu.SemaphoreType.DMA
    anywhere = pl.BlockSpec(memory_space=pl.ANY)
    scalars = pl.BlockSpec(memory_space=pltpu.SMEM)

    def vmem(*shape, kind=bf16):
        return pltpu.VMEM(shape, kind)

    packed = SENT * BLK
    shapes = (
        jax.ShapeDtypeStruct((ROWS, D), bf16),
        jax.ShapeDtypeStruct((ROWS, QH * HD), bf16),
        jax.ShapeDtypeStruct((SHARD, KV), f32),
    )
    return pl.pallas_call(
        kernel,
        name="grouped_attention_backward",
        out_shape=tuple(pltpu.VMEM(shape.shape, shape.dtype) for shape in shapes),
        in_specs=[scalars, scalars, VMEM, VMEM, anywhere, anywhere, anywhere],
        out_specs=(VMEM, VMEM, VMEM),
        scratch_shapes=[
            vmem(ROWS, D),
            vmem(ROWS, QH * HD),
            vmem(ROWS, QH * HD),
            vmem(D, ROWS),
            vmem(2 * KVH, 2, NZ, SHARD, HD),
            vmem(KVH, ROWS, HD),
            vmem(KVH, HD, ROWS),
            vmem(KVH, ROWS, HD),
            vmem(ROWS, HD, kind=f32),
            vmem(ROWS, HD, kind=f32),
            vmem(ROWS, ROWS, kind=f32),
            vmem(ROWS, HD, kind=f32),
            vmem(ROWS, HD, kind=f32),
            vmem(packed, ROWS),
            vmem(ROWS, packed),
            vmem(ROWS, HD, kind=f32),
            vmem(QH - LATE, ROWS, ROWS),
            vmem(QH, ROWS, HD),
            vmem(QH, packed, HD),
            vmem(QH, packed, HD),
            vmem(KVH, 2, ROWS, HD),
            vmem(KVH, 2, packed, HD),
            vmem(KVH, 2, packed, HD),
            vmem(ROWS, KV),
            vmem(KVH, 2, NF, SHARD, HD),
            vmem(KVH, NF, SHARD, HD),
            vmem(KVH, NF, SHARD, HD),
            vmem(2 * KVH, 4, HALF, HD),
            vmem(2 * KVH, 4, HALF, HD),
            vmem(2 * KVH, 4, HALF, HD),
            vmem(2 * KVH, 4, HALF, HD),
            vmem(KVH, NZ, HALF, HD),
            vmem(KVH * (NZ - 1), HALF, HD),
            vmem(KVH, HALF, HD),
            vmem(KVH, 4, HALF, HD),
            vmem(KVH, HALF, HD),
            vmem(KVH, 2, 2, HALF, HD),
            dma((3,)),
            dma((128,)),
            dma((16,)),
            dma((16,)),
            dma((32,)),
            dma((32,)),
            dma((32,)),
            dma((QH,)),
            dma((QH,)),
            dma((KVH,)),
            dma((KVH,)),
            dma((48,)),
            dma((8,)),
            dma((4,)),
            dma((4,)),
            dma((4,)),
            dma((KVH * (NZ - 1),)),
            dma((6,)),
            dma((14,)),
            dma((8,)),
        ],
        compiler_params=pltpu.CompilerParams(
            collective_id=0, has_side_effects=True, vmem_limit_bytes=LIMIT
        ),
    )(passage_blocks, handover, kv_weight, freq, inputs, queries, out_grad)


def solution(mesh):
    rows = P(("dp", "fsdp"), None)
    return jax.shard_map(
        shards,
        mesh=mesh,
        in_specs=(rows, rows, rows, P("fsdp", None), rows, rows),
        out_specs=(rows, rows, P("fsdp", None)),
        check_vma=False,
    )
```

```python
import jax
import jax.numpy as jnp
import numpy as np
from jax import lax
from jax.experimental import pallas as pl
from jax.experimental.pallas import tpu as pltpu
from jax.sharding import PartitionSpec as P

KVH = 2
GROUP = 7
HD = 128
QH = 14
NB = 6
BLK = 64
SENT = NB - 1
ROWS = NB * BLK
D = 3584
NX, NZ, NF = 4, 8, 16
SHARD = D // NF
HALF = SHARD // 2
CHUNK = 4 * SHARD
KV = 2 * KVH * HD
ROPE_BASE = 1000000.0
LOG2E = 1.4426950408889634
MESH = pl.DeviceIdType.MESH
VMEM = pl.BlockSpec(memory_space=pltpu.VMEM)
LIMIT = 56 * 1024 * 1024
f32, bf16 = jnp.float32, jnp.bfloat16


def place():
    d, f = lax.axis_index("dp"), lax.axis_index("fsdp")
    return d // 8, (d // 2) % NX, d % 2, f // NZ, f % NZ


def device(lo, x, c, hi, z):
    return (lo * 8 + x * 2 + c, hi * NZ + z)


def greet(peers):
    barrier = pltpu.get_barrier_semaphore()
    for peer in peers:
        pl.semaphore_signal(barrier, inc=1, device_id=peer, device_id_type=MESH)
    pl.semaphore_wait(barrier, len(peers))


def columns(index, width=HD):
    return pl.ds(pl.multiple_of(index * width, width), width)


def dot(a, b, dims):
    return lax.dot_general(a, b, ((dims[:1], dims[1:]), ((), ())), preferred_element_type=f32)


def handed_blocks(flags):
    rank, ranks = jnp.int32(0), []
    for b in range(NB):
        ranks.append(rank)
        rank = rank + flags[b]
    picks = []
    for r in range(SENT):
        pick = jnp.int32(0)
        for b in range(NB):
            pick = jnp.where((flags[b] == 1) & (ranks[b] == r), b, pick)
        picks.append(pick)
    return ranks, picks


HOPS = {1: 4, -1: 3}
LATE = 9
ARRIVES = {1: 1, 2: 2, 3: 3, 4: 4}
WAYS = [(1, 1), (-1, 1), (1, 2), (-1, 2), (1, 3), (-1, 3), (1, 4)]


def kernel(
    ids_ref, flags_ref, w_ref, freq_ref, x_hbm, q_hbm, g_hbm,
    gi, gq, gw,
    x_ref, q_ref, g_ref, x_t, weight,
    keys, keys_t, vals, kacc, vacc, bias, cosine, sine, to_pack, from_pack, kept,
    held, qg, qp, qr, kvg, kvp, kvr, chosen,
    part, sib, tot, relay_in, relay_out, direct, summed, after_x, z_in, after_z, y_in, final, shared,
    load, g_send, ring_recv, gy_recv, gx_recv, near_recv, far_recv,
    q_send, q_recv, kv_send, kv_recv,
    d_send, sib_recv, relay_recv, direct_recv, summed_recv, z_recv, y_recv, share_send, share_recv,
):
    lo, x, c, hi, z = place()
    y = 2 * hi + lo
    oth = 1 - hi
    sibling = device(lo, x, 1 - c, hi, z)
    partner = device(1 - lo, x, c, hi, z)
    cross = device(1 - lo, x, c, oth, z)
    across = device(lo, x, c, oth, z)
    x_side = ((x + 1) % NX, (x + NX - 1) % NX)
    x_peer = [device(lo, xs, c, hi, z) for xs in x_side]
    z_peer = [device(lo, x, c, hi, (z + s) % NZ) for s in range(1, NZ)]
    row_peer = [
        device(lo, (x + dx) % NX, (c + dc) % 2, hi, z)
        for dx in range(NX)
        for dc in range(2)
        if dx or dc
    ]
    loads = [
        pltpu.make_async_copy(src, dst, load.at[at])
        for at, (src, dst) in enumerate(((x_hbm, x_ref), (q_hbm, q_ref), (g_hbm, g_ref)))
    ]
    for copy in loads:
        copy.start()
    for q in range(2 * KVH):
        weight[q, hi, z] = w_ref[:, q * HD : (q + 1) * HD]
    greet(row_peer + z_peer + [partner, cross, across])

    def remote(src, dst, peer, sent, recv):
        return pltpu.make_async_remote_copy(
            src_ref=src,
            dst_ref=dst,
            send_sem=sent,
            recv_sem=recv,
            device_id=peer,
            device_id_type=MESH,
        )

    def pusher(sems):
        started = []

        def push(src, dst, peer, recv):
            copy = remote(src, dst, peer, sems.at[len(started)], recv)
            copy.start()
            started.append(copy)

        return push, started

    def arrived(dst, recv):
        remote(dst, dst, sibling, g_send.at[0], recv).wait_recv()

    ids = [ids_ref[0, b] for b in range(NB)]
    flags = [flags_ref[0, b] for b in range(NB)]
    ranks, picks = handed_blocks(flags)

    def set_masks():
        tall = lax.broadcasted_iota(jnp.int32, (ROWS, ROWS), 0)
        wide = lax.broadcasted_iota(jnp.int32, (ROWS, ROWS), 1)
        label_k = jnp.zeros((ROWS, ROWS), jnp.int32)
        label_q = jnp.zeros((ROWS, ROWS), jnp.int32)
        for b in range(NB):
            label_k = jnp.where(tall >= b * BLK, ids[b], label_k)
            label_q = jnp.where(wide >= b * BLK, ids[b], label_q)
        bias[...] = jnp.where(label_k == label_q, 0.0, -jnp.inf)

    def set_moves():
        tall = lax.broadcasted_iota(jnp.int32, (SENT * BLK, ROWS), 0)
        wide = lax.broadcasted_iota(jnp.int32, (SENT * BLK, ROWS), 1)
        shift = jnp.zeros((SENT * BLK, ROWS), jnp.int32)
        for r in range(SENT):
            shift = jnp.where(tall >= r * BLK, (picks[r] - r) * BLK, shift)
        to_pack[...] = jnp.where(tall + shift == wide, 1.0, 0.0).astype(bf16)
        tall = lax.broadcasted_iota(jnp.int32, (ROWS, SENT * BLK), 0)
        wide = lax.broadcasted_iota(jnp.int32, (ROWS, SENT * BLK), 1)
        shift = jnp.zeros((ROWS, SENT * BLK), jnp.int32)
        for b in range(NB):
            shift = jnp.where(tall >= b * BLK, (ranks[b] - b) * BLK, shift)
        from_pack[...] = jnp.where(tall + shift == wide, 1.0, 0.0).astype(bf16)
        row = lax.broadcasted_iota(jnp.int32, (ROWS, HD), 0)
        given = jnp.zeros((ROWS, HD), jnp.int32)
        for b in range(NB):
            given = jnp.where(row >= b * BLK, flags[b], given)
        kept[...] = (1 - given).astype(f32)

    def set_angles():
        first = [jnp.int32(0)]
        for b in range(1, NB):
            first.append(jnp.where(ids[b] == ids[b - 1], first[b - 1], b * BLK))
        row = lax.broadcasted_iota(jnp.int32, (ROWS, HD), 0)
        start = jnp.zeros((ROWS, HD), jnp.int32)
        for b in range(NB):
            start = jnp.where(row >= b * BLK, first[b], start)
        angle = (row - start).astype(f32) * freq_ref[...]
        cosine[...] = jnp.cos(angle)
        lane = lax.broadcasted_iota(jnp.int32, (ROWS, HD), 1)
        turn = jnp.sin(angle)
        sine[...] = jnp.where(lane < HD // 2, -turn, turn)

    def turn_inputs(first, count):
        @pl.loop(first, first + count)
        def _(n):
            x_t[pl.ds(pl.multiple_of(n * HD, HD), HD), :] = x_ref[:, columns(n)].T

    def piece_0():
        set_masks()
        set_moves()

    def piece_1():
        loads[0].wait()
        turn_inputs(0, 6)

    def piece_2():
        turn_inputs(6, 6)

    def piece_3():
        set_angles()

    def piece_4():
        turn_inputs(12, 16)

    pieces = {1: piece_1, 2: piece_2, 3: piece_3, 4: piece_4}

    push, gather_started = pusher(g_send)

    def source(way, hop):
        return (z + NZ - way * hop) % NZ

    def slot(way, hop):
        return 7 if hop == 0 else WAYS.index((way, hop))

    def piece(p, kind, row, zs, core):
        rows = pl.ds(pl.multiple_of(core * HALF, HALF), HALF)
        return weight.at[KVH * kind + p, row, zs, rows]

    near, far = x % 2, 1 - x % 2

    def gather_start(p):
        own = piece(p, near, hi, z, c)
        for way, hop in WAYS:
            peer = z_peer[(hop if way == 1 else NZ - hop) - 1]
            push(own, own, peer, ring_recv.at[p * 8 + slot(way, hop)])
            if (way, hop) == (-1, 1):
                push(own, own, cross, gy_recv.at[p * 8 + slot(1, 0)])

    def from_ring(p, way, hop):
        part = piece(p, near, hi, source(way, hop), c)
        at = slot(way, hop)
        arrived(part, ring_recv.at[p * 8 + at])
        push(part, part, cross, gy_recv.at[p * 8 + at])
        push(part, part, x_peer[0 if way == 1 else 1], gx_recv.at[p * 16 + at])
        push(part, part, sibling, near_recv.at[p * 16 + at])

    def from_y(p, way, hop):
        part = piece(p, near, oth, source(way, hop), c)
        at = slot(way, hop)
        arrived(part, gy_recv.at[p * 8 + at])
        push(part, part, x_peer[1 if way == 1 and hop else 0], gx_recv.at[p * 16 + 8 + at])
        push(part, part, sibling, near_recv.at[p * 16 + 8 + at])

    def from_x(p, row, half, way, hop):
        part = piece(p, far, row, source(way, hop), c)
        at = p * 16 + half * 8 + slot(way, hop)
        arrived(part, gx_recv.at[at])
        push(part, part, sibling, far_recv.at[at])

    def gather_step(p, time):
        for way in (1, -1):
            if time in ARRIVES and ARRIVES[time] <= HOPS[way]:
                from_ring(p, way, ARRIVES[time])
        if time == 2:
            from_y(p, 1, 0)
        for way in (1, -1):
            if time - 1 in ARRIVES and ARRIVES[time - 1] <= HOPS[way]:
                from_y(p, way, ARRIVES[time - 1])
        if time == 3:
            from_x(p, oth, 1, 1, 0)
        for way in (1, -1):
            if time - 1 in ARRIVES and ARRIVES[time - 1] <= HOPS[way]:
                from_x(p, hi, 0, way, ARRIVES[time - 1])
            if time - 2 in ARRIVES and ARRIVES[time - 2] <= HOPS[way]:
                from_x(p, oth, 1, way, ARRIVES[time - 2])

    def gather_end(p):
        for half, row in ((0, hi), (1, oth)):
            for way, hop in WAYS + [(1, 0)] * half:
                at = p * 16 + half * 8 + slot(way, hop)
                arrived(piece(p, near, row, source(way, hop), 1 - c), near_recv.at[at])
                arrived(piece(p, far, row, source(way, hop), 1 - c), far_recv.at[at])

    def weight_rows(n, blocks=range(2 * KVH)):
        at = pl.ds((n % 2) * 4, 4)
        return jnp.concatenate([weight[q, n // 2, at].reshape(CHUNK, HD) for q in blocks], axis=1)

    def project(g):
        projected = jnp.zeros((ROWS, 2 * HD), f32)
        for n in range(4):
            rows = weight_rows(n, (g, KVH + g))
            projected += dot(x_ref[:, n * CHUNK : (n + 1) * CHUNK], rows, (1, 0))
        raw = projected[:, :HD]
        key = raw * cosine[...] + pltpu.roll(raw, HD // 2, 1) * sine[...]
        keys[g] = key.astype(bf16)
        keys_t[g] = key.T.astype(bf16)
        vals[g] = projected[:, HD:].astype(bf16)

    gather_start(0)
    piece_0()
    for time in range(1, 7):
        gather_step(0, time)
        if time == 2:
            gather_start(1)
        if time in pieces:
            pieces[time]()
    gather_step(1, 1)
    gather_end(0)
    project(0)
    gather_step(1, 2)
    loads[1].wait()
    loads[2].wait()

    scale = 1.0 / HD**0.5

    def hand_over(h):
        return remote(qp.at[h], qr.at[h], partner, q_send.at[h], q_recv.at[h])

    def query_part(h, dscores_b):
        own = (dot(keys_t[h // GROUP], dscores_b, (1, 0)) * scale).T.astype(bf16)
        qg[h] = own
        qp[h] = dot(to_pack[...], own, (1, 0)).astype(bf16)
        hand_over(h).start()

    def late_queries(first, last):
        for h in range(first, last):
            query_part(h, held[h - LATE])

    def heads(g, first, last):
        for h in range(first, last):
            query, grad = q_ref[:, h * HD : (h + 1) * HD], g_ref[:, h * HD : (h + 1) * HD]
            scores = dot(keys[g], query, (1, 1)) * (scale * LOG2E) + bias[...]
            weights = jnp.exp2(scores - jnp.max(scores, axis=0, keepdims=True))
            probs = weights * (1.0 / jnp.sum(weights, axis=0, keepdims=True))
            probs_b = probs.astype(bf16)
            dprobs = dot(vals[g], grad, (1, 1))
            delta = jnp.sum(probs_b.astype(f32) * dprobs, axis=0, keepdims=True)
            dscores_b = (probs * (dprobs - delta)).astype(bf16)
            vacc[...] += dot(probs_b, grad, (1, 0))
            kacc[...] += dot(dscores_b, query, (1, 0))
            if h < LATE:
                query_part(h, dscores_b)
            else:
                held[h - LATE] = dscores_b

    def clear():
        kacc[...] = jnp.zeros_like(kacc)
        vacc[...] = jnp.zeros_like(vacc)

    def hand_over_kv(g):
        return remote(kvp.at[g], kvr.at[g], partner, kv_send.at[g], kv_recv.at[g])

    def finish_group(g):
        grad_k = kacc[...] * scale
        raw = grad_k * cosine[...] - pltpu.roll(grad_k, HD // 2, 1) * sine[...]
        kvg[g, 0] = raw.astype(bf16)
        kvg[g, 1] = vacc[...].astype(bf16)
        for t in range(2):
            kvp[g, t] = dot(to_pack[...], kvg[g, t], (1, 0)).astype(bf16)
        hand_over_kv(g).start()

    push_d, d_started = pusher(d_send)

    def chunk(i):
        return 2 * (x % 2 if i < 2 else 1 - x % 2) + i % 2

    def product(g, i):
        n = chunk(i)
        pair = jnp.concatenate([kvg[g, 0], kvg[g, 1]], axis=1)
        rows = pl.ds(pl.multiple_of(n * CHUNK, CHUNK), CHUNK)
        result = dot(x_t[rows, :], pair, (1, 0)).astype(bf16)
        four = pl.ds(n * 4, 4)
        for t in range(2):
            part[g, t, four] = result[:, t * HD : (t + 1) * HD].reshape(4, SHARD, HD)
        push_d(part.at[g, 1 - c, four], sib.at[g, four], sibling, sib_recv.at[g * 4 + i])

    def box(xs, side):
        owners = pl.ds((xs % 2) * NZ + 4 * side, 4)
        return owners, pl.ds(pl.multiple_of((xs // 2) * HALF, HALF), HALF)

    def core_sum(g, i):
        four = pl.ds(chunk(i) * 4, 4)
        arrived(sib.at[g, four], sib_recv.at[g * 4 + i])
        total = part[g, c, four].astype(f32) + sib[g, four].astype(f32)
        tot[g, four] = total.astype(bf16)
        if i < 2:
            side, at = i, 2 * g + i
            owners, rows = box((x + 2) % NX, side)
            push_d(tot.at[g, owners, rows], relay_in.at[at], x_peer[side], relay_recv.at[at])
        else:
            side, at = 3 - i, 2 * g + 3 - i
            owners, rows = box(x_side[side], 1 - side)
            push_d(tot.at[g, owners, rows], direct.at[at], x_peer[side], direct_recv.at[at])

    def relay(g):
        for side in range(2):
            at = 2 * g + side
            owners, rows = box(x_side[side], side)
            arrived(relay_in.at[at], relay_recv.at[at])
            total = tot[g, owners, rows].astype(f32) + relay_in[at].astype(f32)
            relay_out[at] = total.astype(bf16)
            push_d(relay_out.at[at], summed.at[at], x_peer[side], summed_recv.at[at])

    def x_sum(g):
        for side in range(2):
            at, other = 2 * g + side, 2 * g + 1 - side
            owners, rows = box(x, side)
            arrived(direct.at[other], direct_recv.at[other])
            arrived(summed.at[at], summed_recv.at[at])
            got = summed[at].astype(f32) + direct[other].astype(f32)
            total = tot[g, owners, rows].astype(f32) + got
            after_x[g, side * 4 : (side + 1) * 4] = total.astype(bf16)
        for s in range(1, NZ):
            at = g * (NZ - 1) + s - 1
            push_d(after_x.at[g, (z + s) % NZ], z_in.at[at], z_peer[s - 1], z_recv.at[at])

    def z_sum(g):
        total = after_x[g, z].astype(f32)
        for s in range(1, NZ):
            at = g * (NZ - 1) + s - 1
            arrived(z_in.at[at], z_recv.at[at])
            total = total + z_in[at].astype(f32)
        after_z[g] = total.astype(bf16)
        y_in[g, y] = after_z[g]
        for n, peer in enumerate((partner, cross, across)):
            push_d(after_z.at[g], y_in.at[g, y], peer, y_recv.at[3 * g + n])

    def share(g):
        return [
            remote(
                final.at[g],
                shared.at[g, x // 2, c],
                peer,
                share_send.at[g * 7 + n],
                share_recv.at[g * 4 + (x // 2) * 2 + c],
            )
            for n, peer in enumerate(row_peer)
        ]

    def y_sum(g):
        arrived(y_in.at[g, 2 * hi + 1 - lo], y_recv.at[3 * g])
        arrived(y_in.at[g, 2 * oth + 1 - lo], y_recv.at[3 * g + 1])
        arrived(y_in.at[g, 2 * oth + lo], y_recv.at[3 * g + 2])
        total = y_in[g, 0].astype(f32)
        for at in range(1, 4):
            total = total + y_in[g, at].astype(f32)
        final[g] = total.astype(bf16)

        @pl.when(x % 2 == hi)
        def _():
            shared[g, x // 2, c] = final[g]
            for copy in share(g):
                copy.start()

    def collect(g):
        for half in range(2):
            for core in range(2):
                mine = (x % 2 == hi) & (x // 2 == half) & (c == core)

                @pl.when(jnp.logical_not(mine))
                def _():
                    at = g * 4 + half * 2 + core
                    arrived(shared.at[g, half, core], share_recv.at[at])

                gw[half * HALF : (half + 1) * HALF, (core * KVH + g) * HD : (core * KVH + g + 1) * HD] = (
                    shared[g, half, core].astype(f32)
                )

    def pick(own, other):
        taken = dot(from_pack[...], other, (1, 0))
        return jnp.where(kept[...] > 0.5, own.astype(f32), taken).astype(bf16)

    def input_grad():
        for g in range(KVH):
            arrived(kvr.at[g], kv_recv.at[g])
        for g in range(KVH):
            for t in range(2):
                at = (t * KVH + g) * HD
                chosen[:, at : at + HD] = pick(kvg[g, t], kvr[g, t])
        for n in range(4):
            cols = slice(n * CHUNK, (n + 1) * CHUNK)
            gi[:, cols] = dot(chosen[...], weight_rows(n), (1, 1)).astype(bf16)

    def place_queries(first, last):
        @pl.loop(first, last)
        def _(h):
            arrived(qr.at[h], q_recv.at[h])
            gq[:, columns(h)] = pick(qg[h], qr[h])

    clear()
    for h in range(GROUP):
        heads(0, h, h + 1)
        if h in (1, 3, 5):
            gather_step(1, 3 + h // 2)
    finish_group(0)
    clear()
    for i in range(4):
        product(0, i)
    gather_step(1, 6)
    for i in range(4):
        core_sum(0, i)
    gather_end(1)
    project(1)
    heads(1, 7, 13)
    relay(0)
    heads(1, 13, 14)
    finish_group(1)
    product(1, 0)
    product(1, 1)
    core_sum(1, 0)
    product(1, 2)
    core_sum(1, 1)
    product(1, 3)
    core_sum(1, 2)
    core_sum(1, 3)
    x_sum(0)
    late_queries(9, 12)
    relay(1)
    z_sum(0)
    late_queries(12, 14)
    x_sum(1)
    y_sum(0)
    input_grad()
    z_sum(1)
    place_queries(0, 7)
    y_sum(1)
    collect(0)
    place_queries(7, 14)
    collect(1)
    for copy in gather_started + d_started:
        copy.wait_send()
    for h in range(QH):
        hand_over(h).wait_send()
    for g in range(KVH):
        hand_over_kv(g).wait_send()

        @pl.when(x % 2 == hi)
        def _():
            for copy in share(g):
                copy.wait_send()


def shards(inputs, queries, out_grad, kv_weight, passage_blocks, handover):
    freq = ROPE_BASE ** (-(np.arange(HD // 2, dtype=np.float32) * 2.0) / HD)
    freq = jnp.asarray(np.concatenate([freq, freq])[None, :].astype(np.float32))
    dma = pltpu.SemaphoreType.DMA
    anywhere = pl.BlockSpec(memory_space=pl.ANY)
    scalars = pl.BlockSpec(memory_space=pltpu.SMEM)

    def vmem(*shape, kind=bf16):
        return pltpu.VMEM(shape, kind)

    packed = SENT * BLK
    shapes = (
        jax.ShapeDtypeStruct((ROWS, D), bf16),
        jax.ShapeDtypeStruct((ROWS, QH * HD), bf16),
        jax.ShapeDtypeStruct((SHARD, KV), f32),
    )
    return pl.pallas_call(
        kernel,
        name="grouped_attention_backward",
        out_shape=tuple(pltpu.VMEM(shape.shape, shape.dtype) for shape in shapes),
        in_specs=[scalars, scalars, VMEM, VMEM, anywhere, anywhere, anywhere],
        out_specs=(VMEM, VMEM, VMEM),
        scratch_shapes=[
            vmem(ROWS, D),
            vmem(ROWS, QH * HD),
            vmem(ROWS, QH * HD),
            vmem(D, ROWS),
            vmem(2 * KVH, 2, NZ, SHARD, HD),
            vmem(KVH, ROWS, HD),
            vmem(KVH, HD, ROWS),
            vmem(KVH, ROWS, HD),
            vmem(ROWS, HD, kind=f32),
            vmem(ROWS, HD, kind=f32),
            vmem(ROWS, ROWS, kind=f32),
            vmem(ROWS, HD, kind=f32),
            vmem(ROWS, HD, kind=f32),
            vmem(packed, ROWS),
            vmem(ROWS, packed),
            vmem(ROWS, HD, kind=f32),
            vmem(QH - LATE, ROWS, ROWS),
            vmem(QH, ROWS, HD),
            vmem(QH, packed, HD),
            vmem(QH, packed, HD),
            vmem(KVH, 2, ROWS, HD),
            vmem(KVH, 2, packed, HD),
            vmem(KVH, 2, packed, HD),
            vmem(ROWS, KV),
            vmem(KVH, 2, NF, SHARD, HD),
            vmem(KVH, NF, SHARD, HD),
            vmem(KVH, NF, SHARD, HD),
            vmem(2 * KVH, 4, HALF, HD),
            vmem(2 * KVH, 4, HALF, HD),
            vmem(2 * KVH, 4, HALF, HD),
            vmem(2 * KVH, 4, HALF, HD),
            vmem(KVH, NZ, HALF, HD),
            vmem(KVH * (NZ - 1), HALF, HD),
            vmem(KVH, HALF, HD),
            vmem(KVH, 4, HALF, HD),
            vmem(KVH, HALF, HD),
            vmem(KVH, 2, 2, HALF, HD),
            dma((3,)),
            dma((128,)),
            dma((16,)),
            dma((16,)),
            dma((32,)),
            dma((32,)),
            dma((32,)),
            dma((QH,)),
            dma((QH,)),
            dma((KVH,)),
            dma((KVH,)),
            dma((48,)),
            dma((8,)),
            dma((4,)),
            dma((4,)),
            dma((4,)),
            dma((KVH * (NZ - 1),)),
            dma((6,)),
            dma((14,)),
            dma((8,)),
        ],
        compiler_params=pltpu.CompilerParams(
            collective_id=0, has_side_effects=True, vmem_limit_bytes=LIMIT
        ),
    )(passage_blocks, handover, kv_weight, freq, inputs, queries, out_grad)


def solution(mesh):
    rows = P(("dp", "fsdp"), None)
    return jax.shard_map(
        shards,
        mesh=mesh,
        in_specs=(rows, rows, rows, P("fsdp", None), rows, rows),
        out_specs=(rows, rows, P("fsdp", None)),
        check_vma=False,
    )
```
